32 devices in a mesh: dp: 8 (over z, y), task: 4 (over x, core).
Axes of the slice: x: 2, y: 2, z: 4, core: 2. Of those that a mesh axis runs over, the one named last changes fastest.
Arguments:
- images: bfloat16 [8, 36, 48, 256], P('dp', 'task'), may hold values from -6 to 6
- w_trunk: bfloat16 [2304, 512], P('dp'), may hold values from -0.125 to 0.125
- trunk_gain: float32 [512], replicated, may hold values from 0.5 to 2
- trunk_bias: float32 [512], replicated, may hold values from -3 to 3
- w_hid: bfloat16 [3, 512, 512], P(None, 'dp'), may hold values from -0.25 to 0.25
- hid_gain: float32 [3, 512], replicated, may hold values from 0.5 to 2
- hid_bias: float32 [3, 512], replicated, may hold values from -3 to 3
- w_attn: bfloat16 [3, 512, 512], P(None, 'dp'), may hold values from -0.25 to 0.25
- attn_gain: float32 [3, 512], replicated, may hold values from 0.5 to 2
- attn_bias: float32 [3, 512], replicated, may hold values from -3 to 3
- w_shared: bfloat16 [4608, 256], P('dp'), may hold values from -0.1875 to 0.1875
- labels: int32 [8, 36, 48], P('dp', 'task'), may hold values from -1 to 12
- depth_valid: int32 [8, 36, 48], P('dp', 'task'), may hold values from 0 to 1, as said below
- trunk_cot: bfloat16 [8, 36, 48, 512], P('dp', 'task'), may hold values from -6 to 6
- task_cot: bfloat16 [3, 8, 36, 48, 256], P(None, 'dp', 'task'), may hold values from -6 to 6
Outputs:
- trunk_out: bfloat16 [8, 36, 48, 512], P('dp', 'task')
- task_out: bfloat16 [3, 8, 36, 48, 256], P(None, 'dp', 'task')
- image_grad: bfloat16 [8, 36, 48, 256], P('dp', 'task')
- w_trunk_grad: float32 [2304, 512], P('dp')
- trunk_gain_grad: float32 [512], replicated
- trunk_bias_grad: float32 [512], replicated
- w_hid_grad: float32 [3, 512, 512], P(None, 'dp')
- hid_gain_grad: float32 [3, 512], replicated
- hid_bias_grad: float32 [3, 512], replicated
- w_attn_grad: float32 [3, 512, 512], P(None, 'dp')
- attn_gain_grad: float32 [3, 512], replicated
- attn_bias_grad: float32 [3, 512], replicated
- w_shared_grad: float32 [4608, 256], P('dp')
The draws below stay inside these ranges and needn't reach their ends.
Inputs may be any that keep to these rules, and one draw needn't show every extreme that they name: `labels`: -1 marks a pixel without a segmentation label. `depth_valid`: the share of pixels with a depth reading differs strongly from image to image.
All inputs are finite; a program needn't handle non-finite values.
Results may differ from the reference program's by a relative error of at most 0.018.
Values may be sent and summed in bfloat16 or wider, within the bound.
No kernel may reach another device: no remote copies, remote signals or barrier semaphores. Data moves between devices by JAX's collectives and lax.ppermute only.
A program may use at most 128 MiB of HBM per device.

```python
import math
import jax
import jax.numpy as jnp
from jax import lax

C_IN = 256
C_MID = 512
C_OUT = 256
TASKS = 3
H = 36
W = 48
IMAGES = 8


def draw_depth_valid(key, part):
    key = jax.random.fold_in(key, 7)
    first_key, second_key = jax.random.split(key)
    position = jnp.arange(IMAGES, dtype=jnp.int32)
    base = 128 + 896 * position // max(IMAGES - 1, 1)
    factor = jax.random.randint(first_key, (IMAGES,), 1, 5)
    limit = jnp.minimum(base * factor // 4, 1024)
    ticket = jax.random.randint(second_key, (IMAGES, H, W), 0, 1024)
    return (ticket < limit[:, None, None]).astype(jnp.int32)


def plant(entries, stream_key, least, high):
    shape = entries.shape
    index_at = [jax.random.randint(jax.random.fold_in(stream_key, axis), (), 0, shape[axis]) for axis in range(len(shape))]
    entries = entries.at[tuple(index_at)].set(least)
    longest = shape.index(max(shape))
    index_at[longest] = (index_at[longest] + 1) % shape[longest]
    return entries.at[tuple(index_at)].set(high)


def levels(key, dims, cuts, least, top_value):
    factor_of = 1.0
    for axis_at, parts in cuts:
        draws = jax.random.uniform(jax.random.fold_in(jax.random.fold_in(key, 6), axis_at), (parts,), jnp.float32, least / len(cuts), top_value / len(cuts))
        factor_of = factor_of * jnp.repeat(jnp.exp(draws), dims[axis_at] // parts).reshape((-1,) + (1,) * (len(dims) - 1 - axis_at))
    return factor_of


def scatter_about(key, dims, deviation, bound, cuts=(), held_as=jnp.bfloat16):
    factor_of = levels(key, dims, cuts, -0.22, 0.18) if cuts else 1.0
    entries = jax.random.normal(key, dims, jnp.float32) * deviation * factor_of
    return jnp.minimum(jnp.maximum(entries, -bound), bound).astype(held_as)


def setup_inputs(seed: int = 0) -> dict:
    splits = jax.random.split(jax.random.key(seed), 16)
    images = scatter_about(splits[0], (IMAGES, H, W, C_IN), 1.0, 6.0, ((0, 8), (1, 4)))
    w_trunk = scatter_about(splits[1], (9 * C_IN, C_MID), (9 * C_IN) ** -0.5, 0.125, ((0, 8),))
    trunk_gain = jnp.clip(jnp.exp(jax.random.uniform(splits[2], (C_MID,), jnp.float32, math.log(0.5), math.log(2.0))), 0.5, 2.0)
    trunk_bias = scatter_about(splits[3], (C_MID,), 0.5, 3.0, (), jnp.float32)
    w_hid = scatter_about(splits[4], (TASKS, C_MID, C_MID), C_MID ** -0.5, 0.25, ((1, 8),))
    hid_gain = jnp.clip(jnp.exp(jax.random.uniform(splits[5], (TASKS, C_MID), jnp.float32, math.log(0.5), math.log(2.0))), 0.5, 2.0)
    hid_bias = scatter_about(splits[6], (TASKS, C_MID), 0.5, 3.0, (), jnp.float32)
    w_attn = scatter_about(splits[7], (TASKS, C_MID, C_MID), C_MID ** -0.5, 0.25, ((1, 8),))
    attn_gain = jnp.clip(jnp.exp(jax.random.uniform(splits[8], (TASKS, C_MID), jnp.float32, math.log(0.5), math.log(2.0))), 0.5, 2.0)
    attn_bias = scatter_about(splits[9], (TASKS, C_MID), 0.5, 3.0, (), jnp.float32)
    w_shared = scatter_about(splits[10], (9 * C_MID, C_OUT), (9 * C_MID // 4) ** -0.5, 0.1875, ((0, 8),))
    labels = plant(jax.random.randint(splits[11], (IMAGES, H, W), -1, 13), jax.random.fold_in(splits[11], 1), -1, 12).astype(jnp.int32)
    depth_valid = draw_depth_valid(jax.random.fold_in(splits[15], 71), 0)
    trunk_cot = scatter_about(splits[13], (IMAGES, H, W, C_MID), 1.0, 6.0, ((0, 8), (1, 4)))
    task_cot = scatter_about(splits[14], (TASKS, IMAGES, H, W, C_OUT), 1.0, 6.0, ((1, 8), (2, 4)))
    return {"images": images, "w_trunk": w_trunk, "trunk_gain": trunk_gain, "trunk_bias": trunk_bias, "w_hid": w_hid, "hid_gain": hid_gain, "hid_bias": hid_bias, "w_attn": w_attn, "attn_gain": attn_gain, "attn_bias": attn_bias, "w_shared": w_shared, "labels": labels, "depth_valid": depth_valid, "trunk_cot": trunk_cot, "task_cot": task_cot}


@jax.custom_vjp
def low(v):
    return lax.optimization_barrier(v.astype(jnp.bfloat16)).astype(jnp.float32)

@jax.custom_vjp
def low_back(v):
    return v

def low_keep(v):
    return (low(v), None)

def low_pass(kept, grad):
    return (grad,)

def back_keep(v):
    return (v, None)

def back_low(kept, grad):
    return (low(grad),)
low.defvjp(low_keep, low_pass)
low_back.defvjp(back_keep, back_low)
epsilon = 1e-05

def convolve(tensor, kernel, in_width, out_width):
    return lax.conv_general_dilated(tensor, kernel.reshape(3, 3, in_width, out_width), (1, 1), ((1, 1), (1, 1)), dimension_numbers=('NHWC', 'HWIO', 'NHWC'), precision=lax.Precision.HIGHEST)

def normalize(tensor, mask, gain, shift):
    count = jnp.maximum(jnp.sum(mask), 1.0)
    mean = lax.optimization_barrier(jnp.sum(mask * tensor, axis=(0, 1, 2))) / count
    second = lax.optimization_barrier(jnp.sum(mask * tensor * tensor, axis=(0, 1, 2))) / count
    return gain * (tensor - mean) * lax.rsqrt(second - mean * mean + epsilon) + shift

def reference(images, w_trunk, trunk_gain, trunk_bias, w_hid, hid_gain, hid_bias, w_attn, attn_gain, attn_bias, w_shared, labels, depth_valid, trunk_cot, task_cot):
    label_mask = (labels >= 0).astype(jnp.float32)[..., None]
    depth_mask = depth_valid.astype(jnp.float32)[..., None]
    masks = [label_mask, depth_mask, depth_mask]

    def forward(pixels_in, kernel_trunk, scale_trunk, shift_trunk, kernel_hid, scale_hid, shift_hid, kernel_attn, scale_attn, shift_attn, kernel_shared):
        trunk_pre = low_back(convolve(pixels_in, kernel_trunk, C_IN, C_MID))
        trunk_feat = low(jax.nn.gelu(normalize(trunk_pre, label_mask, scale_trunk, shift_trunk)))
        results = []
        for branch in range(TASKS):
            hid_pre = low_back(jnp.einsum('ihwc,cd->ihwd', trunk_feat, kernel_hid[branch], precision=lax.Precision.HIGHEST))
            hidden = low(jax.nn.gelu(normalize(hid_pre, masks[branch], scale_hid[branch], shift_hid[branch])))
            gate_pre = low_back(jnp.einsum('ihwc,cd->ihwd', hidden, kernel_attn[branch], precision=lax.Precision.HIGHEST))
            attention = jax.nn.sigmoid(normalize(gate_pre, masks[branch], scale_attn[branch], shift_attn[branch]))
            features = low(attention * trunk_feat)
            results.append(convolve(features, kernel_shared, C_MID, C_OUT))
        return (trunk_feat, jnp.stack(results))
    outputs, backward = jax.vjp(forward, images.astype(jnp.float32), w_trunk.astype(jnp.float32), trunk_gain.astype(jnp.float32), trunk_bias.astype(jnp.float32), w_hid.astype(jnp.float32), hid_gain.astype(jnp.float32), hid_bias.astype(jnp.float32), w_attn.astype(jnp.float32), attn_gain.astype(jnp.float32), attn_bias.astype(jnp.float32), w_shared.astype(jnp.float32))
    grads = backward((trunk_cot.astype(jnp.float32), task_cot.astype(jnp.float32) * jnp.stack(masks)))
    return (outputs[0].astype(jnp.bfloat16), outputs[1].astype(jnp.bfloat16), grads[0].astype(jnp.bfloat16), grads[1], grads[2], grads[3], grads[4], grads[5], grads[6], grads[7], grads[8], grads[9], grads[10])
```

```python
import jax
import jax.numpy as jnp
from jax import lax
from jax.sharding import PartitionSpec as P

EPS = 1e-05
BF = jnp.bfloat16
F32 = jnp.float32


def swap(x, axis, step):
    count = lax.axis_size(axis)
    return lax.ppermute(x, axis, [(i, i ^ step) for i in range(count)])


def levels(axis):
    count = lax.axis_size(axis)
    assert count & (count - 1) == 0
    return count.bit_length() - 1


def slice_index(axis):
    me, out = lax.axis_index(axis), 0
    for bit in range(levels(axis)):
        out = out * 2 + (me >> bit) % 2
    return out


def slice_of(place, axis):
    out = 0
    for bit in range(levels(axis)):
        out = out * 2 + (place >> bit) % 2
    return out


def sum_dp(x):
    bits = levels("dp")
    low = 1
    while low < bits:
        steps = [1 << low]
        if low + 1 < bits:
            steps += [2 << low, 3 << low]
        got = [swap(x, "dp", s) for s in steps]
        x = sum(got, x)
        low += 2
    return x + swap(x, "dp", 1) if bits else x


def sum_task(x):
    got = [swap(x, "task", s) for s in range(1, lax.axis_size("task"))]
    return sum(got, x)


def sum_all(x):
    return sum_dp(sum_task(x))


def gather_dp(x):
    count = lax.axis_size("dp")
    return lax.all_to_all(jnp.broadcast_to(x[None], (count,) + x.shape), "dp", 0, 0, tiled=True)


def gather_slices(x, dim):
    me = lax.axis_index("task")
    for bit in reversed(range(levels("task"))):
        other = swap(x, "task", 1 << bit)
        upper = (me >> bit) % 2 == 1
        x = jnp.concatenate(
            [jnp.where(upper, other, x), jnp.where(upper, x, other)], axis=dim
        )
    return x


def scatter_slices(x, dim):
    me = lax.axis_index("task")
    for bit in range(levels("task")):
        half = x.shape[dim] // 2
        mine = (me >> bit) % 2
        kept = lax.dynamic_slice_in_dim(x, mine * half, half, axis=dim)
        sent = lax.dynamic_slice_in_dim(x, (1 - mine) * half, half, axis=dim)
        x = (kept.astype(F32) + swap(sent.astype(BF), "task", 1 << bit).astype(F32))
    return x


def scatter_dp(x, dim):
    count = lax.axis_size("dp")
    shape = x.shape[:dim] + (count, x.shape[dim] // count) + x.shape[dim + 1 :]
    parts = lax.all_to_all(x.astype(BF).reshape(shape), "dp", dim, dim, tiled=True)
    return jnp.sum(parts.astype(F32), axis=dim)


def rows_to_slices(x):
    count, me = lax.axis_size("task"), lax.axis_index("task")
    width = x.shape[-1] // count
    rows = x.shape[1]
    out = jnp.zeros((x.shape[0], rows * count, x.shape[2], width), x.dtype)
    for step in range(count):
        peer = me ^ step
        part = lax.dynamic_slice_in_dim(x, slice_of(peer, "task") * width, width, axis=3)
        got = swap(part, "task", step) if step else part
        out = lax.dynamic_update_slice_in_dim(out, got, peer * rows, axis=1)
    return out


def slices_to_rows(x):
    count, me = lax.axis_size("task"), lax.axis_index("task")
    rows = x.shape[1] // count
    width = x.shape[3]
    out = jnp.zeros((x.shape[0], rows, x.shape[2], width * count), x.dtype)
    for step in range(count):
        peer = me ^ step
        part = lax.dynamic_slice_in_dim(x, peer * rows, rows, axis=1)
        got = swap(part, "task", step) if step else part
        out = lax.dynamic_update_slice_in_dim(out, got, slice_of(peer, "task") * width, axis=3)
    return out


def sum_to_rows(x):
    count, me = lax.axis_size("task"), lax.axis_index("task")
    rows = x.shape[1] // count
    out = 0.0
    for step in range(count):
        part = lax.dynamic_slice_in_dim(x, (me ^ step) * rows, rows, axis=1)
        out = out + (swap(part.astype(BF), "task", step).astype(F32) if step else part)
    return out


def halo(cells, dim):
    count = lax.axis_size("task")
    head = lax.slice_in_dim(cells, 0, 1, axis=dim)
    tail = lax.slice_in_dim(cells, cells.shape[dim] - 1, cells.shape[dim], axis=dim)
    return jnp.concatenate(
        [
            lax.ppermute(tail, "task", [(i, i + 1) for i in range(count - 1)]),
            cells,
            lax.ppermute(head, "task", [(i + 1, i) for i in range(count - 1)]),
        ],
        axis=dim,
    )


def pad_rows(x):
    return jnp.pad(x, ((0, 0), (1, 1), (0, 0), (0, 0)))


def windows(padded, reverse=False):
    wide = jnp.pad(padded, ((0, 0), (0, 0), (1, 1), (0, 0)))
    cols = padded.shape[2]
    order = (2, 1, 0) if reverse else (0, 1, 2)
    return jnp.concatenate([wide[:, :, q : q + cols] for q in order], axis=-1)


def conv(wide, kernel, reverse=False):
    rows = wide.shape[1] - 2
    total = 0.0
    for p in range(3):
        at = 2 - p if reverse else p
        part = wide[:, at : at + rows].reshape(-1, wide.shape[-1])
        total = total + jnp.dot(part, kernel[p], preferred_element_type=F32)
    return total


def conv_weights(wide, grad):
    rows = wide.shape[1] - 2
    return jnp.concatenate(
        [
            lax.dot_general(
                wide[:, p : p + rows].reshape(-1, wide.shape[-1]),
                grad,
                (((0,), (0,)), ((), ())),
                preferred_element_type=F32,
            )
            for p in range(3)
        ]
    )


def turned(kernel, width):
    taps = kernel.reshape(9, width, -1)
    return jnp.swapaxes(taps, 1, 2).reshape(3, -1, width)


def scales(first, second, count):
    total = jnp.maximum(count, 1.0)
    mean = first / total
    return mean, lax.rsqrt(second / total - mean * mean + EPS), total


def norm_back(upstream, normed, mask, gain, rstd, count, s_bias, s_gain):
    return rstd * (upstream * gain - mask / count * (gain * s_bias + normed * gain * s_gain))


def shards(
    images,
    w_trunk,
    trunk_gain,
    trunk_bias,
    w_hid,
    hid_gain,
    hid_bias,
    w_attn,
    attn_gain,
    attn_bias,
    w_shared,
    labels,
    depth_valid,
    trunk_cot,
    task_cot,
):
    image_count, row_count, col_count, in_width = images.shape
    mid = w_trunk.shape[1]
    out_width = w_shared.shape[1]
    tasks = w_hid.shape[0]
    parts = lax.axis_size("task")
    part = mid // parts
    s = slice_index("task")
    pixels = image_count * row_count * col_count

    lane = s * part
    w_slice = gather_dp(lax.dynamic_slice_in_dim(w_trunk, lane, part, axis=1)).reshape(-1, part)
    all_images = lax.all_gather(images, "task", axis=1, tiled=True)
    label_mask = (labels >= 0).astype(F32)
    depth_mask = depth_valid.astype(F32)
    counts = sum_all(jnp.stack([jnp.sum(label_mask), jnp.sum(depth_mask)])[None])
    all_labels = lax.all_gather(label_mask, "task", axis=1, tiled=True).reshape(-1, 1)
    label_mask = label_mask.reshape(pixels, 1)
    depth_mask = depth_mask.reshape(pixels, 1)
    masks = jnp.stack([label_mask, depth_mask, depth_mask][:tasks])
    n_label = jnp.maximum(counts[0, 0], 1.0)
    n_depth = jnp.maximum(counts[0, 1], 1.0)
    n_task = jnp.stack([n_label, n_depth, n_depth][:tasks])[:, None]

    def weights(w):
        own = lax.dynamic_slice_in_dim(w, lane, part, axis=w.ndim - 1)
        got = lax.all_gather(own, "dp", axis=w.ndim - 2, tiled=True)
        return gather_slices(got, w.ndim - 1)

    full_hid = weights(w_hid)
    full_attn = weights(w_attn)
    full_shared = lax.all_gather(w_shared, "dp", axis=0, tiled=True)

    image_wide = windows(pad_rows(all_images))
    trunk_pre = conv(image_wide, w_slice.reshape(3, -1, part))
    own_gain = lax.dynamic_slice_in_dim(trunk_gain, lane, part)
    own_bias = lax.dynamic_slice_in_dim(trunk_bias, lane, part)
    sums = sum_dp(
        jnp.stack(
            [jnp.sum(all_labels * trunk_pre, 0), jnp.sum(all_labels * trunk_pre * trunk_pre, 0)]
        )
    )
    trunk_mean, trunk_rstd, _ = scales(sums[0], sums[1], n_label)
    trunk_normed = (trunk_pre - trunk_mean) * trunk_rstd
    trunk_act, gelu_back = jax.vjp(jax.nn.gelu, trunk_normed * own_gain + own_bias)
    trunk_rows = slices_to_rows(
        trunk_act.astype(BF).reshape(image_count, -1, col_count, part)
    )
    feat = trunk_rows.reshape(pixels, mid)
    feat_value = feat.astype(F32)

    def each(f, *xs):
        return jnp.stack([f(*(x[t] for x in xs)) for t in range(tasks)])

    def moments(v):
        return jnp.concatenate([jnp.sum(masks * v, 1), jnp.sum(masks * v * v, 1)])

    def dot(a, b):
        return jnp.dot(a, b, preferred_element_type=F32)

    def dot_nt(a, b):
        return lax.dot_general(a, b, (((1,), (1,)), ((), ())), preferred_element_type=F32)

    def dot_tn(a, b):
        return lax.dot_general(a, b, (((0,), (0,)), ((), ())), preferred_element_type=F32)

    hid_pre = each(lambda w: dot(feat, w), full_hid)
    sums = sum_all(moments(hid_pre))
    hid_mean, hid_rstd, _ = scales(sums[:tasks], sums[tasks:], n_task)
    hid_normed = (hid_pre - hid_mean[:, None]) * hid_rstd[:, None]
    hid_act, hid_gelu_back = jax.vjp(
        jax.nn.gelu, hid_normed * hid_gain[:, None] + hid_bias[:, None]
    )
    hidden = hid_act.astype(BF)
    gate_pre = each(dot, hidden, full_attn)
    sums = sum_all(moments(gate_pre))
    gate_mean, gate_rstd, _ = scales(sums[:tasks], sums[tasks:], n_task)
    gate_normed = (gate_pre - gate_mean[:, None]) * gate_rstd[:, None]
    attention = jax.nn.sigmoid(gate_normed * attn_gain[:, None] + attn_bias[:, None])
    features = (attention * feat_value).astype(BF)

    upstream = task_cot * masks.astype(BF).reshape(tasks, image_count, row_count, col_count, 1)
    up_halo = halo(upstream, 2)
    up_wide = [windows(up_halo[t], reverse=True) for t in range(tasks)]
    turned_shared = turned(full_shared, mid)
    feature_grad = each(lambda t: conv(up_wide[t], turned_shared, reverse=True), range(tasks))

    gate_grad = feature_grad * feat_value * attention * (1.0 - attention)
    gate_sums = sum_all(
        jnp.concatenate([jnp.sum(gate_grad, 1), jnp.sum(gate_grad * gate_normed, 1)])
    )
    attn_bias_grad, attn_gain_grad = gate_sums[:tasks], gate_sums[tasks:]
    pre_grad = norm_back(
        gate_grad,
        gate_normed,
        masks,
        attn_gain[:, None],
        gate_rstd[:, None],
        n_task[:, None],
        attn_bias_grad[:, None],
        attn_gain_grad[:, None],
    ).astype(BF)
    hid_grad = each(dot_nt, pre_grad, full_attn)
    hid_act_grad = hid_gelu_back(hid_grad)[0]
    hid_sums = sum_all(
        jnp.concatenate([jnp.sum(hid_act_grad, 1), jnp.sum(hid_act_grad * hid_normed, 1)])
    )
    hid_bias_grad, hid_gain_grad = hid_sums[:tasks], hid_sums[tasks:]
    hid_pre_grad = norm_back(
        hid_act_grad,
        hid_normed,
        masks,
        hid_gain[:, None],
        hid_rstd[:, None],
        n_task[:, None],
        hid_bias_grad[:, None],
        hid_gain_grad[:, None],
    ).astype(BF)
    feat_grad = trunk_cot.astype(F32).reshape(pixels, mid) + jnp.sum(feature_grad * attention, 0)
    for t in range(tasks):
        feat_grad = feat_grad + dot_nt(hid_pre_grad[t], full_hid[t])

    slice_grad = rows_to_slices(
        feat_grad.astype(BF).reshape(image_count, row_count, col_count, mid)
    ).reshape(-1, part)
    act_grad = gelu_back(slice_grad.astype(F32))[0]
    trunk_sums = sum_dp(jnp.stack([jnp.sum(act_grad, 0), jnp.sum(act_grad * trunk_normed, 0)]))
    trunk_pre_grad = norm_back(
        act_grad,
        trunk_normed,
        all_labels,
        own_gain,
        trunk_rstd,
        n_label,
        trunk_sums[0],
        trunk_sums[1],
    ).astype(BF)
    trunk_grad = scatter_dp(conv_weights(image_wide, trunk_pre_grad), 0)
    trunk_grad = gather_slices(trunk_grad.astype(BF), 1).astype(F32)
    trunk_totals = gather_slices(trunk_sums, 1)
    grad_wide = windows(
        pad_rows(trunk_pre_grad.reshape(image_count, -1, col_count, part)), reverse=True
    )
    image_grad = conv(grad_wide, turned(w_slice, in_width), reverse=True)
    image_grad = sum_to_rows(image_grad.reshape(image_count, -1, col_count, in_width)).astype(BF)

    def weight_grads(g, dim):
        g = scatter_dp(scatter_slices(g, g.ndim - 1), dim)
        return gather_slices(g.astype(BF), g.ndim - 1).astype(F32)

    shared_grad = 0.0
    feature_halo = halo(features.reshape(tasks, image_count, row_count, col_count, mid), 2)
    task_out = []
    kernel_shared = full_shared.reshape(3, -1, out_width)
    for t in range(tasks):
        feature_wide = windows(feature_halo[t])
        task_out.append(conv(feature_wide, kernel_shared).astype(BF))
        shared_grad = shared_grad + conv_weights(
            feature_wide, upstream[t].reshape(pixels, out_width)
        )
    task_out = jnp.stack(task_out).reshape(tasks, image_count, row_count, col_count, out_width)
    return (
        trunk_rows,
        task_out,
        image_grad,
        trunk_grad,
        trunk_totals[1],
        trunk_totals[0],
        weight_grads(each(lambda g: dot_tn(feat, g), hid_pre_grad), 1),
        hid_gain_grad,
        hid_bias_grad,
        weight_grads(each(dot_tn, hidden, pre_grad), 1),
        attn_gain_grad,
        attn_bias_grad,
        weight_grads(shared_grad, 0),
    )


def solution(mesh):
    rows = P("dp", "task", None, None)
    task_rows = P(None, "dp", "task", None, None)
    flat, stacked = P("dp", None), P(None, "dp", None)
    pixel = P("dp", "task", None)
    return jax.shard_map(
        shards,
        mesh=mesh,
        in_specs=(
            rows,
            flat,
            P(),
            P(),
            stacked,
            P(),
            P(),
            stacked,
            P(),
            P(),
            flat,
            pixel,
            pixel,
            rows,
            task_rows,
        ),
        out_specs=(
            rows,
            task_rows,
            rows,
            flat,
            P(),
            P(),
            stacked,
            P(),
            P(),
            stacked,
            P(),
            P(),
            flat,
        ),
        check_vma=False,
    )
```

```python
import jax
import jax.numpy as jnp
from jax import lax
from jax.sharding import PartitionSpec as P

EPS = 1e-05
BF = jnp.bfloat16
F32 = jnp.float32


def swap(x, axis, step):
    count = lax.axis_size(axis)
    return lax.ppermute(x, axis, [(i, i ^ step) for i in range(count)])


def levels(axis):
    count = lax.axis_size(axis)
    assert count & (count - 1) == 0
    return count.bit_length() - 1


def slice_of(place):
    out = 0
    for bit in range(levels("task")):
        out = out * 2 + (place >> bit) % 2
    return out


def sum_dp(x):
    bits = levels("dp")
    low = 1
    while low < bits:
        steps = [1 << low]
        if low + 1 < bits:
            steps += [2 << low, 3 << low]
        x = sum([swap(x, "dp", s) for s in steps], x)
        low += 2
    return x + swap(x, "dp", 1) if bits else x


def gather_dp(x):
    count = lax.axis_size("dp")
    stacked = jnp.broadcast_to(x[None], (count,) + x.shape)
    return lax.all_to_all(stacked, "dp", 0, 0, tiled=True).reshape((-1,) + x.shape[1:])


def scatter_dp(x):
    count = lax.axis_size("dp")
    parts = x.astype(BF).reshape((count, -1) + x.shape[1:])
    return jnp.sum(lax.all_to_all(parts, "dp", 0, 0, tiled=True).astype(F32), axis=0)


def fan(x):
    got = {0: x}
    for bit in reversed(range(levels("task"))):
        for k in sorted(got):
            got[k | 1 << bit] = swap(got[k], "task", 1 << bit)
    return got


def place_slices(got, dim):
    me = lax.axis_index("task")
    width = got[0].shape[dim]
    shape = list(got[0].shape)
    shape[dim] = width * len(got)
    out = jnp.zeros(shape, got[0].dtype)
    for k, piece in got.items():
        out = lax.dynamic_update_slice_in_dim(out, piece, slice_of(me ^ k) * width, axis=dim)
    return out


def scatter_slices(x, dim):
    me = lax.axis_index("task")
    for bit in range(levels("task")):
        half = x.shape[dim] // 2
        mine = (me >> bit) % 2
        kept = lax.dynamic_slice_in_dim(x, mine * half, half, axis=dim)
        sent = lax.dynamic_slice_in_dim(x, (1 - mine) * half, half, axis=dim)
        x = kept.astype(F32) + swap(sent.astype(BF), "task", 1 << bit).astype(F32)
    return x


def exchange(pick, place, shape, dtype):
    me = lax.axis_index("task")
    out = jnp.zeros(shape, dtype)
    for step in range(lax.axis_size("task")):
        peer = me ^ step
        piece = pick(peer)
        out = place(out, swap(piece, "task", step) if step else piece, peer)
    return out


def pad_rows(x):
    return jnp.pad(x, ((0, 0), (1, 1), (0, 0), (0, 0)))


def windows(x, reverse=False):
    cols = x.shape[2]
    wide = jnp.pad(x, ((0, 0), (1, 1), (1, 1), (0, 0)))
    order = (2, 1, 0) if reverse else (0, 1, 2)
    return jnp.concatenate([wide[:, :, q : q + cols] for q in order], axis=-1)


def conv(wide, kernel, reverse=False):
    rows = wide.shape[1] - 2
    total = 0.0
    for p in range(3):
        at = 2 - p if reverse else p
        part = wide[:, at : at + rows].reshape(-1, wide.shape[-1])
        total = total + jnp.dot(part, kernel[p], preferred_element_type=F32)
    return total


def conv_weights(wide, grad):
    rows = wide.shape[1] - 2
    return jnp.concatenate(
        [dot_tn(wide[:, p : p + rows].reshape(-1, wide.shape[-1]), grad) for p in range(3)]
    )


def turned(kernel, width):
    taps = kernel.reshape(9, width, -1)
    return jnp.swapaxes(taps, 1, 2).reshape(3, -1, width)


def dot(a, b):
    return jnp.dot(a, b, preferred_element_type=F32)


def dot_nt(a, b):
    return lax.dot_general(a, b, (((1,), (1,)), ((), ())), preferred_element_type=F32)


def dot_tn(a, b):
    return lax.dot_general(a, b, (((0,), (0,)), ((), ())), preferred_element_type=F32)


def moments(v, mask):
    return jnp.stack([jnp.sum(mask * v, 0), jnp.sum(mask * v * v, 0)])


def scales(first, second, count):
    mean = first / count
    return mean, lax.rsqrt(second / count - mean * mean + EPS)


def norm_back(upstream, normed, mask, gain, rstd, count, s_bias, s_gain):
    return rstd * (upstream * gain - mask / count * (gain * s_bias + normed * gain * s_gain))


def shards(
    images,
    w_trunk,
    trunk_gain,
    trunk_bias,
    w_hid,
    hid_gain,
    hid_bias,
    w_attn,
    attn_gain,
    attn_bias,
    w_shared,
    labels,
    depth_valid,
    trunk_cot,
    task_cot,
):
    image_count, row_count, col_count, in_width = images.shape
    mid = w_trunk.shape[1]
    out_width = w_shared.shape[1]
    tasks = w_hid.shape[0]
    places = lax.axis_size("task")
    part = mid // places
    me = lax.axis_index("task")
    lane = slice_of(me) * part
    task = jnp.minimum(me, tasks - 1)
    active = (me < tasks).astype(F32)
    all_rows = row_count * places
    pixels = image_count * all_rows * col_count

    def own_rows(x, place):
        return lax.dynamic_slice_in_dim(x, place * row_count, row_count, axis=1)

    def put_rows(out, piece, place):
        return lax.dynamic_update_slice_in_dim(out, piece, place * row_count, axis=1)

    def of_task(x):
        return lax.dynamic_index_in_dim(x, task, 0, keepdims=False)

    w_slice = gather_dp(lax.dynamic_slice_in_dim(w_trunk, lane, part, axis=1))
    all_images = exchange(
        lambda peer: images,
        put_rows,
        (image_count, all_rows, col_count, in_width),
        images.dtype,
    )
    marks = jnp.stack([(labels >= 0).astype(F32), depth_valid.astype(F32)], axis=-1)
    marks = exchange(
        lambda peer: marks, put_rows, (image_count, all_rows, col_count, 2), F32
    ).reshape(pixels, 2)
    label_mask = marks[:, :1]
    mask = jnp.where(task == 0, label_mask, marks[:, 1:])
    shared_quarter = lax.dynamic_slice_in_dim(
        w_shared, slice_of(me) * (w_shared.shape[0] // places), w_shared.shape[0] // places, axis=0
    )
    full_shared = lax.all_gather(shared_quarter, ("dp", "task"), axis=0, tiled=False)
    order = [sum(((t >> b) & 1) << (levels("task") - 1 - b) for b in range(levels("task"))) for t in range(places)]
    full_shared = full_shared.reshape((-1, places) + shared_quarter.shape)
    full_shared = jnp.stack([full_shared[:, order.index(i)] for i in range(places)], 1).reshape(
        -1, out_width
    )
    task_hid = gather_dp(of_task(w_hid))
    task_attn = gather_dp(of_task(w_attn))
    out_cot = exchange(
        lambda peer: lax.dynamic_index_in_dim(
            task_cot, jnp.minimum(peer, tasks - 1), 0, keepdims=False
        ),
        put_rows,
        (image_count, all_rows, col_count, out_width),
        BF,
    )
    slice_cot = exchange(
        lambda peer: lax.dynamic_slice_in_dim(trunk_cot, slice_of(peer) * part, part, axis=3),
        put_rows,
        (image_count, all_rows, col_count, part),
        BF,
    ).reshape(pixels, part)

    image_wide = windows(all_images)
    trunk_pre = conv(image_wide, w_slice.reshape(3, -1, part))
    own_mean = jnp.mean(trunk_pre, 0)
    centred = trunk_pre - own_mean
    own_dev = jnp.sqrt(jnp.mean(centred * centred, 0) + 1e-30)
    scaled = (centred / own_dev).astype(BF)
    counts = jnp.zeros((1, part), F32).at[0, :2].set(jnp.sum(marks, 0))
    stats = jnp.concatenate([moments(trunk_pre, label_mask), counts, own_mean[None], own_dev[None]])
    stats = place_slices(fan(stats), 1)
    totals = sum_dp(stats[:3])
    own_mean, own_dev = stats[3], stats[4]
    n_label = jnp.maximum(totals[2, 0], 1.0)
    n_task = jnp.maximum(jnp.where(task == 0, totals[2, 0], totals[2, 1]), 1.0)
    trunk_mean, trunk_rstd = scales(totals[0], totals[1], n_label)
    scaled = place_slices(fan(scaled), 1)
    slope = trunk_rstd * trunk_gain
    feat = jax.nn.gelu(
        scaled.astype(F32) * (own_dev * slope) + ((own_mean - trunk_mean) * slope + trunk_bias)
    ).astype(BF)
    trunk_out = own_rows(feat.reshape(image_count, all_rows, col_count, mid), me)
    feat_value = feat.astype(F32)

    h_gain, h_bias, a_gain, a_bias = map(of_task, (hid_gain, hid_bias, attn_gain, attn_bias))
    hid_pre = dot(feat, task_hid)
    sums = sum_dp(moments(hid_pre, mask))
    hid_mean, hid_rstd = scales(sums[0], sums[1], n_task)
    hid_normed = (hid_pre - hid_mean) * hid_rstd
    hid_act, hid_gelu_back = jax.vjp(jax.nn.gelu, hid_normed * h_gain + h_bias)
    hidden = hid_act.astype(BF)
    gate_pre = dot(hidden, task_attn)
    sums = sum_dp(moments(gate_pre, mask))
    gate_mean, gate_rstd = scales(sums[0], sums[1], n_task)
    gate_normed = (gate_pre - gate_mean) * gate_rstd
    attention = jax.nn.sigmoid(gate_normed * a_gain + a_bias)
    features = (attention * feat_value).astype(BF)

    upstream = out_cot * mask.astype(BF).reshape(image_count, all_rows, col_count, 1)
    feature_grad = conv(windows(upstream, reverse=True), turned(full_shared, mid), reverse=True)
    gate_grad = feature_grad * feat_value * attention * (1.0 - attention)
    gate_sums = sum_dp(jnp.stack([jnp.sum(gate_grad, 0), jnp.sum(gate_grad * gate_normed, 0)]))
    pre_grad = norm_back(
        gate_grad, gate_normed, mask, a_gain, gate_rstd, n_task, gate_sums[0], gate_sums[1]
    ).astype(BF)
    hid_act_grad = hid_gelu_back(dot_nt(pre_grad, task_attn))[0]
    hid_sums = sum_dp(
        jnp.stack([jnp.sum(hid_act_grad, 0), jnp.sum(hid_act_grad * hid_normed, 0)])
    )
    hid_pre_grad = norm_back(
        hid_act_grad, hid_normed, mask, h_gain, hid_rstd, n_task, hid_sums[0], hid_sums[1]
    ).astype(BF)
    feat_part = (feature_grad * attention + dot_nt(hid_pre_grad, task_hid)) * active

    slice_grad = scatter_slices(feat_part, 1) + slice_cot.astype(F32)
    own_gain = lax.dynamic_slice_in_dim(trunk_gain, lane, part)
    own_bias = lax.dynamic_slice_in_dim(trunk_bias, lane, part)
    own_trunk_mean = lax.dynamic_slice_in_dim(trunk_mean, lane, part)
    own_rstd = lax.dynamic_slice_in_dim(trunk_rstd, lane, part)
    trunk_normed = (trunk_pre - own_trunk_mean) * own_rstd
    gelu_back = jax.vjp(jax.nn.gelu, trunk_normed * own_gain + own_bias)[1]
    act_grad = gelu_back(slice_grad)[0]
    trunk_sums = sum_dp(jnp.stack([jnp.sum(act_grad, 0), jnp.sum(act_grad * trunk_normed, 0)]))
    trunk_pre_grad = norm_back(
        act_grad,
        trunk_normed,
        label_mask,
        own_gain,
        own_rstd,
        n_label,
        trunk_sums[0],
        trunk_sums[1],
    ).astype(BF)
    trunk_grad = scatter_dp(conv_weights(image_wide, trunk_pre_grad))
    trunk_grad = place_slices(fan(trunk_grad.astype(BF)), 1).astype(F32)
    trunk_totals = place_slices(fan(trunk_sums), 1)
    grad_wide = windows(
        trunk_pre_grad.reshape(image_count, all_rows, col_count, part), reverse=True
    )
    image_part = conv(grad_wide, turned(w_slice, in_width), reverse=True).reshape(
        image_count, all_rows, col_count, in_width
    )
    image_grad = own_rows(image_part, me)
    for step in range(1, places):
        image_grad = image_grad + swap(
            own_rows(image_part, me ^ step).astype(BF), "task", step
        ).astype(F32)
    image_grad = image_grad.astype(BF)

    def to_all(x):
        got = fan(x)
        out = jnp.zeros((places,) + x.shape, x.dtype)
        for k, piece in got.items():
            out = lax.dynamic_update_index_in_dim(out, piece, me ^ k, 0)
        return out[:tasks]

    feature_wide = windows(features.reshape(image_count, all_rows, col_count, mid))
    task_part = (
        conv(feature_wide, full_shared.reshape(3, -1, out_width))
        .astype(BF)
        .reshape(image_count, all_rows, col_count, out_width)
    )
    task_out = exchange(
        lambda peer: own_rows(task_part, peer),
        lambda out, piece, peer: lax.dynamic_update_index_in_dim(out, piece, peer, 0),
        (places, image_count, row_count, col_count, out_width),
        BF,
    )[:tasks]
    shared_grad = conv_weights(feature_wide, upstream.reshape(pixels, out_width)) * active
    blocks = lax.axis_size("dp")
    shared_grad = scatter_slices(shared_grad.reshape(blocks, -1, out_width), 1)
    shared_grad = scatter_dp(shared_grad.reshape(-1, out_width))
    shared_grad = place_slices(fan(shared_grad.astype(BF)), 0).astype(F32)
    attn_grad = to_all(scatter_dp(dot_tn(hidden, pre_grad)).astype(BF)).astype(F32)
    hid_grad = to_all(scatter_dp(dot_tn(feat, hid_pre_grad)).astype(BF)).astype(F32)
    small = to_all(jnp.concatenate([gate_sums, hid_sums]))
    return (
        trunk_out,
        task_out,
        image_grad,
        trunk_grad,
        trunk_totals[1],
        trunk_totals[0],
        hid_grad,
        small[:, 3],
        small[:, 2],
        attn_grad,
        small[:, 1],
        small[:, 0],
        shared_grad,
    )


def solution(mesh):
    rows = P("dp", "task", None, None)
    task_rows = P(None, "dp", "task", None, None)
    flat, stacked = P("dp", None), P(None, "dp", None)
    pixel = P("dp", "task", None)
    return jax.shard_map(
        shards,
        mesh=mesh,
        in_specs=(
            rows,
            flat,
            P(),
            P(),
            stacked,
            P(),
            P(),
            stacked,
            P(),
            P(),
            flat,
            pixel,
            pixel,
            rows,
            task_rows,
        ),
        out_specs=(
            rows,
            task_rows,
            rows,
            flat,
            P(),
            P(),
            stacked,
            P(),
            P(),
            stacked,
            P(),
            P(),
            flat,
        ),
        check_vma=False,
    )
```

```python
import math

import jax
import jax.numpy as jnp
from jax import lax
from jax.experimental import pallas as pl
from jax.experimental.pallas import tpu as pltpu
from jax.sharding import PartitionSpec as P

EPS = 1e-05
BF = jnp.bfloat16
F32 = jnp.float32
ROOT = math.sqrt(2.0 / math.pi)
CUBE = 0.044715
VMEM = pl.BlockSpec(memory_space=pltpu.VMEM)
TRUNK_GAIN, TRUNK_BIAS, HID_GAIN, HID_BIAS, ATTN_GAIN, ATTN_BIAS = (slice(k, k + 1) for k in range(6))


def swap(x, axis, step):
    count = lax.axis_size(axis)
    return lax.ppermute(x, axis, [(i, i ^ step) for i in range(count)])


def levels(axis):
    count = lax.axis_size(axis)
    assert count & (count - 1) == 0
    return count.bit_length() - 1


def slice_of(place):
    out = 0
    for bit in range(levels("task")):
        out = out * 2 + (place >> bit) % 2
    return out


def dp_steps():
    bits, low, out = levels("dp"), 1, []
    while low < bits:
        out.append([1 << low] + ([2 << low, 3 << low] if low + 1 < bits else []))
        low += 2
    return out + ([[1]] if bits else [])


def sum_dp(x, work=None):
    steps = dp_steps()
    for step in steps[:-1]:
        x = add_up(x, *[swap(x, "dp", s) for s in step])
    done = work() if work else None
    if work:
        x, done = together(x, done)
    for step in steps[-1:]:
        x = add_up(x, *[swap(x, "dp", s) for s in step])
    return (x, done) if work else x


def together(*xs):
    return lax.optimization_barrier(xs)


def others(x, axis):
    return [x] + [swap(x, axis, k) for k in range(1, lax.axis_size(axis))]


def in_blocks(rows):
    return rows % 16 == 0 and lax.axis_size("dp") <= 8


def gather_dp(x):
    if in_blocks(x.shape[0]):
        return others(x, "dp")
    return [lax.all_gather(x, "dp", axis=0, tiled=True)]


def scatter_dp(parts):
    count = lax.axis_size("dp")
    if len(parts) == 1:
        whole = parts[0].reshape((count, -1) + parts[0].shape[1:])
        return gathered_sum(lax.all_to_all(whole, "dp", 0, 0, tiled=True), BF)
    if len(parts) == 2 and count > 2:
        parts = add_cut(parts[0], swap(parts[1], "dp", 1), count // 2)
        return piece_sum([swap(p, "dp", 2 * k) if k else p for k, p in enumerate(parts)], BF)
    return piece_sum([swap(p, "dp", k) if k else p for k, p in enumerate(parts)], BF)


def fan(x, first=None):
    got = {0: x}
    for bit in reversed(range(levels("task"))):
        for k in sorted(got):
            got[k | 1 << bit] = swap(got[k], "task", 1 << bit) if first is None else first
            first = None
    return [got[k] for k in range(len(got))]


def first_hop(x):
    return swap(x, "task", lax.axis_size("task") // 2)


def kernel_call(name, body, grid, ins, in_specs, outs, out_specs, scratch=(), limit=16, flops=0):
    return pl.pallas_call(
        body,
        name=name,
        grid=grid,
        in_specs=in_specs,
        out_specs=out_specs,
        out_shape=[jax.ShapeDtypeStruct(s, d) for s, d in outs],
        scratch_shapes=list(scratch),
        compiler_params=pltpu.CompilerParams(vmem_limit_bytes=limit * 2**20),
        cost_estimate=pl.CostEstimate(
            flops=flops, bytes_accessed=sum(x.size * x.dtype.itemsize for x in ins), transcendentals=0
        ),
    )(*ins)


def peer(k):
    return lax.axis_index("task") ^ k


def lanes_of(place, width):
    return ds(slice_of(place) * width, width, 128)


def halves(level, size, unit=16):
    bit = (lax.axis_index("task") >> level) % 2
    return ds(bit * size, size, unit), ds((1 - bit) * size, size, unit)


def ds(start, size, unit=16):
    if isinstance(start, int):
        return pl.ds(start, size)
    return pl.ds(pl.multiple_of(start, unit), size)


def dot(a, b):
    return jnp.dot(a, b, preferred_element_type=F32)


def dot_nt(a, b):
    return lax.dot_general(a, b, (((1,), (1,)), ((), ())), preferred_element_type=F32)


def dot_tn(a, b):
    return lax.dot_general(a, b, (((0,), (0,)), ((), ())), preferred_element_type=F32)


def gelu_parts(v):
    square = v * v
    t = jnp.tanh(ROOT * v * (1.0 + CUBE * square))
    return square, t


def gelu(v):
    _, t = gelu_parts(v)
    return 0.5 * v * (1.0 + t)


def gelu_slope(v):
    square, t = gelu_parts(v)
    return 0.5 * (1.0 + t) + (0.5 * ROOT) * v * (1.0 - t * t) * (1.0 + (3.0 * CUBE) * square)


def sigmoid(v):
    return 0.5 * (1.0 + jnp.tanh(0.5 * v))


def scales(first, second, count):
    mean = first / count
    return mean, lax.rsqrt(second / count - mean * mean + EPS)


def fold(v):
    return jnp.sum(v.reshape(-1, 8, v.shape[-1]), axis=0)


def sweep(rows, width, step, sums):
    block = 16

    def body(i, carry):
        values = step(ds(i * block, block))
        return tuple(c + fold(v) for c, v in zip(carry, values, strict=True))

    start = tuple(jnp.zeros((8, width), F32) for _ in range(sums))
    out = lax.fori_loop(0, rows // block, body, start, unroll=3)
    return [jnp.sum(c, axis=0, keepdims=True) for c in out]


def spread(ref, at, width):
    m = ref[at, :]
    return m if width == 128 else jnp.concatenate([m] * (width // 128), axis=1)


def each_block(rows, step):
    def body(i, carry):
        step(ds(i * 16, 16))
        return carry

    lax.fori_loop(0, rows // 16, body, 0, unroll=3)


def accumulate(ref, parts):
    total = jnp.concatenate(parts, axis=0)

    @pl.when(pl.program_id(0) == 0)
    def _():
        ref[...] = total

    @pl.when(pl.program_id(0) != 0)
    def _():
        ref[...] += total


def fill_wide(wide_ref, piece_refs, shape, reverse, change=None, place=peer):
    image_count, row_count, places, cols = shape
    rows = row_count * cols
    width = piece_refs[0].shape[-1]
    span = (row_count * places + 2) * cols
    zero = jnp.zeros((cols, wide_ref.shape[1]), BF)
    column = lax.broadcasted_iota(jnp.int32, (row_count, cols, width), 1).reshape(rows, width)
    for i in range(image_count):
        wide_ref[ds(i * span, cols), :] = zero
        wide_ref[ds((i + 1) * span - cols, cols), :] = zero
        for k, ref in enumerate(piece_refs):
            start = place(k) * rows
            x = ref[i]
            if change is not None:
                x = change(x, ds(i * rows * places + start, rows))
            wide = x.astype(F32)
            left = jnp.where(column == 0, 0.0, pltpu.roll(wide, 1, 0)).astype(BF)
            right = jnp.where(column == cols - 1, 0.0, pltpu.roll(wide, rows - 1, 0)).astype(BF)
            if reverse:
                left, right = right, left
            at = ds(i * span + cols + start, rows)
            wide_ref[at, :width] = left
            wide_ref[at, width : 2 * width] = x.astype(BF)
            wide_ref[at, 2 * width :] = right


def turn_taps(turned_ref, kernel_ref, width):
    n = kernel_ref.shape[1]
    for tap in range(9):
        p, q = divmod(tap, 3)
        turned_ref[p, :, q * n : (q + 1) * n] = kernel_ref[tap * width : (tap + 1) * width, :]


def conv_rows(wide_ref, i, c, shape, product, reverse):
    row_count, places, cols = shape[1:]
    rows = row_count * cols
    start = i * (row_count * places + 2) * cols + c * rows
    total = None
    for p in range(3):
        at = (2 - p if reverse else p) * cols
        term = product(p, wide_ref[ds(start + at, rows), :])
        total = term if total is None else total + term
    return total


def add_up(*xs):
    def body(*refs):
        total = refs[0][...]
        for ref in refs[1:-1]:
            total = total + ref[...]
        refs[-1][...] = total

    return kernel_call(
        "add_up", body, (), list(xs), [VMEM] * len(xs), [(xs[0].shape, F32)], [VMEM], limit=2
    )[0]


def side_by_side(xs):
    def body(*refs):
        width = refs[0].shape[1]
        for k, ref in enumerate(refs[:-1]):
            refs[-1][:, k * width : (k + 1) * width] = ref[...]

    shape = (xs[0].shape[0], xs[0].shape[1] * len(xs))
    return kernel_call(
        "side_by_side", body, (), list(xs), [VMEM] * len(xs), [(shape, F32)], [VMEM], limit=2
    )[0]


def pack_weights(w_trunk, w_hid, w_attn, w_shared, vectors, part, quarter):
    rows, (depth, width) = w_trunk.shape[0], w_hid.shape[1:]
    tasks = w_hid.shape[0]
    block = w_shared.shape[1]
    cuts = width // block
    n = len(vectors)

    def body(trunk_ref, hid_ref, attn_ref, shared_ref, *refs):
        vector_refs = refs[:n]
        first_ref, second_ref, out_ref = refs[n:]
        me = lax.axis_index("task")
        task = jnp.minimum(me, tasks - 1)
        first_ref[...] = trunk_ref[:, lanes_of(me, part)]
        for c in range(cuts):
            here = slice(c * block, (c + 1) * block)
            second_ref[c * depth : (c + 1) * depth, :] = hid_ref[task, :, here]
            second_ref[(cuts + c) * depth : (cuts + c + 1) * depth, :] = attn_ref[task, :, here]
        if quarter:
            second_ref[2 * cuts * depth :, :] = shared_ref[ds(me * quarter, quarter), :]
        out_ref[...] = jnp.zeros_like(out_ref)
        for k, ref in enumerate(vector_refs):
            row = ref[...] if ref.shape[0] == 1 else ref[pl.ds(task, 1), :]
            out_ref[k : k + 1, :] = row

    ins = [w_trunk, w_hid, w_attn, w_shared, *vectors]
    return kernel_call(
        "pack_weights",
        body,
        (),
        ins,
        [VMEM] * len(ins),
        [
            ((rows, part), BF),
            ((2 * cuts * depth + quarter, block), BF),
            ((8, width), F32),
        ],
        [VMEM] * 3,
        limit=56,
    )


def unpack_weights(gathered, depth, width, quarter):
    count, _, block = gathered.shape
    cuts = width // block

    def body(gathered_ref, layers_ref, *outs):
        for k in range(count):
            for c in range(2 * cuts):
                layers_ref[k * depth : (k + 1) * depth, c * block : (c + 1) * block] = gathered_ref[
                    k, c * depth : (c + 1) * depth, :
                ]
            if quarter:
                outs[0][k] = gathered_ref[k, 2 * cuts * depth :, :]

    outs = [((count * depth, 2 * width), BF)]
    if quarter:
        outs.append(((count, quarter, block), BF))
    return kernel_call("unpack_weights", body, (), [gathered], [VMEM], outs, [VMEM] * len(outs))


def gathered_sum(parts, dtype):
    shape = parts.shape[1:]

    def body(parts_ref, out_ref):
        total = parts_ref[0].astype(F32)
        for k in range(1, parts.shape[0]):
            total = total + parts_ref[k].astype(F32)
        out_ref[...] = total.astype(dtype)

    return kernel_call("gathered_sum", body, (), [parts], [VMEM], [(shape, dtype)], [VMEM])[0]


def piece_sum(pieces, dtype):
    def body(*refs):
        total = refs[0][...].astype(F32)
        for ref in refs[1:-1]:
            total = total + ref[...].astype(F32)
        refs[-1][...] = total.astype(dtype)

    return kernel_call(
        "piece_sum", body, (), list(pieces), [VMEM] * len(pieces), [(pieces[0].shape, dtype)], [VMEM]
    )[0]


def blocks_of(whole_ref, out_refs, rows):
    me = lax.axis_index("dp")
    if len(out_refs) == 1:
        out_refs[0][...] = whole_ref[...]
    elif len(out_refs) == 2:
        for k in range(whole_ref.shape[0] // rows):
            at = k // 2 * rows
            out_refs[k % 2][at : at + rows, :] = whole_ref[ds((me ^ k) * rows, rows), :]
    else:
        for k, ref in enumerate(out_refs):
            ref[...] = whole_ref[ds((me ^ k) * rows, rows), :]


def block_shapes(rows, width, pairs):
    count = lax.axis_size("dp")
    if not in_blocks(rows):
        return [((count * rows, width), BF)]
    if pairs:
        return [((count // 2 * rows, width), BF)] * 2
    return [((rows, width), BF)] * count


def add_cut(kept, got, count):
    rows, width = kept.shape[0] // count, kept.shape[1]

    def body(kept_ref, got_ref, *out_refs):
        for k, ref in enumerate(out_refs):
            at = slice(k * rows, (k + 1) * rows)
            ref[...] = (kept_ref[at, :].astype(F32) + got_ref[at, :].astype(F32)).astype(BF)

    return kernel_call(
        "add_cut", body, (), [kept, got], [VMEM] * 2, [((rows, width), BF)] * count, [VMEM] * count
    )


def sum_in_blocks(kept, got):
    rows, width = kept.shape[0] // lax.axis_size("dp"), kept.shape[1]
    outs = block_shapes(rows, width, True)

    def body(kept_ref, got_ref, *refs):
        refs[-1][...] = (kept_ref[...].astype(F32) + got_ref[...].astype(F32)).astype(BF)
        blocks_of(refs[-1], refs[:-1], rows)

    return kernel_call(
        "sum_in_blocks",
        body,
        (),
        [kept, got],
        [VMEM] * 2,
        outs,
        [VMEM] * len(outs),
        [pltpu.VMEM(kept.shape, BF)],
    )


def own_rows(x, image_count, places):
    rows, width = x.shape[0] // image_count // places, x.shape[1]

    def body(x_ref, out_ref):
        for i in range(image_count):
            out_ref[i] = x_ref[ds((i * places + peer(0)) * rows, rows), :]

    return kernel_call(
        "own_rows", body, (), [x], [VMEM], [((image_count, rows, width), x.dtype)], [VMEM]
    )[0]


def by_task(pieces, tasks, dtype, cuts):
    rows, width = pieces[0].shape
    by_row = cuts == rows
    shape = (tasks, width) if by_row else (tasks, rows, width // cuts)

    def body(*refs):
        outs = refs[len(pieces) :]
        for k in range(len(pieces)):
            place = peer(k)

            @pl.when(place < tasks)
            def _(k=k, place=place):
                for c, ref in enumerate(outs):
                    if by_row:
                        ref[pl.ds(place, 1), :] = refs[k][c : c + 1, :].astype(dtype)
                    else:
                        here = slice(c * shape[2], (c + 1) * shape[2])
                        ref[place] = refs[k][:, here].astype(dtype)

    return kernel_call(
        "by_task",
        body,
        (),
        list(pieces),
        [VMEM] * len(pieces),
        [(shape, dtype)] * cuts,
        [VMEM] * cuts,
    )


def lay_out(order, pieces, dtype, along, count=None):
    n = len(pieces)
    shape = list(pieces[0].shape)
    if along == 0 and shape[0] % 16:
        out = jnp.zeros([shape[0] * n] + shape[1:], dtype)
        for k, piece in enumerate(pieces):
            out = lax.dynamic_update_slice_in_dim(out, piece.astype(dtype), order(k) * shape[0], axis=0)
        return out
    if along is None:
        whole = [count or n] + shape
    else:
        whole = list(shape)
        whole[along] *= n

    def body(*refs):
        for k in range(n):
            value = refs[k][...].astype(dtype)
            if along is None:

                @pl.when(order(k) < whole[0])
                def _(k=k, value=value):
                    refs[-1][order(k)] = value

            elif along == 0:
                refs[-1][ds(order(k) * shape[0], shape[0]), :] = value
            else:
                refs[-1][:, ds(order(k) * shape[1], shape[1], 128)] = value

    return kernel_call(
        "lay_out", body, (), list(pieces), [VMEM] * n, [(tuple(whole), dtype)], [VMEM]
    )[0]


def pack_cots(task_cot, trunk_cot, places):
    tasks, image_count, rows, out_width = task_cot.shape
    part = trunk_cot.shape[-1] // places

    def body(task_ref, trunk_ref, *out_refs):
        for k in range(places):
            out_refs[k][...] = task_ref[jnp.minimum(peer(k), tasks - 1)]
            out_refs[places + k][...] = trunk_ref[:, :, lanes_of(peer(k), part)]

    return kernel_call(
        "pack_cots",
        body,
        (),
        [task_cot, trunk_cot],
        [VMEM, VMEM],
        [((image_count, rows, out_width), BF)] * places + [((image_count, rows, part), BF)] * places,
        [VMEM] * (2 * places),
    )


def trunk_forward(marks, images, pieces, shape):
    image_count, row_count, places, cols = shape
    rows = row_count * cols
    part = pieces[0].shape[1]
    depth = sum(p.shape[0] for p in pieces)
    pixels = image_count * places * rows
    in_width = images[0].shape[-1]
    n_images, n_pieces = len(images), len(pieces)

    def body(*refs):
        mark_refs = refs[:n_images]
        image_refs = refs[n_images : 2 * n_images]
        piece_refs = refs[2 * n_images : 2 * n_images + n_pieces]
        outs = refs[2 * n_images + n_pieces :]
        centred_ref, stats_ref, kernel_ref, mask_ref, chosen_ref, whole_ref, wide_ref, pre_ref = outs
        labelled = valid = jnp.zeros((8, part), F32)
        for i in range(image_count):
            for k, ref in enumerate(mark_refs):
                at = ds((i * places + peer(k)) * rows, rows)
                whole_ref[at, :] = image_refs[k][i]
                first = jnp.broadcast_to(ref[i, :, 0:1], (rows, 128))
                second = jnp.broadcast_to(ref[i, :, 1:2], (rows, 128))
                mask_ref[at, :] = first
                chosen_ref[at, :] = jnp.where(lax.axis_index("task") == 0, first, second)
                labelled += fold(first)
                valid += fold(second)
        counts = [jnp.sum(c, axis=0, keepdims=True) for c in (labelled, valid)]
        for k, ref in enumerate(piece_refs):
            at = ds((lax.axis_index("dp") ^ k) * ref.shape[0], ref.shape[0]) if n_pieces > 1 else slice(None)
            kernel_ref[at, :] = ref[...]
        fill_wide(wide_ref, image_refs, shape, False)
        block = 3 * in_width

        def chunk(c, carry):
            for i in range(image_count):
                value = conv_rows(
                    wide_ref,
                    i,
                    c,
                    shape,
                    lambda p, x: dot(x, kernel_ref[p * block : (p + 1) * block, :]),
                    False,
                )
                pre_ref[ds((i * places + c) * rows, rows), :] = value
            return carry

        lax.fori_loop(0, places, chunk, 0)

        def moments(at):
            v = pre_ref[at, :]
            mv = mask_ref[at, :] * v
            return mv, mv * v, v

        sums = sweep(pixels, part, moments, 3)
        mean = sums[2] / pixels
        stats_ref[...] = jnp.concatenate(sums[:2] + counts + [mean] * 4, axis=0)

        def centre(at):
            centred_ref[at, :] = (pre_ref[at, :] - mean).astype(BF)

        each_block(pixels, centre)

    return kernel_call(
        "trunk_forward",
        body,
        (),
        [*marks, *images, *pieces],
        [VMEM] * (2 * n_images + n_pieces),
        [
            ((pixels, part), BF),
            ((8, part), F32),
            ((depth, part), BF),
            ((pixels, 128), F32),
            ((pixels, 128), F32),
            ((pixels, in_width), BF),
        ],
        [VMEM] * 6,
        [
            pltpu.VMEM((image_count * (row_count * places + 2) * cols, 3 * in_width), BF),
            pltpu.VMEM((pixels, part), F32),
        ],
        flops=2 * pixels * depth * part,
    )


def rows_spec(rows, width):
    return pl.BlockSpec((rows, width), lambda i: (i, 0))


def fixed_spec(shape):
    return pl.BlockSpec(shape, lambda i: (0,) * len(shape))


def centre_on_first(value_ref, centre_ref, centred_ref):
    @pl.when(pl.program_id(0) == 0)
    def _():
        rows = value_ref.shape[0]
        (total,) = sweep(rows, value_ref.shape[1], lambda at: (value_ref[at, :],), 1)
        centre_ref[...] = total / rows

    centre = centre_ref[...]

    def step(at):
        centred_ref[at, :] = (value_ref[at, :] - centre).astype(BF)

    each_block(value_ref.shape[0], step)


def feat_hid(scaled, stats, totals, vectors, mask, kernel, rows):
    pixels, part = scaled[0].shape
    n = len(scaled)
    mid = part * n
    out_mid = mid

    def body(*refs):
        scaled_refs = refs[:n]
        stats_ref, totals_ref, vectors_ref, mask_ref, kernel_ref = refs[n : 5 + n]
        feat_ref, centred_ref, centre_ref, sums_ref, affine_ref, hid_ref = refs[5 + n :]

        @pl.when(pl.program_id(0) == 0)
        def _():
            count = jnp.maximum(totals_ref[2:3, :], 1.0)
            mean, rstd = scales(totals_ref[0:1, :], totals_ref[1:2, :], count)
            for k in range(n):
                here = slice(k * part, (k + 1) * part)
                at = lanes_of(peer(k), part)
                slope = rstd[:, here] * vectors_ref[TRUNK_GAIN, at]
                affine_ref[0:1, here] = slope
                affine_ref[1:2, here] = (stats_ref[4:5, here] - mean[:, here]) * slope + vectors_ref[TRUNK_BIAS, at]

        def activate(at):
            for k in range(n):
                here = slice(k * part, (k + 1) * part)
                v = scaled_refs[k][at, :].astype(F32) * affine_ref[0:1, here] + affine_ref[1:2, here]
                feat_ref[at, lanes_of(peer(k), part)] = gelu(v).astype(BF)

        each_block(rows, activate)
        hid_ref[...] = dot(feat_ref[...], kernel_ref[...])

        def moments(at):
            v = hid_ref[at, :]
            mv = spread(mask_ref, at, out_mid) * v
            return mv, mv * v

        accumulate(sums_ref, sweep(rows, out_mid, moments, 2))
        centre_on_first(hid_ref, centre_ref, centred_ref)

    return kernel_call(
        "feat_hid",
        body,
        (pixels // rows,),
        [*scaled, stats, totals, vectors, mask, kernel],
        [rows_spec(rows, part)] * n
        + [fixed_spec(x.shape) for x in (stats, totals, vectors)]
        + [rows_spec(rows, 128), pl.BlockSpec((mid, out_mid), lambda i: (0, 0))],
        [
            ((pixels, mid), BF),
            ((pixels, out_mid), BF),
            ((1, out_mid), F32),
            ((2, out_mid), F32),
        ],
        [
            rows_spec(rows, mid),
            rows_spec(rows, out_mid),
            fixed_spec((1, out_mid)),
            fixed_spec((2, out_mid)),
        ],
        [pltpu.VMEM((2, mid), F32), pltpu.VMEM((rows, out_mid), F32)],
        flops=2 * pixels * mid * out_mid,
    )


def task_count(totals_ref):
    chosen = jnp.where(lax.axis_index("task") == 0, totals_ref[2:3, 0:1], totals_ref[3:4, 0:1])
    return jnp.maximum(chosen, 1.0)


def normed_rows(sums, count, centre):
    mean, rstd = scales(sums[0:1, :], sums[1:2, :], count)
    return rstd, (centre - mean) * rstd


def hid_gate(hid, centre, sums, totals, vectors, mask, kernel, rows):
    pixels, mid = hid.shape

    def body(*refs):
        hid_ref, middle_ref, sums_ref, totals_ref, vectors_ref, mask_ref, kernel_ref = refs[:7]
        hidden_ref, centred_ref, centre_ref, out_ref, gate_ref = refs[7:]
        count = task_count(totals_ref)
        gain, bias = vectors_ref[HID_GAIN, :], vectors_ref[HID_BIAS, :]
        scale, shift = normed_rows(sums_ref[...], count, middle_ref[...])
        scale, shift = scale * gain, shift * gain + bias

        def activate(at):
            hidden_ref[at, :] = gelu(hid_ref[at, :].astype(F32) * scale + shift).astype(BF)

        each_block(rows, activate)
        gate_ref[...] = dot(hidden_ref[...], kernel_ref[...])

        def moments(at):
            v = gate_ref[at, :]
            mv = spread(mask_ref, at, mid) * v
            return mv, mv * v

        accumulate(out_ref, sweep(rows, mid, moments, 2))
        centre_on_first(gate_ref, centre_ref, centred_ref)

    wide = rows_spec(rows, mid)
    return kernel_call(
        "hid_gate",
        body,
        (pixels // rows,),
        [hid, centre, sums, totals, vectors, mask, kernel],
        [wide]
        + [fixed_spec(x.shape) for x in (centre, sums, totals, vectors)]
        + [rows_spec(rows, 128), pl.BlockSpec((mid, mid), lambda i: (0, 1))],
        [((pixels, mid), BF), ((pixels, mid), BF), ((1, mid), F32), ((2, mid), F32)],
        [wide, wide, fixed_spec((1, mid)), fixed_spec((2, mid))],
        [pltpu.VMEM((rows, mid), F32)],
        flops=2 * pixels * mid * mid,
    )


def feature_back(cot, mask, kernels, shape):
    image_count, row_count, places, cols = shape
    rows = row_count * cols
    out_width = cot[0].shape[-1]
    mid = sum(x.size for x in kernels) // out_width // 9
    pixels = image_count * places * rows
    n, m = len(cot), len(kernels)

    def body(*refs):
        cot_refs = refs[:n]
        mask_ref = refs[n]
        quarter_refs = refs[1 + n : 1 + n + m]
        out_ref, kernel_ref, wide_ref, turned_ref = refs[1 + n + m :]
        blocks, quarter = quarter_refs[0].shape[:2]
        for k, ref in enumerate(quarter_refs):
            for j in range(blocks):
                kernel_ref[ds((j * m + (peer(k) if m > 1 else 0)) * quarter, quarter), :] = ref[j]
        turn_taps(turned_ref, kernel_ref, mid)
        fill_wide(
            wide_ref,
            cot_refs,
            shape,
            True,
            lambda x, at: x.astype(F32) * spread(mask_ref, at, out_width),
        )

        def chunk(c, carry):
            for i in range(image_count):
                value = conv_rows(
                    wide_ref, i, c, shape, lambda p, x: dot_nt(x, turned_ref[p]), True
                )
                out_ref[ds((i * places + c) * rows, rows), :] = value.astype(BF)
            return carry

        lax.fori_loop(0, places, chunk, 0)

    return kernel_call(
        "feature_back",
        body,
        (),
        [*cot, mask, *kernels],
        [VMEM] * (n + 1 + m),
        [((pixels, mid), BF), ((9 * mid, out_width), BF)],
        [VMEM] * 2,
        [
            pltpu.VMEM((image_count * (row_count * places + 2) * cols, 3 * out_width), BF),
            pltpu.VMEM((3, mid, 3 * out_width), BF),
        ],
        limit=24,
        flops=2 * pixels * 9 * mid * out_width,
    )


def gate_back(gate, centre, sums, totals, vectors, feature_grad, feat, rows):
    pixels, mid = gate.shape

    def body(gate_ref, centre_ref, sums_ref, totals_ref, vectors_ref, grad_ref, feat_ref, *outs):
        features_ref, gate_grad_ref, share_ref, out_ref = outs
        scale, shift = normed_rows(sums_ref[...], task_count(totals_ref), centre_ref[...])
        slope = 0.5 * vectors_ref[ATTN_GAIN, :]
        offset = 0.5 * vectors_ref[ATTN_BIAS, :]

        def step(at):
            normed = gate_ref[at, :].astype(F32) * scale + shift
            t = jnp.tanh(normed * slope + offset)
            attention = 0.5 + 0.5 * t
            features = attention * feat_ref[at, :].astype(F32)
            features_ref[at, :] = features.astype(BF)
            grad = grad_ref[at, :].astype(F32)
            share_ref[at, :] = (grad * attention).astype(BF)
            gate_grad = grad * features * (0.5 - 0.5 * t)
            gate_grad_ref[at, :] = gate_grad.astype(BF)
            return gate_grad, gate_grad * normed

        accumulate(out_ref, sweep(rows, mid, step, 2))

    wide = rows_spec(rows, mid)
    return kernel_call(
        "gate_back",
        body,
        (pixels // rows,),
        [gate, centre, sums, totals, vectors, feature_grad, feat],
        [wide] + [fixed_spec(x.shape) for x in (centre, sums, totals, vectors)] + [wide, wide],
        [((pixels, mid), BF)] * 3 + [((2, mid), F32)],
        [wide] * 3 + [fixed_spec((2, mid))],
    )


def back_rows(gain, sums, count, centre, back):
    rstd, shift = normed_rows(sums, count, centre)
    scale = gain * rstd
    tilt = scale * back[1:2, :] / count
    return scale, scale * back[0:1, :] / count + tilt * shift, tilt * rstd


def hid_back(grad, gate, mask, centre, sums, totals, vectors, back, hid, h_centre, h_sums, kernel, rows):
    pixels, mid = grad.shape

    def body(*refs):
        grad_ref, gate_ref, mask_ref, centre_ref, sums_ref, totals_ref, vectors_ref, back_ref = refs[:8]
        hid_ref, h_centre_ref, h_sums_ref, kernel_ref = refs[8:12]
        pre_ref, act_ref, out_ref, value_ref = refs[12:]
        count = task_count(totals_ref)
        h_gain, h_bias = vectors_ref[HID_GAIN, :], vectors_ref[HID_BIAS, :]
        scale, lean, tilt = back_rows(
            vectors_ref[ATTN_GAIN, :], sums_ref[...], count, centre_ref[...], back_ref[...]
        )

        def step(at):
            lost = spread(mask_ref, at, mid) * (lean + gate_ref[at, :].astype(F32) * tilt)
            pre_ref[at, :] = (grad_ref[at, :].astype(F32) * scale - lost).astype(BF)

        each_block(rows, step)
        value_ref[...] = dot_nt(pre_ref[...], kernel_ref[...])
        h_scale, h_shift = normed_rows(h_sums_ref[...], count, h_centre_ref[...])

        def slope(at):
            x = hid_ref[at, :].astype(F32) * h_scale + h_shift
            value = value_ref[at, :] * gelu_slope(x * h_gain + h_bias)
            act_ref[at, :] = value.astype(BF)
            return value, value * x

        accumulate(out_ref, sweep(rows, mid, slope, 2))

    wide = rows_spec(rows, mid)
    return kernel_call(
        "hid_back",
        body,
        (pixels // rows,),
        [grad, gate, mask, centre, sums, totals, vectors, back, hid, h_centre, h_sums, kernel],
        [wide, wide, rows_spec(rows, 128)]
        + [fixed_spec(x.shape) for x in (centre, sums, totals, vectors, back)]
        + [wide]
        + [fixed_spec(x.shape) for x in (h_centre, h_sums)]
        + [pl.BlockSpec((mid, mid), lambda i: (0, 1))],
        [((pixels, mid), BF), ((pixels, mid), BF), ((2, mid), F32)],
        [wide, wide, fixed_spec((2, mid))],
        [pltpu.VMEM((rows, mid), F32)],
        flops=2 * pixels * mid * mid,
    )


def feat_back(act_grad, hid, mask, centre, sums, totals, vectors, back, share, kernel, rows, tasks):
    pixels, mid = act_grad.shape
    half = mid // 2

    def body(*refs):
        act_ref, hid_ref, mask_ref, centre_ref, sums_ref, totals_ref = refs[:6]
        vectors_ref, back_ref, share_ref, kernel_ref, pre_ref, kept_ref, sent_ref, part_ref = refs[6:]
        active = jnp.where(lax.axis_index("task") < tasks, 1.0, 0.0)
        scale, lean, tilt = back_rows(
            vectors_ref[HID_GAIN, :],
            sums_ref[...],
            task_count(totals_ref),
            centre_ref[...],
            back_ref[...],
        )

        def step(at):
            lost = spread(mask_ref, at, mid) * (lean + hid_ref[at, :].astype(F32) * tilt)
            pre_ref[at, :] = (act_ref[at, :].astype(F32) * scale - lost).astype(BF)

        each_block(rows, step)
        part_ref[...] = dot_nt(pre_ref[...], kernel_ref[...])

        def add(at):
            for ref, here in zip((kept_ref, sent_ref), halves(0, half, 128), strict=True):
                value = part_ref[at, here] + share_ref[at, here].astype(F32)
                ref[at, :] = (value * active).astype(BF)

        each_block(rows, add)

    wide = rows_spec(rows, mid)
    return kernel_call(
        "feat_back",
        body,
        (pixels // rows,),
        [act_grad, hid, mask, centre, sums, totals, vectors, back, share, kernel],
        [wide, wide, rows_spec(rows, 128)]
        + [fixed_spec(x.shape) for x in (centre, sums, totals, vectors, back)]
        + [wide]
        + [pl.BlockSpec((mid, mid), lambda i: (0, 0))],
        [((pixels, mid), BF), ((pixels, half), BF), ((pixels, half), BF)],
        [wide, rows_spec(rows, half), rows_spec(rows, half)],
        [pltpu.VMEM((rows, mid), F32)],
        flops=2 * pixels * mid * mid,
    )


def add_halve(level, kept, got, rows):
    pixels, width = kept.shape
    half = width // 2

    def body(kept_ref, got_ref, a_ref, b_ref):
        for ref, here in zip((a_ref, b_ref), halves(level, half, 128), strict=True):
            ref[...] = (kept_ref[:, here].astype(F32) + got_ref[:, here].astype(F32)).astype(BF)

    wide, slim = rows_spec(rows, width), rows_spec(rows, half)
    return kernel_call(
        "add_halve",
        body,
        (pixels // rows,),
        [kept, got],
        [wide, wide],
        [((pixels, half), BF)] * 2,
        [slim, slim],
    )


def trunk_back(parts, cots, trunk, stats, totals, vectors, shape):
    image_count, row_count, places, cols = shape
    rows = row_count * cols
    pixels, width = trunk.shape
    n = len(parts)

    def body(*refs):
        part_refs = refs[:n]
        cot_refs = refs[n : n + places]
        trunk_ref, stats_ref, totals_ref, vectors_ref, grad_ref, out_ref = refs[n + places :]
        lanes = lanes_of(peer(0), width)
        gain, bias = vectors_ref[TRUNK_GAIN, lanes], vectors_ref[TRUNK_BIAS, lanes]
        totals = totals_ref[:, :width]
        count = jnp.maximum(totals[2:3, :], 1.0)
        scale, shift = normed_rows(totals, count, stats_ref[4:5, :])
        total = [0.0, 0.0]
        for i in range(image_count):
            for k, cot_ref in enumerate(cot_refs):
                start = (i * places + peer(k)) * rows

                def step(at, start=start, cot_ref=cot_ref, i=i):
                    here = ds(start + at.start, at.size)
                    x = trunk_ref[here, :].astype(F32) * scale + shift
                    grad = cot_ref[i, at, :].astype(F32)
                    for ref in part_refs:
                        grad = grad + ref[here, :].astype(F32)
                    grad = grad * gelu_slope(x * gain + bias)
                    grad_ref[here, :] = grad.astype(BF)
                    return grad, grad * x

                found = sweep(rows, width, step, 2)
                total = [a + b for a, b in zip(total, found, strict=True)]
        out_ref[...] = jnp.concatenate(total, axis=0)

    return kernel_call(
        "trunk_back",
        body,
        (),
        [*parts, *cots, trunk, stats, totals, vectors],
        [VMEM] * (n + places + 4),
        [((pixels, width), BF), ((2, width), F32)],
        [VMEM] * 2,
    )


def trunk_weights(images, grad, trunk, mask, stats, totals, vectors, back, shape):
    image_count, row_count, places, cols = shape
    rows = row_count * cols
    in_width = images.shape[-1]
    pixels, part = grad.shape
    depth = 9 * in_width // lax.axis_size("dp")
    outs = block_shapes(depth, part, False)
    span = (row_count * places + 2) * cols
    whole = row_count * places * cols

    def body(*refs):
        images_ref, grad_ref, trunk_ref, mask_ref, stats_ref, totals_ref, vectors_ref, back_ref = refs[:8]
        out_ref = refs[8]
        weight_ref, wide_ref = refs[-2:]
        totals = totals_ref[:, :part]
        count = jnp.maximum(totals[2:3, :], 1.0)
        scale, lean, tilt = back_rows(
            vectors_ref[TRUNK_GAIN, lanes_of(peer(0), part)], totals, count, stats_ref[4:5, :], back_ref[...]
        )

        def step(at):
            lost = mask_ref[at, :] * (lean + trunk_ref[at, :].astype(F32) * tilt)
            out_ref[at, :] = (grad_ref[at, :].astype(F32) * scale - lost).astype(BF)

        each_block(pixels, step)
        fill_wide(
            wide_ref,
            [images_ref.at[:, k] for k in range(places)],
            shape,
            False,
            place=lambda k: k,
        )
        for p in range(3):
            total = None
            for i in range(image_count):
                term = dot_tn(
                    wide_ref[ds(i * span + p * cols, whole), :], out_ref[ds(i * whole, whole), :]
                )
                total = term if total is None else total + term
            weight_ref[p * 3 * in_width : (p + 1) * 3 * in_width, :] = total.astype(BF)
        blocks_of(weight_ref, refs[9:-2], depth)

    return kernel_call(
        "trunk_weights",
        body,
        (),
        [images.reshape(image_count, places, rows, in_width), grad, trunk, mask, stats, totals, vectors, back],
        [VMEM] * 8,
        [((pixels, part), BF), *outs],
        [VMEM] * (1 + len(outs)),
        [
            pltpu.VMEM((9 * in_width, part), BF),
            pltpu.VMEM((image_count * span, 3 * in_width), BF),
        ],
        flops=2 * pixels * 9 * in_width * part,
    )


def image_back(grad, kernel, shape):
    image_count, row_count, places, cols = shape
    rows = row_count * cols
    part = grad.shape[-1]
    in_width = kernel.shape[0] // 9

    def body(grad_ref, kernel_ref, *refs):
        out_refs = refs[:places]
        wide_ref, turned_ref = refs[places:]
        turn_taps(turned_ref, kernel_ref, in_width)
        pieces = [grad_ref.at[:, k] for k in range(places)]
        fill_wide(wide_ref, pieces, shape, True, place=lambda k: k)
        for k, ref in enumerate(out_refs):
            for i in range(image_count):
                value = conv_rows(
                    wide_ref, i, peer(k), shape, lambda p, x: dot_nt(x, turned_ref[p]), True
                )
                ref[i] = value.astype(BF)

    return kernel_call(
        "image_back",
        body,
        (),
        [grad.reshape(image_count, places, rows, part), kernel],
        [VMEM, VMEM],
        [((image_count, rows, in_width), BF)] * places,
        [VMEM] * places,
        [
            pltpu.VMEM((image_count * (row_count * places + 2) * cols, 3 * part), BF),
            pltpu.VMEM((3, in_width, 3 * part), BF),
        ],
        flops=2 * grad.size * 9 * in_width,
    )


def task_forward(features, kernel, shape):
    image_count, row_count, places, cols = shape
    rows = row_count * cols
    mid = features.shape[-1]
    out_width = kernel.shape[1]
    block = 3 * mid

    def body(features_ref, kernel_ref, *refs):
        out_refs = refs[:places]
        (wide_ref,) = refs[places:]
        pieces = [features_ref.at[:, k] for k in range(places)]
        fill_wide(wide_ref, pieces, shape, False, place=lambda k: k)
        for k, ref in enumerate(out_refs):
            for i in range(image_count):
                value = conv_rows(
                    wide_ref,
                    i,
                    peer(k),
                    shape,
                    lambda p, x: dot(x, kernel_ref[p * block : (p + 1) * block, :]),
                    False,
                )
                ref[i] = value.astype(BF)

    return kernel_call(
        "task_forward",
        body,
        (),
        [features.reshape(image_count, places, rows, mid), kernel],
        [VMEM, VMEM],
        [((image_count, rows, out_width), BF)] * places,
        [VMEM] * places,
        [
            pltpu.VMEM((image_count * (row_count * places + 2) * cols, 3 * mid), BF),
        ],
        limit=24,
        flops=2 * features.size * 9 * out_width,
    )


def add_split(level, kept, got, blocks):
    rows, width = kept.shape
    half = rows // blocks // 2

    def body(kept_ref, got_ref, a_ref, b_ref):
        bit = (lax.axis_index("task") >> level) % 2
        for ref, which in ((a_ref, bit), (b_ref, 1 - bit)):
            for j in range(blocks):
                at = ds((2 * j + which) * half, half)
                value = kept_ref[at, :].astype(F32) + got_ref[at, :].astype(F32)
                ref[j] = value.astype(BF)

    return kernel_call(
        "add_split",
        body,
        (),
        [kept, got],
        [VMEM, VMEM],
        [((blocks, half, width), BF)] * 2,
        [VMEM] * 2,
    )


def layer_weights(pairs):
    mid = pairs[0][0].shape[1]
    rows = mid // lax.axis_size("dp")
    outs = block_shapes(rows, mid * len(pairs), True)
    n = 2 * len(pairs)

    def body(*refs):
        for k in range(len(pairs)):
            value = dot_tn(refs[2 * k][...], refs[2 * k + 1][...])
            refs[-1][:, k * mid : (k + 1) * mid] = value.astype(BF)
        blocks_of(refs[-1], refs[n:-1], rows)

    ins = [x for pair in pairs for x in pair]
    return kernel_call(
        "layer_weights",
        body,
        (),
        ins,
        [VMEM] * n,
        outs,
        [VMEM] * len(outs),
        [pltpu.VMEM((mid, mid * len(pairs)), BF)],
        flops=2 * pairs[0][0].size * mid * len(pairs),
    )


def shared_weights(cot, mask, features, shape, tasks):
    image_count, row_count, places, cols = shape
    rows = row_count * cols
    out_width = cot[0].shape[-1]
    mid = features.shape[-1]
    n = len(cot)
    half = out_width // 2
    span = (row_count * places + 2) * cols
    whole = row_count * places * cols

    def body(*refs):
        cot_refs = refs[:n]
        mask_ref, features_ref, kept_ref, sent_ref, wide_ref, part_ref = refs[n:]
        active = jnp.where(lax.axis_index("task") < tasks, 1.0, 0.0)
        fill_wide(
            wide_ref,
            cot_refs,
            shape,
            True,
            lambda x, at: x.astype(F32) * spread(mask_ref, at, out_width) * active,
        )
        for tap in range(9):
            p, q = divmod(tap, 3)
            total = None
            for i in range(image_count):
                term = dot_tn(
                    features_ref[ds(i * whole, whole), :],
                    wide_ref[
                        ds(i * span + (2 - p) * cols, whole), q * out_width : (q + 1) * out_width
                    ],
                )
                total = term if total is None else total + term
            part_ref[...] = total
            for ref, here in zip((kept_ref, sent_ref), halves(0, half, 128), strict=True):
                ref[tap * mid : (tap + 1) * mid, :] = part_ref[:, here].astype(BF)

    return kernel_call(
        "shared_weights",
        body,
        (),
        [*cot, mask, features],
        [VMEM] * (n + 2),
        [((9 * mid, half), BF)] * 2,
        [VMEM, VMEM],
        [
            pltpu.VMEM((image_count * span, 3 * out_width), BF),
            pltpu.VMEM((mid, out_width), F32),
        ],
        flops=2 * features.size * 9 * out_width,
    )


def shards(
    images,
    w_trunk,
    trunk_gain,
    trunk_bias,
    w_hid,
    hid_gain,
    hid_bias,
    w_attn,
    attn_gain,
    attn_bias,
    w_shared,
    labels,
    depth_valid,
    trunk_cot,
    task_cot,
):
    image_count, row_count, cols, in_width = images.shape
    mid = w_trunk.shape[1]
    out_width = w_shared.shape[1]
    tasks, depth, width = w_hid.shape
    places = lax.axis_size("task")
    assert tasks <= places
    part = mid // places
    me = lax.axis_index("task")
    rows = row_count * cols
    shape = (image_count, row_count, places, cols)
    blocks = lax.axis_size("dp")

    quarter = w_shared.shape[0] // places
    staged = quarter % 16 == 0
    vectors = [trunk_gain[None], trunk_bias[None], hid_gain, hid_bias, attn_gain, attn_bias]
    first, second, vectors = pack_weights(
        w_trunk, w_hid, w_attn, w_shared, vectors, part, quarter * staged
    )
    trunk_shards = gather_dp(first)
    gathered = lax.all_gather(second, "dp", axis=0, tiled=False)
    image_pieces = others(images.reshape(image_count, rows, in_width), "task")
    marks = jnp.stack([(labels >= 0).astype(F32), depth_valid.astype(F32)], axis=-1)
    mark_pieces = others(marks.reshape(image_count, rows, 2), "task")
    trunk_shards, image_pieces, mark_pieces, trunk_cot, task_cot = together(
        trunk_shards, image_pieces, mark_pieces, trunk_cot, task_cot
    )

    trunk, own_stats, w_slice, labelled, mask, all_images = trunk_forward(
        mark_pieces, image_pieces, trunk_shards, shape
    )
    hop, trunk = together(first_hop(own_stats), trunk)
    stats = side_by_side(fan(own_stats, hop))
    scaled = fan(trunk)
    totals = sum_dp(stats)
    totals, gathered = together(totals, gathered)
    layers, *quarters = unpack_weights(gathered, depth, width, quarter * staged)
    if staged:
        hop = first_hop(quarters[0])
    feat, hid, hid_centre, sums = feat_hid(scaled, stats, totals, vectors, mask, layers, rows)
    sums, trunk_cot, task_cot = together(sums, trunk_cot, task_cot)
    cots = pack_cots(
        task_cot.reshape(tasks, image_count, rows, out_width),
        trunk_cot.reshape(image_count, rows, mid),
        places,
    )
    cot_pieces = [swap(c, "task", k) if k else c for k, c in enumerate(cots[:places])]
    slice_cots = [swap(c, "task", k) if k else c for k, c in enumerate(cots[places:])]
    if staged:
        hid_totals, hop = sum_dp(sums, lambda: hop)
        quarters = fan(quarters[0], hop)
    else:
        hid_totals = sum_dp(sums)
        quarters = [lax.all_gather(w_shared, "dp", axis=0, tiled=True)[None]]
    hidden, gate, gate_centre, sums = hid_gate(
        hid, hid_centre, hid_totals, totals, vectors, mask, layers, rows
    )
    gate_totals, (feature_grad, full_shared) = sum_dp(
        sums, lambda: feature_back(cot_pieces, mask, quarters, shape)
    )
    features, gate_grad, share, sums = gate_back(
        gate, gate_centre, gate_totals, totals, vectors, feature_grad, feat, rows
    )

    sums, features = together(sums, features)
    gate_sums, (shared_kept, sent) = sum_dp(
        sums, lambda: shared_weights(cot_pieces, mask, features, shape, tasks)
    )
    pre_grad, act_grad, sums = hid_back(
        gate_grad, gate, mask, gate_centre, gate_totals, totals, vectors, gate_sums, hid, hid_centre, hid_totals, layers, rows
    )
    shared_got = swap(sent, "task", 1)
    sums, features, shared_got = together(sums, features, shared_got)

    def beside():
        return task_forward(features, full_shared, shape), halve_shared(1, shared_kept, shared_got)

    def halve_shared(level, kept, got):
        if level == levels("task"):
            return kept, got
        kept, got = kept.reshape(-1, out_width // 2), got.reshape(-1, out_width // 2)
        if kept.shape[0] // blocks // 2 % 16 == 0:
            return add_split(level, kept, got, blocks)
        both = (kept.astype(F32) + got.astype(F32)).astype(BF)
        both = both.reshape(blocks, 2, -1, out_width // 2)
        bit = (me >> level) % 2
        return (
            lax.dynamic_index_in_dim(both, bit, 1, keepdims=False),
            lax.dynamic_index_in_dim(both, 1 - bit, 1, keepdims=False),
        )

    hid_sums, (task_parts, (shared_kept, sent)) = sum_dp(sums, beside)
    for level in range(1, levels("task")):
        shared_got = swap(sent, "task", 1 << level)
        shared_kept, sent = halve_shared(level + 1, shared_kept, shared_got)
    hid_pre_grad, kept, sent = feat_back(
        act_grad, hid, mask, hid_centre, hid_totals, totals, vectors, hid_sums, share, layers, rows, tasks
    )
    got = swap(sent, "task", 1)
    for level in range(1, levels("task")):
        kept, sent = add_halve(level, kept, got, rows)
        if level == 1:
            sent, shared_kept, hidden, pre_grad, feat, hid_pre_grad = together(
                sent, shared_kept, hidden, pre_grad, feat, hid_pre_grad
            )
        got = swap(sent, "task", 1 << level)
    shared_parts = sum_in_blocks(
        shared_kept.reshape(-1, out_width // 2), shared_got.reshape(-1, out_width // 2)
    )
    layer_parts = layer_weights([(hidden, pre_grad), (feat, hid_pre_grad)])
    shared_grad = scatter_dp(shared_parts)
    layer_grads = scatter_dp(layer_parts)
    act_grad, sums = trunk_back([kept, got], slice_cots, trunk, own_stats, totals, vectors, shape)
    sums, task_parts = together(sums, task_parts)
    trunk_sums = sum_dp(sums)
    trunk_sums, layer_grads = together(trunk_sums, layer_grads)
    trunk_pre_grad, *weight_parts = trunk_weights(
        all_images, act_grad, trunk, labelled, own_stats, totals, vectors, trunk_sums, shape
    )
    weight_parts, trunk_sums, gate_sums, hid_sums, feat, layer_grads, shared_grad = together(
        weight_parts, trunk_sums, gate_sums, hid_sums, feat, layer_grads, shared_grad
    )
    trunk_grad = scatter_dp(weight_parts)
    image_parts = image_back(trunk_pre_grad, w_slice, shape)
    image_parts = [swap(piece, "task", k) if k else piece for k, piece in enumerate(image_parts)]
    trunk_out = own_rows(feat, image_count, places)
    trunk_out = trunk_out.reshape(image_count, row_count, cols, mid)
    task_parts = [swap(piece, "task", k) if k else piece for k, piece in enumerate(task_parts)]
    task_out = lay_out(peer, task_parts, BF, None, tasks)
    task_out = task_out.reshape(tasks, image_count, row_count, cols, out_width)
    layer_grads = fan(layer_grads)
    for level in reversed(range(levels("task"))):
        pair = [shared_grad, swap(shared_grad, "task", 1 << level)]
        last = level == 0
        shared_grad = lay_out(
            lambda k, level=level: (lax.axis_index("task") >> level) % 2 ^ k,
            pair,
            F32 if last else BF,
            1 if last else 0,
        )
    attn_grad, hid_grad = by_task(layer_grads, tasks, F32, 2)
    attn_bias_grad, attn_gain_grad = by_task(fan(gate_sums), tasks, F32, 2)
    hid_bias_grad, hid_gain_grad = by_task(fan(hid_sums), tasks, F32, 2)
    trunk_sums = lay_out(lambda k: slice_of(peer(k)), fan(trunk_sums), F32, 1)
    image_grad = piece_sum(image_parts, BF).reshape(images.shape)
    trunk_grad = lay_out(lambda k: slice_of(peer(k)), fan(trunk_grad), F32, 1)
    return (
        trunk_out,
        task_out,
        image_grad,
        trunk_grad,
        trunk_sums[1],
        trunk_sums[0],
        hid_grad,
        hid_gain_grad,
        hid_bias_grad,
        attn_grad,
        attn_gain_grad,
        attn_bias_grad,
        shared_grad,
    )


def solution(mesh):
    rows = P("dp", "task", None, None)
    task_rows = P(None, "dp", "task", None, None)
    flat, stacked = P("dp", None), P(None, "dp", None)
    pixel = P("dp", "task", None)
    return jax.shard_map(
        shards,
        mesh=mesh,
        in_specs=(
            rows,
            flat,
            P(),
            P(),
            stacked,
            P(),
            P(),
            stacked,
            P(),
            P(),
            flat,
            pixel,
            pixel,
            rows,
            task_rows,
        ),
        out_specs=(
            rows,
            task_rows,
            rows,
            flat,
            P(),
            P(),
            stacked,
            P(),
            P(),
            stacked,
            P(),
            P(),
            flat,
        ),
        check_vma=False,
    )
```

```python
import math

import jax
import jax.numpy as jnp
from jax import lax
from jax.experimental import pallas as pl
from jax.experimental.pallas import tpu as pltpu
from jax.sharding import PartitionSpec as P

EPS = 1e-05
BF = jnp.bfloat16
F32 = jnp.float32
ROOT = math.sqrt(2.0 / math.pi)
CUBE = 0.044715
VMEM = pl.BlockSpec(memory_space=pltpu.VMEM)
TRUNK_GAIN, TRUNK_BIAS, HID_GAIN, HID_BIAS, ATTN_GAIN, ATTN_BIAS = (slice(k, k + 1) for k in range(6))


def swap(x, axis, step):
    count = lax.axis_size(axis)
    return lax.ppermute(x, axis, [(i, i ^ step) for i in range(count)])


def levels(axis):
    count = lax.axis_size(axis)
    assert count & (count - 1) == 0
    return count.bit_length() - 1


def slice_of(place):
    out = 0
    for bit in range(levels("task")):
        out = out * 2 + (place >> bit) % 2
    return out


def dp_steps():
    bits, low, out = levels("dp"), 1, []
    while low < bits:
        out.append([1 << low] + ([2 << low, 3 << low] if low + 1 < bits else []))
        low += 2
    return out + ([[1]] if bits else [])


def sum_dp(x, work=None):
    steps = dp_steps()
    for step in steps[:-1]:
        x = add_up(x, *[swap(x, "dp", s) for s in step])
    done = work() if work else None
    if work:
        x, done = together(x, done)
    for step in steps[-1:]:
        x = add_up(x, *[swap(x, "dp", s) for s in step])
    return (x, done) if work else x


def together(*xs):
    return lax.optimization_barrier(xs)


def others(x, axis):
    return [x] + [swap(x, axis, k) for k in range(1, lax.axis_size(axis))]


def in_blocks(rows):
    return rows % 16 == 0 and lax.axis_size("dp") <= 8


def gather_dp(x):
    if in_blocks(x.shape[0]):
        return others(x, "dp")
    return [lax.all_gather(x, "dp", axis=0, tiled=True)]


def scatter_dp(parts):
    count = lax.axis_size("dp")
    if len(parts) == 1:
        whole = parts[0].reshape((count, -1) + parts[0].shape[1:])
        return gathered_sum(lax.all_to_all(whole, "dp", 0, 0, tiled=True), BF)
    if len(parts) == 2 and count > 2:
        parts = add_cut(parts[0], swap(parts[1], "dp", 1), count // 2)
        return piece_sum([swap(p, "dp", 2 * k) if k else p for k, p in enumerate(parts)], BF)
    return piece_sum([swap(p, "dp", k) if k else p for k, p in enumerate(parts)], BF)


def first_hop(x):
    return swap(x, "task", 2)


def relay(x, hop=None):
    near = stack_two(x, first_hop(x) if hop is None else hop)
    return near, swap(near, "task", 1)


def trade(stay, cross, hop=None):
    got = first_hop(cross) if hop is None else hop
    return stay, got, swap(second_of(stay, got), "task", 1)


def kernel_call(name, body, grid, ins, in_specs, outs, out_specs, scratch=(), limit=16, flops=0):
    return pl.pallas_call(
        body,
        name=name,
        grid=grid,
        in_specs=in_specs,
        out_specs=out_specs,
        out_shape=[jax.ShapeDtypeStruct(s, d) for s, d in outs],
        scratch_shapes=list(scratch),
        compiler_params=pltpu.CompilerParams(vmem_limit_bytes=limit * 2**20),
        cost_estimate=pl.CostEstimate(
            flops=flops, bytes_accessed=sum(x.size * x.dtype.itemsize for x in ins), transcendentals=0
        ),
    )(*ins)


def views(refs):
    if len(refs) == 2:
        near, far = refs
        return [near.at[0], far.at[0], near.at[1], far.at[1]]
    stay, got, back = refs
    return [stay.at[0], back.at[0], got.at[0], back.at[1]]


def peer(k):
    return lax.axis_index("task") ^ k


def lanes_of(place, width):
    return ds(slice_of(place) * width, width, 128)


def halves(level, size, unit=16):
    bit = (lax.axis_index("task") >> level) % 2
    return ds(bit * size, size, unit), ds((1 - bit) * size, size, unit)


def ds(start, size, unit=16):
    if isinstance(start, int):
        return pl.ds(start, size)
    return pl.ds(pl.multiple_of(start, unit), size)


def dot(a, b):
    return jnp.dot(a, b, preferred_element_type=F32)


def dot_nt(a, b):
    return lax.dot_general(a, b, (((1,), (1,)), ((), ())), preferred_element_type=F32)


def dot_tn(a, b):
    return lax.dot_general(a, b, (((0,), (0,)), ((), ())), preferred_element_type=F32)


def gelu_parts(v):
    square = v * v
    t = jnp.tanh(ROOT * v * (1.0 + CUBE * square))
    return square, t


def gelu(v):
    _, t = gelu_parts(v)
    return 0.5 * v * (1.0 + t)


def gelu_slope(v):
    square, t = gelu_parts(v)
    return 0.5 * (1.0 + t) + (0.5 * ROOT) * v * (1.0 - t * t) * (1.0 + (3.0 * CUBE) * square)


def sigmoid(v):
    return 0.5 * (1.0 + jnp.tanh(0.5 * v))


def scales(first, second, count):
    mean = first / count
    return mean, lax.rsqrt(second / count - mean * mean + EPS)


def fold(v):
    return jnp.sum(v.reshape(-1, 8, v.shape[-1]), axis=0)


def sweep(rows, width, step, sums):
    block = 16

    def body(i, carry):
        values = step(ds(i * block, block))
        return tuple(c + fold(v) for c, v in zip(carry, values, strict=True))

    start = tuple(jnp.zeros((8, width), F32) for _ in range(sums))
    out = lax.fori_loop(0, rows // block, body, start, unroll=3)
    return [jnp.sum(c, axis=0, keepdims=True) for c in out]


def spread(ref, at, width):
    m = ref[at, :]
    return m if width == 128 else jnp.concatenate([m] * (width // 128), axis=1)


def each_block(rows, step):
    def body(i, carry):
        step(ds(i * 16, 16))
        return carry

    lax.fori_loop(0, rows // 16, body, 0, unroll=3)


def accumulate(ref, parts):
    total = jnp.concatenate(parts, axis=0)

    @pl.when(pl.program_id(0) == 0)
    def _():
        ref[...] = total

    @pl.when(pl.program_id(0) != 0)
    def _():
        ref[...] += total


def fill_wide(wide_ref, piece_refs, shape, reverse, change=None, place=peer, width=None):
    image_count, row_count, places, cols = shape
    rows = row_count * cols
    width = width or piece_refs[0].shape[-1]
    span = (row_count * places + 2) * cols
    zero = jnp.zeros((cols, wide_ref.shape[1]), BF)
    column = lax.broadcasted_iota(jnp.int32, (row_count, cols, width), 1).reshape(rows, width)
    for i in range(image_count):
        wide_ref[ds(i * span, cols), :] = zero
        wide_ref[ds((i + 1) * span - cols, cols), :] = zero
        for k, ref in enumerate(piece_refs):
            start = place(k) * rows
            x = ref[i, :, :width]
            if change is not None:
                x = change(x, ds(i * rows * places + start, rows))
            wide = x.astype(F32)
            left = jnp.where(column == 0, 0.0, pltpu.roll(wide, 1, 0)).astype(BF)
            right = jnp.where(column == cols - 1, 0.0, pltpu.roll(wide, rows - 1, 0)).astype(BF)
            if reverse:
                left, right = right, left
            at = ds(i * span + cols + start, rows)
            wide_ref[at, :width] = left
            wide_ref[at, width : 2 * width] = x.astype(BF)
            wide_ref[at, 2 * width :] = right


def turn_taps(turned_ref, kernel_ref, width):
    n = kernel_ref.shape[1]
    for tap in range(9):
        p, q = divmod(tap, 3)
        turned_ref[p, :, q * n : (q + 1) * n] = kernel_ref[tap * width : (tap + 1) * width, :]


def conv_rows(wide_ref, i, c, shape, product, reverse):
    row_count, places, cols = shape[1:]
    rows = row_count * cols
    start = i * (row_count * places + 2) * cols + c * rows
    total = None
    for p in range(3):
        at = (2 - p if reverse else p) * cols
        term = product(p, wide_ref[ds(start + at, rows), :])
        total = term if total is None else total + term
    return total


def add_up(*xs):
    def body(*refs):
        total = refs[0][...]
        for ref in refs[1:-1]:
            total = total + ref[...]
        refs[-1][...] = total

    return kernel_call(
        "add_up", body, (), list(xs), [VMEM] * len(xs), [(xs[0].shape, F32)], [VMEM], limit=2
    )[0]


def side_by_side(pieces):
    rows, width = pieces[0].shape[1:]

    def body(near_ref, far_ref, out_ref):
        for k, ref in enumerate(views((near_ref, far_ref))):
            out_ref[:, k * width : (k + 1) * width] = ref[...]

    return kernel_call(
        "side_by_side", body, (), list(pieces), [VMEM] * 2, [((rows, 4 * width), F32)], [VMEM], limit=2
    )[0]


def stack_two(a, b):
    def body(a_ref, b_ref, out_ref):
        out_ref[0] = a_ref[...]
        out_ref[1] = b_ref[...]

    return kernel_call(
        "stack_two", body, (), [a, b], [VMEM] * 2, [((2,) + a.shape, a.dtype)], [VMEM]
    )[0]


def second_of(a, b):
    def body(a_ref, b_ref, out_ref):
        out_ref[0] = a_ref[1]
        out_ref[1] = b_ref[1]

    return kernel_call("second_of", body, (), [a, b], [VMEM] * 2, [(a.shape, a.dtype)], [VMEM])[0]


def first_sums(stay, got):
    def body(stay_ref, got_ref, own_ref, one_ref):
        own_ref[...] = (stay_ref[0].astype(F32) + got_ref[0].astype(F32)).astype(BF)
        one_ref[...] = (stay_ref[1].astype(F32) + got_ref[1].astype(F32)).astype(BF)

    return kernel_call(
        "first_sums",
        body,
        (),
        [stay, got],
        [VMEM] * 2,
        [(stay.shape[1:], BF)] * 2,
        [VMEM] * 2,
    )


def pack_weights(w_trunk, w_hid, w_attn, w_shared, vectors, part, quarter, copies):
    rows, (depth, width) = w_trunk.shape[0], w_hid.shape[1:]
    tasks = w_hid.shape[0]
    block = w_shared.shape[1]
    cuts = width // block
    n = len(vectors)

    def body(trunk_ref, hid_ref, attn_ref, shared_ref, *refs):
        vector_refs = refs[:n]
        first_ref, second_ref, out_ref = refs[n:]
        me = lax.axis_index("task")
        task = jnp.minimum(me, tasks - 1)
        for k in range(copies):
            first_ref[k] = trunk_ref[:, lanes_of(me, part)]
        for c in range(cuts):
            here = slice(c * block, (c + 1) * block)
            second_ref[c * depth : (c + 1) * depth, :] = hid_ref[task, :, here]
            second_ref[(cuts + c) * depth : (cuts + c + 1) * depth, :] = attn_ref[task, :, here]
        if quarter:
            second_ref[2 * cuts * depth :, :] = shared_ref[ds(me * quarter, quarter), :]
        out_ref[...] = jnp.zeros_like(out_ref)
        for k, ref in enumerate(vector_refs):
            row = ref[...] if ref.shape[0] == 1 else ref[pl.ds(task, 1), :]
            out_ref[k : k + 1, :] = row

    ins = [w_trunk, w_hid, w_attn, w_shared, *vectors]
    return kernel_call(
        "pack_weights",
        body,
        (),
        ins,
        [VMEM] * len(ins),
        [
            ((copies, rows, part), BF),
            ((2 * cuts * depth + quarter, block), BF),
            ((8, width), F32),
        ],
        [VMEM] * 3,
        limit=56,
    )


def unpack_weights(gathered, depth, width, quarter):
    count, _, block = gathered.shape
    cuts = width // block

    def body(gathered_ref, layers_ref, *outs):
        for k in range(count):
            for c in range(2 * cuts):
                layers_ref[k * depth : (k + 1) * depth, c * block : (c + 1) * block] = gathered_ref[
                    k, c * depth : (c + 1) * depth, :
                ]
            if quarter:
                outs[0][k] = gathered_ref[k, 2 * cuts * depth :, :]

    outs = [((count * depth, 2 * width), BF)]
    if quarter:
        outs.append(((count, quarter, block), BF))
    return kernel_call("unpack_weights", body, (), [gathered], [VMEM], outs, [VMEM] * len(outs))


def gathered_sum(parts, dtype):
    shape = parts.shape[1:]

    def body(parts_ref, out_ref):
        total = parts_ref[0].astype(F32)
        for k in range(1, parts.shape[0]):
            total = total + parts_ref[k].astype(F32)
        out_ref[...] = total.astype(dtype)

    return kernel_call("gathered_sum", body, (), [parts], [VMEM], [(shape, dtype)], [VMEM])[0]


def piece_sum(pieces, dtype):
    def body(*refs):
        total = refs[0][...].astype(F32)
        for ref in refs[1:-1]:
            total = total + ref[...].astype(F32)
        refs[-1][...] = total.astype(dtype)

    return kernel_call(
        "piece_sum", body, (), list(pieces), [VMEM] * len(pieces), [(pieces[0].shape, dtype)], [VMEM]
    )[0]


def blocks_of(whole_ref, out_refs, rows):
    me = lax.axis_index("dp")
    if len(out_refs) == 1:
        out_refs[0][...] = whole_ref[...]
    elif len(out_refs) == 2:
        for k in range(whole_ref.shape[0] // rows):
            at = k // 2 * rows
            out_refs[k % 2][at : at + rows, :] = whole_ref[ds((me ^ k) * rows, rows), :]
    else:
        for k, ref in enumerate(out_refs):
            ref[...] = whole_ref[ds((me ^ k) * rows, rows), :]


def block_shapes(rows, width, pairs):
    count = lax.axis_size("dp")
    if not in_blocks(rows):
        return [((count * rows, width), BF)]
    if pairs:
        return [((count // 2 * rows, width), BF)] * 2
    return [((rows, width), BF)] * count


def add_cut(kept, got, count):
    rows, width = kept.shape[0] // count, kept.shape[1]

    def body(kept_ref, got_ref, *out_refs):
        for k, ref in enumerate(out_refs):
            at = slice(k * rows, (k + 1) * rows)
            ref[...] = (kept_ref[at, :].astype(F32) + got_ref[at, :].astype(F32)).astype(BF)

    return kernel_call(
        "add_cut", body, (), [kept, got], [VMEM] * 2, [((rows, width), BF)] * count, [VMEM] * count
    )


def sum_in_blocks(kept, got):
    rows, width = kept.shape[0] // lax.axis_size("dp"), kept.shape[1]
    outs = block_shapes(rows, width, True)

    def body(kept_ref, got_ref, *refs):
        refs[-1][...] = (kept_ref[...].astype(F32) + got_ref[...].astype(F32)).astype(BF)
        blocks_of(refs[-1], refs[:-1], rows)

    return kernel_call(
        "sum_in_blocks",
        body,
        (),
        [kept, got],
        [VMEM] * 2,
        outs,
        [VMEM] * len(outs),
        [pltpu.VMEM(kept.shape, BF)],
    )


def lanes_below(x, width):
    return [x[:, c * width : (c + 1) * width] for c in range(x.shape[1] // width)]


def merge_parts(shared_kept, shared_got, pairs):
    count = lax.axis_size("dp")
    each, width = shared_kept.shape[0] // count, shared_kept.shape[1]
    mid = pairs[0][0].shape[1]
    rows, cuts = mid // count, mid // width
    total = each + len(pairs) * cuts * rows
    n = 2 * len(pairs)

    def body(kept_ref, got_ref, *refs):
        sum_ref, product_ref = refs[-2:]
        out_refs = refs[n : n + 2]
        me = lax.axis_index("dp")
        sum_ref[...] = (kept_ref[...].astype(F32) + got_ref[...].astype(F32)).astype(BF)
        for k in range(count):
            at = k // 2 * total
            out_refs[k % 2][at : at + each, :] = sum_ref[ds((me ^ k) * each, each), :]
        for p in range(len(pairs)):
            product_ref[...] = dot_tn(refs[2 * p][...], refs[2 * p + 1][...]).astype(BF)
            for k in range(count):
                block = product_ref[ds((me ^ k) * rows, rows), :]
                for c in range(cuts):
                    at = k // 2 * total + each + (p * cuts + c) * rows
                    out_refs[k % 2][at : at + rows, :] = block[:, c * width : (c + 1) * width]

    ins = [shared_kept, shared_got, *(x for pair in pairs for x in pair)]
    return kernel_call(
        "merge_parts",
        body,
        (),
        ins,
        [VMEM] * len(ins),
        [((count // 2 * total, width), BF)] * 2,
        [VMEM] * 2,
        [pltpu.VMEM(shared_kept.shape, BF), pltpu.VMEM((mid, mid), BF)],
        flops=2 * pairs[0][0].size * mid * len(pairs),
    )


def split_parts(pieces, shared_rows, layer_shape, tasks):
    rows, columns = layer_shape
    width = pieces[0].shape[2]

    def body(near_ref, far_ref, shared_ref, *layer_refs):
        for k, ref in enumerate(views((near_ref, far_ref))):
            place = peer(k)
            lanes = ds(place % 2 * width, width, 128)
            at = ds(place // 2 * shared_rows, shared_rows)
            shared_ref[at, lanes] = ref[:shared_rows, :].astype(F32)

            @pl.when(place < tasks)
            def _(ref=ref, place=place):
                start = shared_rows
                for layer_ref in layer_refs:
                    for c in range(columns // width):
                        value = ref[start : start + rows, :].astype(F32)
                        layer_ref[place, :, c * width : (c + 1) * width] = value
                        start += rows

    return kernel_call(
        "split_parts",
        body,
        (),
        list(pieces),
        [VMEM] * 2,
        [((shared_rows * 2, 2 * width), F32)] + [((tasks, rows, columns), F32)] * 2,
        [VMEM] * 3,
    )


def own_rows(x, image_count, places):
    rows, width = x.shape[0] // image_count // places, x.shape[1]

    def body(x_ref, out_ref):
        for i in range(image_count):
            out_ref[i] = x_ref[ds((i * places + peer(0)) * rows, rows), :]

    return kernel_call(
        "own_rows", body, (), [x], [VMEM], [((image_count, rows, width), x.dtype)], [VMEM]
    )[0]


def by_task(pieces, tasks, dtype):
    shape = pieces[0].shape[1:]
    n = len(pieces)

    def body(*refs):
        for k, ref in enumerate(views(refs[:n])):
            place = peer(k)

            @pl.when(place < tasks)
            def _(ref=ref, place=place):
                refs[n][place] = ref[...].astype(dtype)

    return kernel_call(
        "by_task", body, (), list(pieces), [VMEM] * n, [((tasks,) + shape, dtype)], [VMEM]
    )[0]


def lay_slices(pieces, dtype):
    rows, width = pieces[0].shape[1:]

    def body(near_ref, far_ref, out_ref):
        for k, ref in enumerate(views((near_ref, far_ref))):
            out_ref[:, lanes_of(peer(k), width)] = ref[...].astype(dtype)

    return kernel_call(
        "lay_slices", body, (), list(pieces), [VMEM] * 2, [((rows, 4 * width), dtype)], [VMEM]
    )[0]


def join_sums(gate_sums, hid_sums, trunk_sums):
    width, part = gate_sums.shape[1], trunk_sums.shape[1]

    def body(gate_ref, hid_ref, trunk_ref, out_ref):
        out_ref[0:2, :] = gate_ref[...]
        out_ref[2:4, :] = hid_ref[...]
        out_ref[4:8, :] = jnp.zeros((4, width), F32)
        out_ref[4:6, :part] = trunk_ref[...]

    return kernel_call(
        "join_sums",
        body,
        (),
        [gate_sums, hid_sums, trunk_sums],
        [VMEM] * 3,
        [((8, width), F32)],
        [VMEM],
    )[0]


def split_sums(pieces, tasks, part):
    width = pieces[0].shape[2]

    def body(*refs):
        outs, trunk_ref = refs[2:6], refs[6]
        for k, piece in enumerate(views(refs[:2])):
            place = peer(k)
            trunk_ref[:, lanes_of(place, part)] = piece[4:6, :part]

            @pl.when(place < tasks)
            def _(piece=piece, place=place):
                for c, ref in enumerate(outs):
                    ref[pl.ds(place, 1), :] = piece[c : c + 1, :]

    return kernel_call(
        "split_sums",
        body,
        (),
        list(pieces),
        [VMEM] * 2,
        [((tasks, width), F32)] * 4 + [((2, part * 4), F32)],
        [VMEM] * 5,
    )


def lay_out(order, pieces, dtype, along, count=None):
    n = len(pieces)
    shape = list(pieces[0].shape)
    if along == 0 and shape[0] % 16:
        out = jnp.zeros([shape[0] * n] + shape[1:], dtype)
        for k, piece in enumerate(pieces):
            out = lax.dynamic_update_slice_in_dim(out, piece.astype(dtype), order(k) * shape[0], axis=0)
        return out
    if along is None:
        whole = [count or n] + shape
    else:
        whole = list(shape)
        whole[along] *= n

    def body(*refs):
        for k in range(n):
            value = refs[k][...].astype(dtype)
            if along is None:

                @pl.when(order(k) < whole[0])
                def _(k=k, value=value):
                    refs[-1][order(k)] = value

            elif along == 0:
                refs[-1][ds(order(k) * shape[0], shape[0]), :] = value
            else:
                refs[-1][:, ds(order(k) * shape[1], shape[1], 128)] = value

    return kernel_call(
        "lay_out", body, (), list(pieces), [VMEM] * n, [(tuple(whole), dtype)], [VMEM]
    )[0]


def pack_cots(task_cot, trunk_cot, places):
    tasks, image_count, rows, out_width = task_cot.shape
    part = trunk_cot.shape[-1] // places

    def body(task_ref, trunk_ref, stay_ref, cross_ref):
        for k in range(places):
            ref = (stay_ref, cross_ref)[k // 2].at[k % 2]
            ref[:, :, :out_width] = task_ref[jnp.minimum(peer(k), tasks - 1)]
            ref[:, :, out_width:] = trunk_ref[:, :, lanes_of(peer(k), part)]

    return kernel_call(
        "pack_cots",
        body,
        (),
        [task_cot, trunk_cot],
        [VMEM, VMEM],
        [((2, image_count, rows, out_width + part), BF)] * 2,
        [VMEM] * 2,
    )


def trunk_forward(labelled, counts, images, shards, shape):
    image_count, row_count, places, cols = shape
    rows = row_count * cols
    count, each, part = shards.shape
    depth = count * each
    pixels = image_count * places * rows
    in_width = images.shape[-1]

    def body(mask_ref, counts_ref, images_ref, shards_ref, centred_ref, stats_ref, kernel_ref, wide_ref, pre_ref):
        for k in range(count):
            kernel_ref[k * each : (k + 1) * each, :] = shards_ref[k]
        pieces = [images_ref.at[:, k] for k in range(places)]
        fill_wide(wide_ref, pieces, shape, False, place=lambda k: k)
        block = 3 * in_width

        def chunk(c, carry):
            for i in range(image_count):
                value = conv_rows(
                    wide_ref,
                    i,
                    c,
                    shape,
                    lambda p, x: dot(x, kernel_ref[p * block : (p + 1) * block, :]),
                    False,
                )
                pre_ref[ds((i * places + c) * rows, rows), :] = value
            return carry

        lax.fori_loop(0, places, chunk, 0)

        def moments(at):
            v = pre_ref[at, :]
            mv = mask_ref[at, :] * v
            return mv, mv * v, v

        sums = sweep(pixels, part, moments, 3)
        mean = sums[2] / pixels
        stats_ref[...] = jnp.concatenate(sums[:2] + [counts_ref[...]] + [mean] * 4, axis=0)

        def centre(at):
            centred_ref[at, :] = (pre_ref[at, :] - mean).astype(BF)

        each_block(pixels, centre)

    return kernel_call(
        "trunk_forward",
        body,
        (),
        [labelled, counts, images, shards],
        [VMEM] * 4,
        [((pixels, part), BF), ((8, part), F32)],
        [VMEM] * 2,
        [
            pltpu.VMEM((depth, part), BF),
            pltpu.VMEM((image_count * (row_count * places + 2) * cols, 3 * in_width), BF),
            pltpu.VMEM((pixels, part), F32),
        ],
        flops=2 * pixels * depth * part,
    )


def rows_spec(rows, width):
    return pl.BlockSpec((rows, width), lambda i: (i, 0))


def fixed_spec(shape):
    return pl.BlockSpec(shape, lambda i: (0,) * len(shape))


def centre_on_first(value_ref, centre_ref, centred_ref):
    @pl.when(pl.program_id(0) == 0)
    def _():
        rows = value_ref.shape[0]
        (total,) = sweep(rows, value_ref.shape[1], lambda at: (value_ref[at, :],), 1)
        centre_ref[...] = total / rows

    centre = centre_ref[...]

    def step(at):
        centred_ref[at, :] = (value_ref[at, :] - centre).astype(BF)

    each_block(value_ref.shape[0], step)


def feat_hid(scaled, stats, totals, vectors, mask, kernel, rows):
    pixels, part = scaled[0].shape[1:]
    n = 2 * len(scaled)
    mid = part * n
    out_mid = mid

    def body(*refs):
        scaled_refs = views(refs[:2])
        stats_ref, totals_ref, vectors_ref, mask_ref, kernel_ref = refs[2:7]
        feat_ref, centred_ref, centre_ref, sums_ref, affine_ref, hid_ref = refs[7:]

        @pl.when(pl.program_id(0) == 0)
        def _():
            count = jnp.maximum(totals_ref[2:3, :], 1.0)
            mean, rstd = scales(totals_ref[0:1, :], totals_ref[1:2, :], count)
            for k in range(n):
                here = slice(k * part, (k + 1) * part)
                at = lanes_of(peer(k), part)
                slope = rstd[:, here] * vectors_ref[TRUNK_GAIN, at]
                affine_ref[0:1, here] = slope
                affine_ref[1:2, here] = (stats_ref[4:5, here] - mean[:, here]) * slope + vectors_ref[TRUNK_BIAS, at]

        def activate(at):
            for k in range(n):
                here = slice(k * part, (k + 1) * part)
                v = scaled_refs[k][at, :].astype(F32) * affine_ref[0:1, here] + affine_ref[1:2, here]
                feat_ref[at, lanes_of(peer(k), part)] = gelu(v).astype(BF)

        each_block(rows, activate)
        hid_ref[...] = dot(feat_ref[...], kernel_ref[...])

        def moments(at):
            v = hid_ref[at, :]
            mv = spread(mask_ref, at, out_mid) * v
            return mv, mv * v

        accumulate(sums_ref, sweep(rows, out_mid, moments, 2))
        centre_on_first(hid_ref, centre_ref, centred_ref)

    return kernel_call(
        "feat_hid",
        body,
        (pixels // rows,),
        [*scaled, stats, totals, vectors, mask, kernel],
        [pl.BlockSpec((2, rows, part), lambda i: (0, i, 0))] * 2
        + [fixed_spec(x.shape) for x in (stats, totals, vectors)]
        + [rows_spec(rows, 128), pl.BlockSpec((mid, out_mid), lambda i: (0, 0))],
        [
            ((pixels, mid), BF),
            ((pixels, out_mid), BF),
            ((1, out_mid), F32),
            ((2, out_mid), F32),
        ],
        [
            rows_spec(rows, mid),
            rows_spec(rows, out_mid),
            fixed_spec((1, out_mid)),
            fixed_spec((2, out_mid)),
        ],
        [pltpu.VMEM((2, mid), F32), pltpu.VMEM((rows, out_mid), F32)],
        flops=2 * pixels * mid * out_mid,
    )


def task_count(totals_ref):
    chosen = jnp.where(lax.axis_index("task") == 0, totals_ref[2:3, 0:1], totals_ref[3:4, 0:1])
    return jnp.maximum(chosen, 1.0)


def normed_rows(sums, count, centre):
    mean, rstd = scales(sums[0:1, :], sums[1:2, :], count)
    return rstd, (centre - mean) * rstd


def hid_gate(hid, centre, sums, totals, vectors, mask, kernel, rows):
    pixels, mid = hid.shape

    def body(*refs):
        hid_ref, middle_ref, sums_ref, totals_ref, vectors_ref, mask_ref, kernel_ref = refs[:7]
        hidden_ref, centred_ref, centre_ref, out_ref, gate_ref = refs[7:]
        count = task_count(totals_ref)
        gain, bias = vectors_ref[HID_GAIN, :], vectors_ref[HID_BIAS, :]
        scale, shift = normed_rows(sums_ref[...], count, middle_ref[...])
        scale, shift = scale * gain, shift * gain + bias

        def activate(at):
            hidden_ref[at, :] = gelu(hid_ref[at, :].astype(F32) * scale + shift).astype(BF)

        each_block(rows, activate)
        gate_ref[...] = dot(hidden_ref[...], kernel_ref[...])

        def moments(at):
            v = gate_ref[at, :]
            mv = spread(mask_ref, at, mid) * v
            return mv, mv * v

        accumulate(out_ref, sweep(rows, mid, moments, 2))
        centre_on_first(gate_ref, centre_ref, centred_ref)

    wide = rows_spec(rows, mid)
    return kernel_call(
        "hid_gate",
        body,
        (pixels // rows,),
        [hid, centre, sums, totals, vectors, mask, kernel],
        [wide]
        + [fixed_spec(x.shape) for x in (centre, sums, totals, vectors)]
        + [rows_spec(rows, 128), pl.BlockSpec((mid, mid), lambda i: (0, 1))],
        [((pixels, mid), BF), ((pixels, mid), BF), ((1, mid), F32), ((2, mid), F32)],
        [wide, wide, fixed_spec((1, mid)), fixed_spec((2, mid))],
        [pltpu.VMEM((rows, mid), F32)],
        flops=2 * pixels * mid * mid,
    )


def feature_back(cot, mask, kernels, shape, out_width):
    image_count, row_count, places, cols = shape
    rows = row_count * cols
    mid = sum(x.size for x in kernels) // out_width // 9
    pixels = image_count * places * rows
    n, m = len(cot), len(kernels)
    count = 2 * m if m > 1 else 1

    def body(*refs):
        cot_refs = views(refs[:n])
        mask_ref = refs[n]
        quarter_refs = refs[1 + n : 1 + n + m]
        if m > 1:
            quarter_refs = views(quarter_refs)
        out_ref, kernel_ref, wide_ref, turned_ref = refs[1 + n + m :]
        blocks, quarter = quarter_refs[0].shape[:2]
        for k, ref in enumerate(quarter_refs):
            for j in range(blocks):
                kernel_ref[ds((j * count + (peer(k) if m > 1 else 0)) * quarter, quarter), :] = ref[j]
        turn_taps(turned_ref, kernel_ref, mid)
        fill_wide(
            wide_ref,
            cot_refs,
            shape,
            True,
            lambda x, at: x.astype(F32) * spread(mask_ref, at, out_width),
            width=out_width,
        )

        def chunk(c, carry):
            for i in range(image_count):
                value = conv_rows(
                    wide_ref, i, c, shape, lambda p, x: dot_nt(x, turned_ref[p]), True
                )
                out_ref[ds((i * places + c) * rows, rows), :] = value.astype(BF)
            return carry

        lax.fori_loop(0, places, chunk, 0)

    return kernel_call(
        "feature_back",
        body,
        (),
        [*cot, mask, *kernels],
        [VMEM] * (n + 1 + m),
        [((pixels, mid), BF), ((9 * mid, out_width), BF)],
        [VMEM] * 2,
        [
            pltpu.VMEM((image_count * (row_count * places + 2) * cols, 3 * out_width), BF),
            pltpu.VMEM((3, mid, 3 * out_width), BF),
        ],
        limit=24,
        flops=2 * pixels * 9 * mid * out_width,
    )


def gate_back(gate, centre, sums, totals, vectors, feature_grad, feat, rows):
    pixels, mid = gate.shape

    def body(gate_ref, centre_ref, sums_ref, totals_ref, vectors_ref, grad_ref, feat_ref, *outs):
        features_ref, gate_grad_ref, share_ref, out_ref = outs
        scale, shift = normed_rows(sums_ref[...], task_count(totals_ref), centre_ref[...])
        slope = 0.5 * vectors_ref[ATTN_GAIN, :]
        offset = 0.5 * vectors_ref[ATTN_BIAS, :]

        def step(at):
            normed = gate_ref[at, :].astype(F32) * scale + shift
            t = jnp.tanh(normed * slope + offset)
            attention = 0.5 + 0.5 * t
            features = attention * feat_ref[at, :].astype(F32)
            features_ref[at, :] = features.astype(BF)
            grad = grad_ref[at, :].astype(F32)
            share_ref[at, :] = (grad * attention).astype(BF)
            gate_grad = grad * features * (0.5 - 0.5 * t)
            gate_grad_ref[at, :] = gate_grad.astype(BF)
            return gate_grad, gate_grad * normed

        accumulate(out_ref, sweep(rows, mid, step, 2))

    wide = rows_spec(rows, mid)
    return kernel_call(
        "gate_back",
        body,
        (pixels // rows,),
        [gate, centre, sums, totals, vectors, feature_grad, feat],
        [wide] + [fixed_spec(x.shape) for x in (centre, sums, totals, vectors)] + [wide, wide],
        [((pixels, mid), BF)] * 3 + [((2, mid), F32)],
        [wide] * 3 + [fixed_spec((2, mid))],
    )


def back_rows(gain, sums, count, centre, back):
    rstd, shift = normed_rows(sums, count, centre)
    scale = gain * rstd
    tilt = scale * back[1:2, :] / count
    return scale, scale * back[0:1, :] / count + tilt * shift, tilt * rstd


def hid_back(grad, gate, mask, centre, sums, totals, vectors, back, hid, h_centre, h_sums, kernel, rows):
    pixels, mid = grad.shape

    def body(*refs):
        grad_ref, gate_ref, mask_ref, centre_ref, sums_ref, totals_ref, vectors_ref, back_ref = refs[:8]
        hid_ref, h_centre_ref, h_sums_ref, kernel_ref = refs[8:12]
        pre_ref, act_ref, out_ref, value_ref = refs[12:]
        count = task_count(totals_ref)
        h_gain, h_bias = vectors_ref[HID_GAIN, :], vectors_ref[HID_BIAS, :]
        scale, lean, tilt = back_rows(
            vectors_ref[ATTN_GAIN, :], sums_ref[...], count, centre_ref[...], back_ref[...]
        )

        def step(at):
            lost = spread(mask_ref, at, mid) * (lean + gate_ref[at, :].astype(F32) * tilt)
            pre_ref[at, :] = (grad_ref[at, :].astype(F32) * scale - lost).astype(BF)

        each_block(rows, step)
        value_ref[...] = dot_nt(pre_ref[...], kernel_ref[...])
        h_scale, h_shift = normed_rows(h_sums_ref[...], count, h_centre_ref[...])

        def slope(at):
            x = hid_ref[at, :].astype(F32) * h_scale + h_shift
            value = value_ref[at, :] * gelu_slope(x * h_gain + h_bias)
            act_ref[at, :] = value.astype(BF)
            return value, value * x

        accumulate(out_ref, sweep(rows, mid, slope, 2))

    wide = rows_spec(rows, mid)
    return kernel_call(
        "hid_back",
        body,
        (pixels // rows,),
        [grad, gate, mask, centre, sums, totals, vectors, back, hid, h_centre, h_sums, kernel],
        [wide, wide, rows_spec(rows, 128)]
        + [fixed_spec(x.shape) for x in (centre, sums, totals, vectors, back)]
        + [wide]
        + [fixed_spec(x.shape) for x in (h_centre, h_sums)]
        + [pl.BlockSpec((mid, mid), lambda i: (0, 1))],
        [((pixels, mid), BF), ((pixels, mid), BF), ((2, mid), F32)],
        [wide, wide, fixed_spec((2, mid))],
        [pltpu.VMEM((rows, mid), F32)],
        flops=2 * pixels * mid * mid,
    )


def feat_back(act_grad, hid, mask, centre, sums, totals, vectors, back, share, kernel, rows, tasks):
    pixels, mid = act_grad.shape
    half = mid // 2

    def body(*refs):
        act_ref, hid_ref, mask_ref, centre_ref, sums_ref, totals_ref = refs[:6]
        vectors_ref, back_ref, share_ref, kernel_ref, pre_ref, kept_ref, sent_ref, part_ref = refs[6:]
        active = jnp.where(lax.axis_index("task") < tasks, 1.0, 0.0)
        scale, lean, tilt = back_rows(
            vectors_ref[HID_GAIN, :],
            sums_ref[...],
            task_count(totals_ref),
            centre_ref[...],
            back_ref[...],
        )

        def step(at):
            lost = spread(mask_ref, at, mid) * (lean + hid_ref[at, :].astype(F32) * tilt)
            pre_ref[at, :] = (act_ref[at, :].astype(F32) * scale - lost).astype(BF)

        each_block(rows, step)
        part_ref[...] = dot_nt(pre_ref[...], kernel_ref[...])

        def add(at):
            for ref, here in zip((kept_ref, sent_ref), halves(0, half, 128), strict=True):
                value = part_ref[at, here] + share_ref[at, here].astype(F32)
                ref[at, :] = (value * active).astype(BF)

        each_block(rows, add)

    wide = rows_spec(rows, mid)
    return kernel_call(
        "feat_back",
        body,
        (pixels // rows,),
        [act_grad, hid, mask, centre, sums, totals, vectors, back, share, kernel],
        [wide, wide, rows_spec(rows, 128)]
        + [fixed_spec(x.shape) for x in (centre, sums, totals, vectors, back)]
        + [wide]
        + [pl.BlockSpec((mid, mid), lambda i: (0, 0))],
        [((pixels, mid), BF), ((pixels, half), BF), ((pixels, half), BF)],
        [wide, rows_spec(rows, half), rows_spec(rows, half)],
        [pltpu.VMEM((rows, mid), F32)],
        flops=2 * pixels * mid * mid,
    )


def add_halve(level, kept, got, rows):
    pixels, width = kept.shape
    half = width // 2

    def body(kept_ref, got_ref, a_ref, b_ref):
        for ref, here in zip((a_ref, b_ref), halves(level, half, 128), strict=True):
            ref[...] = (kept_ref[:, here].astype(F32) + got_ref[:, here].astype(F32)).astype(BF)

    wide, slim = rows_spec(rows, width), rows_spec(rows, half)
    return kernel_call(
        "add_halve",
        body,
        (pixels // rows,),
        [kept, got],
        [wide, wide],
        [((pixels, half), BF)] * 2,
        [slim, slim],
    )


def trunk_back(parts, cots, trunk, stats, totals, vectors, shape):
    image_count, row_count, places, cols = shape
    rows = row_count * cols
    pixels, width = trunk.shape
    first = cots[0].shape[-1] - width
    n, m = len(parts), len(cots)

    def body(*refs):
        part_refs = refs[:n]
        cot_refs = views(refs[n : n + m])
        trunk_ref, stats_ref, totals_ref, vectors_ref, grad_ref, out_ref = refs[n + m :]
        lanes = lanes_of(peer(0), width)
        gain, bias = vectors_ref[TRUNK_GAIN, lanes], vectors_ref[TRUNK_BIAS, lanes]
        totals = totals_ref[:, :width]
        count = jnp.maximum(totals[2:3, :], 1.0)
        scale, shift = normed_rows(totals, count, stats_ref[4:5, :])
        total = [0.0, 0.0]
        for i in range(image_count):
            for k, cot_ref in enumerate(cot_refs):
                start = (i * places + peer(k)) * rows

                def step(at, start=start, cot_ref=cot_ref, i=i):
                    here = ds(start + at.start, at.size)
                    x = trunk_ref[here, :].astype(F32) * scale + shift
                    grad = cot_ref[i, at, first:].astype(F32)
                    for ref in part_refs:
                        grad = grad + ref[here, :].astype(F32)
                    grad = grad * gelu_slope(x * gain + bias)
                    grad_ref[here, :] = grad.astype(BF)
                    return grad, grad * x

                found = sweep(rows, width, step, 2)
                total = [a + b for a, b in zip(total, found, strict=True)]
        out_ref[...] = jnp.concatenate(total, axis=0)

    return kernel_call(
        "trunk_back",
        body,
        (),
        [*parts, *cots, trunk, stats, totals, vectors],
        [VMEM] * (n + m + 4),
        [((pixels, width), BF), ((2, width), F32)],
        [VMEM] * 2,
    )


def trunk_weights(images, grad, trunk, mask, stats, totals, vectors, back, shape):
    image_count, row_count, places, cols = shape
    rows = row_count * cols
    in_width = images.shape[-1]
    pixels, part = grad.shape
    depth = 9 * in_width // lax.axis_size("dp")
    outs = block_shapes(depth, part, True)
    span = (row_count * places + 2) * cols
    whole = row_count * places * cols

    def body(*refs):
        images_ref, grad_ref, trunk_ref, mask_ref, stats_ref, totals_ref, vectors_ref, back_ref = refs[:8]
        out_ref = refs[8]
        weight_ref, wide_ref = refs[-2:]
        totals = totals_ref[:, :part]
        count = jnp.maximum(totals[2:3, :], 1.0)
        scale, lean, tilt = back_rows(
            vectors_ref[TRUNK_GAIN, lanes_of(peer(0), part)], totals, count, stats_ref[4:5, :], back_ref[...]
        )

        def step(at):
            lost = mask_ref[at, :] * (lean + trunk_ref[at, :].astype(F32) * tilt)
            out_ref[at, :] = (grad_ref[at, :].astype(F32) * scale - lost).astype(BF)

        each_block(pixels, step)
        fill_wide(
            wide_ref,
            [images_ref.at[:, k] for k in range(places)],
            shape,
            False,
            place=lambda k: k,
        )
        for p in range(3):
            total = None
            for i in range(image_count):
                term = dot_tn(
                    wide_ref[ds(i * span + p * cols, whole), :], out_ref[ds(i * whole, whole), :]
                )
                total = term if total is None else total + term
            weight_ref[p * 3 * in_width : (p + 1) * 3 * in_width, :] = total.astype(BF)
        blocks_of(weight_ref, refs[9:-2], depth)

    return kernel_call(
        "trunk_weights",
        body,
        (),
        [images, grad, trunk, mask, stats, totals, vectors, back],
        [VMEM] * 8,
        [((pixels, part), BF), *outs],
        [VMEM] * (1 + len(outs)),
        [
            pltpu.VMEM((9 * in_width, part), BF),
            pltpu.VMEM((image_count * span, 3 * in_width), BF),
        ],
        flops=2 * pixels * 9 * in_width * part,
    )


def image_back(grad, shards, shape):
    image_count, row_count, places, cols = shape
    rows = row_count * cols
    part = grad.shape[-1]
    count, each = shards.shape[:2]
    in_width = count * each // 9

    def body(grad_ref, shards_ref, *refs):
        out_refs = [refs[k // 2].at[k % 2] for k in range(places)]
        kernel_ref, wide_ref, turned_ref = refs[2:]
        for k in range(count):
            kernel_ref[k * each : (k + 1) * each, :] = shards_ref[k]
        turn_taps(turned_ref, kernel_ref, in_width)
        pieces = [grad_ref.at[:, k] for k in range(places)]
        fill_wide(wide_ref, pieces, shape, True, place=lambda k: k)
        for k, ref in enumerate(out_refs):
            for i in range(image_count):
                value = conv_rows(
                    wide_ref, i, peer(k), shape, lambda p, x: dot_nt(x, turned_ref[p]), True
                )
                ref[i] = value.astype(BF)

    return kernel_call(
        "image_back",
        body,
        (),
        [grad.reshape(image_count, places, rows, part), shards],
        [VMEM, VMEM],
        [((2, image_count, rows, in_width), BF)] * 2,
        [VMEM] * 2,
        [
            pltpu.VMEM((count * each, part), BF),
            pltpu.VMEM((image_count * (row_count * places + 2) * cols, 3 * part), BF),
            pltpu.VMEM((3, in_width, 3 * part), BF),
        ],
        flops=2 * grad.size * 9 * in_width,
    )


def task_forward(features, kernel, shape):
    image_count, row_count, places, cols = shape
    rows = row_count * cols
    mid = features.shape[-1]
    out_width = kernel.shape[1]
    block = 3 * mid

    def body(features_ref, kernel_ref, *refs):
        out_refs = [refs[k // 2].at[k % 2] for k in range(places)]
        (wide_ref,) = refs[2:]
        pieces = [features_ref.at[:, k] for k in range(places)]
        fill_wide(wide_ref, pieces, shape, False, place=lambda k: k)
        for k, ref in enumerate(out_refs):
            for i in range(image_count):
                value = conv_rows(
                    wide_ref,
                    i,
                    peer(k),
                    shape,
                    lambda p, x: dot(x, kernel_ref[p * block : (p + 1) * block, :]),
                    False,
                )
                ref[i] = value.astype(BF)

    return kernel_call(
        "task_forward",
        body,
        (),
        [features.reshape(image_count, places, rows, mid), kernel],
        [VMEM, VMEM],
        [((2, image_count, rows, out_width), BF)] * 2,
        [VMEM] * 2,
        [
            pltpu.VMEM((image_count * (row_count * places + 2) * cols, 3 * mid), BF),
        ],
        limit=24,
        flops=2 * features.size * 9 * out_width,
    )


def add_split(level, kept, got, blocks):
    rows, width = kept.shape
    half = rows // blocks // 2

    def body(kept_ref, got_ref, a_ref, b_ref):
        bit = (lax.axis_index("task") >> level) % 2
        for ref, which in ((a_ref, bit), (b_ref, 1 - bit)):
            for j in range(blocks):
                at = ds((2 * j + which) * half, half)
                value = kept_ref[at, :].astype(F32) + got_ref[at, :].astype(F32)
                ref[j] = value.astype(BF)

    return kernel_call(
        "add_split",
        body,
        (),
        [kept, got],
        [VMEM, VMEM],
        [((blocks, half, width), BF)] * 2,
        [VMEM] * 2,
    )


def layer_weights(pairs):
    mid = pairs[0][0].shape[1]
    rows = mid // lax.axis_size("dp")
    outs = block_shapes(rows, mid * len(pairs), True)
    n = 2 * len(pairs)

    def body(*refs):
        for k in range(len(pairs)):
            value = dot_tn(refs[2 * k][...], refs[2 * k + 1][...])
            refs[-1][:, k * mid : (k + 1) * mid] = value.astype(BF)
        blocks_of(refs[-1], refs[n:-1], rows)

    ins = [x for pair in pairs for x in pair]
    return kernel_call(
        "layer_weights",
        body,
        (),
        ins,
        [VMEM] * n,
        outs,
        [VMEM] * len(outs),
        [pltpu.VMEM((mid, mid * len(pairs)), BF)],
        flops=2 * pairs[0][0].size * mid * len(pairs),
    )


def shared_weights(cot, mask, features, shape, tasks, out_width):
    image_count, row_count, places, cols = shape
    rows = row_count * cols
    mid = features.shape[-1]
    n = len(cot)
    half = out_width // 2
    span = (row_count * places + 2) * cols
    whole = row_count * places * cols

    def body(*refs):
        cot_refs = views(refs[:n])
        mask_ref, features_ref, kept_ref, sent_ref, wide_ref, part_ref = refs[n:]
        active = jnp.where(lax.axis_index("task") < tasks, 1.0, 0.0)
        fill_wide(
            wide_ref,
            cot_refs,
            shape,
            True,
            lambda x, at: x.astype(F32) * spread(mask_ref, at, out_width) * active,
            width=out_width,
        )
        for tap in range(9):
            p, q = divmod(tap, 3)
            total = None
            for i in range(image_count):
                term = dot_tn(
                    features_ref[ds(i * whole, whole), :],
                    wide_ref[
                        ds(i * span + (2 - p) * cols, whole), q * out_width : (q + 1) * out_width
                    ],
                )
                total = term if total is None else total + term
            part_ref[...] = total
            for ref, here in zip((kept_ref, sent_ref), halves(0, half, 128), strict=True):
                ref[tap * mid : (tap + 1) * mid, :] = part_ref[:, here].astype(BF)

    return kernel_call(
        "shared_weights",
        body,
        (),
        [*cot, mask, features],
        [VMEM] * (n + 2),
        [((9 * mid, half), BF)] * 2,
        [VMEM, VMEM],
        [
            pltpu.VMEM((image_count * span, 3 * out_width), BF),
            pltpu.VMEM((mid, out_width), F32),
        ],
        flops=2 * features.size * 9 * out_width,
    )


def shards(
    images,
    w_trunk,
    trunk_gain,
    trunk_bias,
    w_hid,
    hid_gain,
    hid_bias,
    w_attn,
    attn_gain,
    attn_bias,
    w_shared,
    labels,
    depth_valid,
    trunk_cot,
    task_cot,
):
    image_count, row_count, cols, in_width = images.shape
    mid = w_trunk.shape[1]
    out_width = w_shared.shape[1]
    tasks, depth, width = w_hid.shape
    places = lax.axis_size("task")
    assert tasks <= places == 4
    part = mid // places
    me = lax.axis_index("task")
    rows = row_count * cols
    pixels = image_count * places * rows
    shape = (image_count, row_count, places, cols)
    blocks = lax.axis_size("dp")

    quarter = w_shared.shape[0] // places
    staged = quarter % 16 == 0 and in_blocks(w_trunk.shape[0]) and blocks >= 4
    vectors = [trunk_gain[None], trunk_bias[None], hid_gain, hid_bias, attn_gain, attn_bias]
    first, second, vectors = pack_weights(
        w_trunk, w_hid, w_attn, w_shared, vectors, part, quarter * staged, blocks
    )
    trunk_shards = lax.all_to_all(first, "dp", 0, 0, tiled=True)
    gathered = lax.all_gather(second, "dp", axis=0, tiled=False)
    marks = jnp.stack([(labels >= 0).astype(F32), depth_valid.astype(F32)])
    marks = lax.all_gather(marks, "task", axis=2, tiled=True).reshape(2, pixels)
    marks, images = together(marks, images)
    all_images = lax.all_gather(
        images.reshape(image_count, rows, in_width), "task", axis=1, tiled=False
    )
    counts = jnp.broadcast_to(jnp.sum(marks, 1)[:, None], (2, part))
    labelled = jnp.broadcast_to(marks[0][:, None], (pixels, 128))
    mask = jnp.where(me == 0, labelled, jnp.broadcast_to(marks[1][:, None], (pixels, 128)))
    trunk_shards, all_images, labelled, mask, counts = together(
        trunk_shards, all_images, labelled, mask, counts
    )

    trunk, own_stats = trunk_forward(labelled, counts, all_images, trunk_shards, shape)
    hop, trunk = together(first_hop(own_stats), trunk)
    stats = side_by_side(relay(own_stats, hop))
    totals, (trunk, hop) = sum_dp(stats, lambda: (trunk, first_hop(trunk)))
    scaled = relay(trunk, hop)
    totals, gathered, trunk_cot, task_cot = together(totals, gathered, trunk_cot, task_cot)
    layers, *quarters = unpack_weights(gathered, depth, width, quarter * staged)
    if staged:
        hop = first_hop(quarters[0])
    stay, cross = pack_cots(
        task_cot.reshape(tasks, image_count, rows, out_width),
        trunk_cot.reshape(image_count, rows, mid),
        places,
    )
    cot_hop = first_hop(cross)
    feat, hid, hid_centre, sums = feat_hid(scaled, stats, totals, vectors, mask, layers, rows)
    if staged:
        hid_totals, hop = sum_dp(sums, lambda: hop)
        quarters = relay(quarters[0], hop)
    else:
        hid_totals = sum_dp(sums)
        quarters = [lax.all_gather(w_shared, "dp", axis=0, tiled=True)[None]]
    hidden, gate, gate_centre, sums = hid_gate(
        hid, hid_centre, hid_totals, totals, vectors, mask, layers, rows
    )
    sums, cot_hop = together(sums, cot_hop)
    cots = trade(stay, cross, cot_hop)
    gate_totals, (feature_grad, full_shared) = sum_dp(
        sums, lambda: feature_back(cots, mask, quarters, shape, out_width)
    )
    features, gate_grad, share, sums = gate_back(
        gate, gate_centre, gate_totals, totals, vectors, feature_grad, feat, rows
    )

    sums, features = together(sums, features)
    gate_sums, (shared_kept, sent) = sum_dp(
        sums, lambda: shared_weights(cots, mask, features, shape, tasks, out_width)
    )
    def halve_shared(level, kept, got):
        if level == levels("task"):
            return kept, got
        kept, got = kept.reshape(-1, out_width // 2), got.reshape(-1, out_width // 2)
        if kept.shape[0] // blocks // 2 % 16 == 0:
            return add_split(level, kept, got, blocks)
        both = (kept.astype(F32) + got.astype(F32)).astype(BF)
        both = both.reshape(blocks, 2, -1, out_width // 2)
        bit = (me >> level) % 2
        return (
            lax.dynamic_index_in_dim(both, bit, 1, keepdims=False),
            lax.dynamic_index_in_dim(both, 1 - bit, 1, keepdims=False),
        )

    shared_got = swap(sent, "task", 1)
    gate_sums, shared_got = together(gate_sums, shared_got)
    shared_kept, sent = halve_shared(1, shared_kept, shared_got)
    gate_sums, sent = together(gate_sums, sent)
    shared_got = first_hop(sent)
    pre_grad, act_grad, sums = hid_back(
        gate_grad, gate, mask, gate_centre, gate_totals, totals, vectors, gate_sums, hid, hid_centre, hid_totals, layers, rows
    )
    hid_sums = sum_dp(sums)
    hid_sums, shared_got = together(hid_sums, shared_got)
    shared_kept = shared_kept.reshape(-1, out_width // 2)
    shared_got = shared_got.reshape(-1, out_width // 2)
    merged = staged and in_blocks(shared_kept.shape[0] // blocks)
    hid_pre_grad, kept, sent = feat_back(
        act_grad, hid, mask, hid_centre, hid_totals, totals, vectors, hid_sums, share, layers, rows, tasks
    )
    got = swap(sent, "task", 1)
    kept, sent = add_halve(1, kept, got, rows)
    sent, shared_kept, features, feat, hid_pre_grad = together(
        sent, shared_kept, features, feat, hid_pre_grad
    )
    got = first_hop(sent)
    pairs = [(hidden, pre_grad), (feat, hid_pre_grad)]
    if merged:
        even, odd = merge_parts(shared_kept, shared_got, pairs)
        odd, features = together(odd, features)
        part_got = swap(odd, "dp", 1)
    task_stay, task_cross = task_forward(features, full_shared, shape)
    got, task_stay, task_cross = together(got, task_stay, task_cross)
    act_grad, sums = trunk_back([kept, got], cots, trunk, own_stats, totals, vectors, shape)
    sums, task_cross = together(sums, task_cross)
    task_hop = first_hop(task_cross)
    if merged:
        trunk_sums, (even, part_got) = sum_dp(sums, lambda: (even, part_got))
        parts = add_cut(even, part_got, blocks // 2)
        parts = [swap(p, "dp", 2 * k) if k else p for k, p in enumerate(parts)]
    else:
        trunk_sums = sum_dp(sums)
    trunk_pre_grad, *weight_parts = trunk_weights(
        all_images, act_grad, trunk, labelled, own_stats, totals, vectors, trunk_sums, shape
    )
    if len(weight_parts) == 2:
        weight_got = swap(weight_parts[1], "dp", 1)
    image_stay, image_cross = image_back(trunk_pre_grad, trunk_shards, shape)
    image_hop = first_hop(image_cross)
    if len(weight_parts) == 2:
        if merged:
            weight_got, parts = together(weight_got, parts)
        weight_parts = add_cut(weight_parts[0], weight_got, blocks // 2)
        weight_parts = [swap(p, "dp", 2 * k) if k else p for k, p in enumerate(weight_parts)]
        weight_parts, image_hop, task_hop = together(weight_parts, image_hop, task_hop)
        trunk_grad = piece_sum(weight_parts, BF)
    else:
        trunk_grad = scatter_dp(weight_parts)
    trunk_grad, gate_sums, hid_sums, feat = together(trunk_grad, gate_sums, hid_sums, feat)
    trunk_grad = lay_slices(relay(trunk_grad), F32)
    own, one = first_sums(image_stay, image_hop)
    image_grad = piece_sum([own, swap(one, "task", 1)], BF).reshape(images.shape)
    if merged:
        shared_grad, attn_grad, hid_grad = split_parts(
            relay(piece_sum(parts, BF)),
            w_shared.shape[0] // (places // 2),
            (depth, width),
            tasks,
        )
    else:
        shared_grad = scatter_dp(sum_in_blocks(shared_kept, shared_got))
        for level in reversed(range(levels("task"))):
            pair = [shared_grad, swap(shared_grad, "task", 1 << level)]
            last = level == 0
            shared_grad = lay_out(
                lambda k, level=level: (lax.axis_index("task") >> level) % 2 ^ k,
                pair,
                F32 if last else BF,
                1 if last else 0,
            )
        attn_grad, hid_grad = (
            by_task(relay(scatter_dp(layer_weights([pair]))), tasks, F32) for pair in pairs
        )
    task_out = by_task(trade(task_stay, task_cross, task_hop), tasks, BF)
    task_out = task_out.reshape(tasks, image_count, row_count, cols, out_width)
    attn_bias_grad, attn_gain_grad, hid_bias_grad, hid_gain_grad, trunk_sums = split_sums(
        relay(join_sums(gate_sums, hid_sums, trunk_sums)), tasks, part
    )
    trunk_out = own_rows(feat, image_count, places)
    trunk_out = trunk_out.reshape(image_count, row_count, cols, mid)
    return (
        trunk_out,
        task_out,
        image_grad,
        trunk_grad,
        trunk_sums[1],
        trunk_sums[0],
        hid_grad,
        hid_gain_grad,
        hid_bias_grad,
        attn_grad,
        attn_gain_grad,
        attn_bias_grad,
        shared_grad,
    )


def solution(mesh):
    rows = P("dp", "task", None, None)
    task_rows = P(None, "dp", "task", None, None)
    flat, stacked = P("dp", None), P(None, "dp", None)
    pixel = P("dp", "task", None)
    return jax.shard_map(
        shards,
        mesh=mesh,
        in_specs=(
            rows,
            flat,
            P(),
            P(),
            stacked,
            P(),
            P(),
            stacked,
            P(),
            P(),
            flat,
            pixel,
            pixel,
            rows,
            task_rows,
        ),
        out_specs=(
            rows,
            task_rows,
            rows,
            flat,
            P(),
            P(),
            stacked,
            P(),
            P(),
            stacked,
            P(),
            P(),
            flat,
        ),
        check_vma=False,
    )
```

```python
import math

import jax
import jax.numpy as jnp
from jax import lax
from jax.experimental import pallas as pl
from jax.experimental.pallas import tpu as pltpu
from jax.sharding import PartitionSpec as P

EPS = 1e-05
BF = jnp.bfloat16
F32 = jnp.float32
ROOT = math.sqrt(2.0 / math.pi)
CUBE = 0.044715
VMEM = pl.BlockSpec(memory_space=pltpu.VMEM)
TRUNK_GAIN, TRUNK_BIAS, HID_GAIN, HID_BIAS, ATTN_GAIN, ATTN_BIAS = (slice(k, k + 1) for k in range(6))


def swap(x, axis, step):
    count = lax.axis_size(axis)
    return lax.ppermute(x, axis, [(i, i ^ step) for i in range(count)])


def levels(axis):
    count = lax.axis_size(axis)
    assert count & (count - 1) == 0
    return count.bit_length() - 1


def slice_of(place):
    out = 0
    for bit in range(levels("task")):
        out = out * 2 + (place >> bit) % 2
    return out


def dp_steps():
    bits, low, out = levels("dp"), 1, []
    while low < bits:
        out.append([1 << low] + ([2 << low, 3 << low] if low + 1 < bits else []))
        low += 2
    return out + ([[1]] if bits else [])


def sum_dp(x, work=None):
    steps = dp_steps()
    for step in steps[:-1]:
        x = add_up(x, *[swap(x, "dp", s) for s in step])
    done = work() if work else None
    if work:
        x, done = together(x, done)
    for step in steps[-1:]:
        x = add_up(x, *[swap(x, "dp", s) for s in step])
    return (x, done) if work else x


def together(*xs):
    return lax.optimization_barrier(xs)


def others(x, axis):
    return [x] + [swap(x, axis, k) for k in range(1, lax.axis_size(axis))]


def in_blocks(rows):
    return rows % 16 == 0 and lax.axis_size("dp") <= 8


def gather_dp(x):
    if in_blocks(x.shape[0]):
        return others(x, "dp")
    return [lax.all_gather(x, "dp", axis=0, tiled=True)]


def scatter_dp(parts):
    count = lax.axis_size("dp")
    if len(parts) == 1:
        whole = parts[0].reshape((count, -1) + parts[0].shape[1:])
        return gathered_sum(lax.all_to_all(whole, "dp", 0, 0, tiled=True), BF)
    if len(parts) == 2 and count > 2:
        parts = add_cut(parts[0], swap(parts[1], "dp", 1), count // 2)
        return piece_sum([swap(p, "dp", 2 * k) if k else p for k, p in enumerate(parts)], BF)
    return piece_sum([swap(p, "dp", k) if k else p for k, p in enumerate(parts)], BF)


def first_hop(x):
    return swap(x, "task", 2)


def relay(x, hop=None):
    near = stack_two(x, first_hop(x) if hop is None else hop)
    return near, swap(near, "task", 1)


def trade(stay, cross, hop=None):
    got = first_hop(cross) if hop is None else hop
    return stay, got, swap(second_of(stay, got), "task", 1)


def kernel_call(name, body, grid, ins, in_specs, outs, out_specs, scratch=(), limit=16, flops=0):
    return pl.pallas_call(
        body,
        name=name,
        grid=grid,
        in_specs=in_specs,
        out_specs=out_specs,
        out_shape=[jax.ShapeDtypeStruct(s, d) for s, d in outs],
        scratch_shapes=list(scratch),
        compiler_params=pltpu.CompilerParams(vmem_limit_bytes=limit * 2**20),
        cost_estimate=pl.CostEstimate(
            flops=flops, bytes_accessed=sum(x.size * x.dtype.itemsize for x in ins), transcendentals=0
        ),
    )(*ins)


def views(refs):
    if len(refs) == 2:
        near, far = refs
        return [near.at[0], far.at[0], near.at[1], far.at[1]]
    stay, got, back = refs
    return [stay.at[0], back.at[0], got.at[0], back.at[1]]


def peer(k):
    return lax.axis_index("task") ^ k


def lanes_of(place, width):
    return ds(slice_of(place) * width, width, 128)


def halves(level, size, unit=16):
    bit = (lax.axis_index("task") >> level) % 2
    return ds(bit * size, size, unit), ds((1 - bit) * size, size, unit)


def ds(start, size, unit=16):
    if isinstance(start, int):
        return pl.ds(start, size)
    return pl.ds(pl.multiple_of(start, unit), size)


def dot(a, b):
    return jnp.dot(a, b, preferred_element_type=F32)


def dot_nt(a, b):
    return lax.dot_general(a, b, (((1,), (1,)), ((), ())), preferred_element_type=F32)


def dot_tn(a, b):
    return lax.dot_general(a, b, (((0,), (0,)), ((), ())), preferred_element_type=F32)


def gelu_parts(v):
    square = v * v
    t = jnp.tanh(ROOT * v * (1.0 + CUBE * square))
    return square, t


def gelu(v):
    _, t = gelu_parts(v)
    return 0.5 * v * (1.0 + t)


def gelu_slope(v):
    square, t = gelu_parts(v)
    return 0.5 * (1.0 + t) + (0.5 * ROOT) * v * (1.0 - t * t) * (1.0 + (3.0 * CUBE) * square)


def sigmoid(v):
    return 0.5 * (1.0 + jnp.tanh(0.5 * v))


def scales(first, second, count):
    mean = first / count
    return mean, lax.rsqrt(second / count - mean * mean + EPS)


def fold(v):
    return jnp.sum(v.reshape(-1, 8, v.shape[-1]), axis=0)


def sweep(rows, width, step, sums):
    block = 16

    def body(i, carry):
        values = step(ds(i * block, block))
        return tuple(c + fold(v) for c, v in zip(carry, values, strict=True))

    start = tuple(jnp.zeros((8, width), F32) for _ in range(sums))
    out = lax.fori_loop(0, rows // block, body, start, unroll=9)
    return [jnp.sum(c, axis=0, keepdims=True) for c in out]


def spread(ref, at, width):
    m = ref[at, :]
    return m if width == 128 else jnp.concatenate([m] * (width // 128), axis=1)


def each_block(rows, step):
    def body(i, carry):
        step(ds(i * 16, 16))
        return carry

    lax.fori_loop(0, rows // 16, body, 0, unroll=9)


def accumulate(ref, parts):
    total = jnp.concatenate(parts, axis=0)

    @pl.when(pl.program_id(0) == 0)
    def _():
        ref[...] = total

    @pl.when(pl.program_id(0) != 0)
    def _():
        ref[...] += total


def fill_wide(wide_ref, piece_refs, shape, reverse, change=None, place=peer, width=None):
    image_count, row_count, places, cols = shape
    rows = row_count * cols
    width = width or piece_refs[0].shape[-1]
    span = (row_count * places + 2) * cols
    zero = jnp.zeros((cols, wide_ref.shape[1]), BF)
    column = lax.broadcasted_iota(jnp.int32, (row_count, cols, width), 1).reshape(rows, width)
    for i in range(image_count):
        wide_ref[ds(i * span, cols), :] = zero
        wide_ref[ds((i + 1) * span - cols, cols), :] = zero
        for k, ref in enumerate(piece_refs):
            start = place(k) * rows
            x = ref[i, :, :width]
            if change is not None:
                x = change(x, ds(i * rows * places + start, rows))
            wide = x.astype(F32)
            left = jnp.where(column == 0, 0.0, pltpu.roll(wide, 1, 0)).astype(BF)
            right = jnp.where(column == cols - 1, 0.0, pltpu.roll(wide, rows - 1, 0)).astype(BF)
            if reverse:
                left, right = right, left
            at = ds(i * span + cols + start, rows)
            wide_ref[at, :width] = left
            wide_ref[at, width : 2 * width] = x.astype(BF)
            wide_ref[at, 2 * width :] = right


def turn_taps(turned_ref, kernel_ref, width):
    n = kernel_ref.shape[1]
    for tap in range(9):
        p, q = divmod(tap, 3)
        turned_ref[p, :, q * n : (q + 1) * n] = kernel_ref[tap * width : (tap + 1) * width, :]


def conv_rows(wide_ref, i, c, shape, product, reverse):
    row_count, places, cols = shape[1:]
    rows = row_count * cols
    start = i * (row_count * places + 2) * cols + c * rows
    total = None
    for p in range(3):
        at = (2 - p if reverse else p) * cols
        term = product(p, wide_ref[ds(start + at, rows), :])
        total = term if total is None else total + term
    return total


def add_up(*xs):
    def body(*refs):
        total = refs[0][...]
        for ref in refs[1:-1]:
            total = total + ref[...]
        refs[-1][...] = total

    return kernel_call(
        "add_up", body, (), list(xs), [VMEM] * len(xs), [(xs[0].shape, F32)], [VMEM], limit=2
    )[0]


def side_by_side(pieces):
    rows, width = pieces[0].shape[1:]

    def body(near_ref, far_ref, out_ref):
        for k, ref in enumerate(views((near_ref, far_ref))):
            out_ref[:, k * width : (k + 1) * width] = ref[...]

    return kernel_call(
        "side_by_side", body, (), list(pieces), [VMEM] * 2, [((rows, 4 * width), F32)], [VMEM], limit=2
    )[0]


def stack_two(a, b):
    def body(a_ref, b_ref, out_ref):
        out_ref[0] = a_ref[...]
        out_ref[1] = b_ref[...]

    return kernel_call(
        "stack_two", body, (), [a, b], [VMEM] * 2, [((2,) + a.shape, a.dtype)], [VMEM]
    )[0]


def second_of(a, b):
    def body(a_ref, b_ref, out_ref):
        out_ref[0] = a_ref[1]
        out_ref[1] = b_ref[1]

    return kernel_call("second_of", body, (), [a, b], [VMEM] * 2, [(a.shape, a.dtype)], [VMEM])[0]


def first_sums(stay, got):
    def body(stay_ref, got_ref, own_ref, one_ref):
        own_ref[...] = (stay_ref[0].astype(F32) + got_ref[0].astype(F32)).astype(BF)
        one_ref[...] = (stay_ref[1].astype(F32) + got_ref[1].astype(F32)).astype(BF)

    return kernel_call(
        "first_sums",
        body,
        (),
        [stay, got],
        [VMEM] * 2,
        [(stay.shape[1:], BF)] * 2,
        [VMEM] * 2,
    )


def pack_weights(w_trunk, w_hid, w_attn, w_shared, vectors, part, quarter, copies):
    rows, (depth, width) = w_trunk.shape[0], w_hid.shape[1:]
    tasks = w_hid.shape[0]
    block = w_shared.shape[1]
    cuts = width // block
    n = len(vectors)

    def body(trunk_ref, hid_ref, attn_ref, shared_ref, *refs):
        vector_refs = refs[:n]
        first_ref, second_ref, out_ref = refs[n:]
        me = lax.axis_index("task")
        task = jnp.minimum(me, tasks - 1)
        for k in range(copies):
            first_ref[k] = trunk_ref[:, lanes_of(me, part)]
        for c in range(cuts):
            here = slice(c * block, (c + 1) * block)
            second_ref[c * depth : (c + 1) * depth, :] = hid_ref[task, :, here]
            second_ref[(cuts + c) * depth : (cuts + c + 1) * depth, :] = attn_ref[task, :, here]
        if quarter:
            second_ref[2 * cuts * depth :, :] = shared_ref[ds(me * quarter, quarter), :]
        out_ref[...] = jnp.zeros_like(out_ref)
        for k, ref in enumerate(vector_refs):
            row = ref[...] if ref.shape[0] == 1 else ref[pl.ds(task, 1), :]
            out_ref[k : k + 1, :] = row

    ins = [w_trunk, w_hid, w_attn, w_shared, *vectors]
    return kernel_call(
        "pack_weights",
        body,
        (),
        ins,
        [VMEM] * len(ins),
        [
            ((copies, rows, part), BF),
            ((2 * cuts * depth + quarter, block), BF),
            ((8, width), F32),
        ],
        [VMEM] * 3,
        limit=56,
    )


def unpack_weights(gathered, depth, width, quarter):
    count, _, block = gathered.shape
    cuts = width // block

    def body(gathered_ref, layers_ref, *outs):
        for k in range(count):
            for c in range(2 * cuts):
                layers_ref[k * depth : (k + 1) * depth, c * block : (c + 1) * block] = gathered_ref[
                    k, c * depth : (c + 1) * depth, :
                ]
            if quarter:
                outs[0][k] = gathered_ref[k, 2 * cuts * depth :, :]

    outs = [((count * depth, 2 * width), BF)]
    if quarter:
        outs.append(((count, quarter, block), BF))
    return kernel_call(
        "unpack_weights", body, (), [gathered], [VMEM], outs, [VMEM] * len(outs), limit=44
    )


def gathered_sum(parts, dtype):
    shape = parts.shape[1:]

    def body(parts_ref, out_ref):
        total = parts_ref[0].astype(F32)
        for k in range(1, parts.shape[0]):
            total = total + parts_ref[k].astype(F32)
        out_ref[...] = total.astype(dtype)

    return kernel_call("gathered_sum", body, (), [parts], [VMEM], [(shape, dtype)], [VMEM])[0]


def piece_sum(pieces, dtype):
    def body(*refs):
        total = refs[0][...].astype(F32)
        for ref in refs[1:-1]:
            total = total + ref[...].astype(F32)
        refs[-1][...] = total.astype(dtype)

    return kernel_call(
        "piece_sum", body, (), list(pieces), [VMEM] * len(pieces), [(pieces[0].shape, dtype)], [VMEM]
    )[0]


def blocks_of(whole_ref, out_refs, rows):
    me = lax.axis_index("dp")
    if len(out_refs) == 1:
        out_refs[0][...] = whole_ref[...]
    elif len(out_refs) == 2:
        for k in range(whole_ref.shape[0] // rows):
            at = k // 2 * rows
            out_refs[k % 2][at : at + rows, :] = whole_ref[ds((me ^ k) * rows, rows), :]
    else:
        for k, ref in enumerate(out_refs):
            ref[...] = whole_ref[ds((me ^ k) * rows, rows), :]


def block_shapes(rows, width, pairs):
    count = lax.axis_size("dp")
    if not in_blocks(rows):
        return [((count * rows, width), BF)]
    if pairs:
        return [((count // 2 * rows, width), BF)] * 2
    return [((rows, width), BF)] * count


def add_cut(kept, got, count):
    rows, width = kept.shape[0] // count, kept.shape[1]

    def body(kept_ref, got_ref, *out_refs):
        for k, ref in enumerate(out_refs):
            at = slice(k * rows, (k + 1) * rows)
            ref[...] = (kept_ref[at, :].astype(F32) + got_ref[at, :].astype(F32)).astype(BF)

    return kernel_call(
        "add_cut", body, (), [kept, got], [VMEM] * 2, [((rows, width), BF)] * count, [VMEM] * count
    )


def sum_in_blocks(kept, got):
    rows, width = kept.shape[0] // lax.axis_size("dp"), kept.shape[1]
    outs = block_shapes(rows, width, True)

    def body(kept_ref, got_ref, *refs):
        refs[-1][...] = (kept_ref[...].astype(F32) + got_ref[...].astype(F32)).astype(BF)
        blocks_of(refs[-1], refs[:-1], rows)

    return kernel_call(
        "sum_in_blocks",
        body,
        (),
        [kept, got],
        [VMEM] * 2,
        outs,
        [VMEM] * len(outs),
        [pltpu.VMEM(kept.shape, BF)],
    )


def lanes_below(x, width):
    return [x[:, c * width : (c + 1) * width] for c in range(x.shape[1] // width)]


def merge_parts(shared_kept, shared_got, pairs):
    count = lax.axis_size("dp")
    each, width = shared_kept.shape[0] // count, shared_kept.shape[1]
    mid = pairs[0][0].shape[1]
    rows, cuts = mid // count, mid // width
    total = each + len(pairs) * cuts * rows
    n = 2 * len(pairs)

    def body(kept_ref, got_ref, *refs):
        sum_ref, product_ref = refs[-2:]
        out_refs = refs[n : n + 2]
        me = lax.axis_index("dp")
        sum_ref[...] = (kept_ref[...].astype(F32) + got_ref[...].astype(F32)).astype(BF)
        for k in range(count):
            at = k // 2 * total
            out_refs[k % 2][at : at + each, :] = sum_ref[ds((me ^ k) * each, each), :]
        for p in range(len(pairs)):
            product_ref[...] = dot_tn(refs[2 * p][...], refs[2 * p + 1][...]).astype(BF)
            for k in range(count):
                block = product_ref[ds((me ^ k) * rows, rows), :]
                for c in range(cuts):
                    at = k // 2 * total + each + (p * cuts + c) * rows
                    out_refs[k % 2][at : at + rows, :] = block[:, c * width : (c + 1) * width]

    ins = [shared_kept, shared_got, *(x for pair in pairs for x in pair)]
    return kernel_call(
        "merge_parts",
        body,
        (),
        ins,
        [VMEM] * len(ins),
        [((count // 2 * total, width), BF)] * 2,
        [VMEM] * 2,
        [pltpu.VMEM(shared_kept.shape, BF), pltpu.VMEM((mid, mid), BF)],
        flops=2 * pairs[0][0].size * mid * len(pairs),
    )


def split_parts(pieces, shared_rows, layer_shape, tasks):
    rows, columns = layer_shape
    width = pieces[0].shape[2]

    def body(near_ref, far_ref, shared_ref, *layer_refs):
        for k, ref in enumerate(views((near_ref, far_ref))):
            place = peer(k)
            lanes = ds(place % 2 * width, width, 128)
            at = ds(place // 2 * shared_rows, shared_rows)
            shared_ref[at, lanes] = ref[:shared_rows, :].astype(F32)

            @pl.when(place < tasks)
            def _(ref=ref, place=place):
                start = shared_rows
                for layer_ref in layer_refs:
                    for c in range(columns // width):
                        value = ref[start : start + rows, :].astype(F32)
                        layer_ref[place, :, c * width : (c + 1) * width] = value
                        start += rows

    return kernel_call(
        "split_parts",
        body,
        (),
        list(pieces),
        [VMEM] * 2,
        [((shared_rows * 2, 2 * width), F32)] + [((tasks, rows, columns), F32)] * 2,
        [VMEM] * 3,
    )


def by_task(pieces, tasks, dtype):
    shape = pieces[0].shape[1:]
    n = len(pieces)

    def body(*refs):
        for k, ref in enumerate(views(refs[:n])):
            place = peer(k)

            @pl.when(place < tasks)
            def _(ref=ref, place=place):
                refs[n][place] = ref[...].astype(dtype)

    return kernel_call(
        "by_task", body, (), list(pieces), [VMEM] * n, [((tasks,) + shape, dtype)], [VMEM]
    )[0]


def trunk_total(parts, gate_sums, hid_sums, trunk_sums):
    rows, part = parts[0].shape
    width = gate_sums.shape[1]
    n = len(parts)

    def body(*refs):
        gate_ref, hid_ref, trunk_ref, out_ref = refs[n:]
        total = refs[0][...].astype(F32)
        for ref in refs[1:n]:
            total = total + ref[...].astype(F32)
        out_ref[:rows, :] = total
        out_ref[rows:, :] = jnp.zeros((out_ref.shape[0] - rows, part), F32)
        for c in range(width // part):
            here = slice(c * part, (c + 1) * part)
            at = rows + 8 * c
            out_ref[at : at + 2, :] = gate_ref[:, here]
            out_ref[at + 2 : at + 4, :] = hid_ref[:, here]
        out_ref[rows + 4 : rows + 6, :] = trunk_ref[...]

    ins = [*parts, gate_sums, hid_sums, trunk_sums]
    shape = (rows + 8 * (width // part), part)
    return kernel_call(
        "trunk_total", body, (), ins, [VMEM] * len(ins), [(shape, F32)], [VMEM]
    )[0]


def split_trunk(pieces, rows, tasks):
    part = pieces[0].shape[2]
    width = 4 * part

    def body(near_ref, far_ref, weight_ref, *refs):
        outs, trunk_ref = refs[:4], refs[4]
        for k, piece in enumerate(views((near_ref, far_ref))):
            place = peer(k)
            lanes = lanes_of(place, part)
            weight_ref[:, lanes] = piece[:rows, :]
            trunk_ref[:, lanes] = piece[rows + 4 : rows + 6, :]

            @pl.when(place < tasks)
            def _(piece=piece, place=place):
                for r, ref in enumerate(outs):
                    at = [rows + 8 * c + r for c in range(4)]
                    row = jnp.concatenate([piece[i : i + 1, :] for i in at], axis=1)
                    ref[pl.ds(place, 1), :] = row

    return kernel_call(
        "split_trunk",
        body,
        (),
        list(pieces),
        [VMEM] * 2,
        [((rows, width), F32)] + [((tasks, width), F32)] * 4 + [((2, width), F32)],
        [VMEM] * 6,
    )


def lay_out(order, pieces, dtype, along, count=None):
    n = len(pieces)
    shape = list(pieces[0].shape)
    if along == 0 and shape[0] % 16:
        out = jnp.zeros([shape[0] * n] + shape[1:], dtype)
        for k, piece in enumerate(pieces):
            out = lax.dynamic_update_slice_in_dim(out, piece.astype(dtype), order(k) * shape[0], axis=0)
        return out
    if along is None:
        whole = [count or n] + shape
    else:
        whole = list(shape)
        whole[along] *= n

    def body(*refs):
        for k in range(n):
            value = refs[k][...].astype(dtype)
            if along is None:

                @pl.when(order(k) < whole[0])
                def _(k=k, value=value):
                    refs[-1][order(k)] = value

            elif along == 0:
                refs[-1][ds(order(k) * shape[0], shape[0]), :] = value
            else:
                refs[-1][:, ds(order(k) * shape[1], shape[1], 128)] = value

    return kernel_call(
        "lay_out", body, (), list(pieces), [VMEM] * n, [(tuple(whole), dtype)], [VMEM]
    )[0]


def pack_cots(task_cot, trunk_cot, places):
    tasks, image_count, rows, out_width = task_cot.shape
    part = trunk_cot.shape[-1] // places

    def body(task_ref, trunk_ref, stay_ref, cross_ref):
        for k in range(places):
            ref = (stay_ref, cross_ref)[k // 2].at[k % 2]
            ref[:, :, :out_width] = task_ref[jnp.minimum(peer(k), tasks - 1)]
            ref[:, :, out_width:] = trunk_ref[:, :, lanes_of(peer(k), part)]

    return kernel_call(
        "pack_cots",
        body,
        (),
        [task_cot, trunk_cot],
        [VMEM, VMEM],
        [((2, image_count, rows, out_width + part), BF)] * 2,
        [VMEM] * 2,
    )


def trunk_forward(labelled, counts, images, shards, shape):
    image_count, row_count, places, cols = shape
    rows = row_count * cols
    count, each, part = shards.shape
    depth = count * each
    pixels = image_count * places * rows
    in_width = images.shape[-1]

    def body(mask_ref, counts_ref, images_ref, shards_ref, centred_ref, stats_ref, kernel_ref, wide_ref, pre_ref):
        for k in range(count):
            kernel_ref[k * each : (k + 1) * each, :] = shards_ref[k]
        pieces = [images_ref.at[:, k] for k in range(places)]
        fill_wide(wide_ref, pieces, shape, False, place=lambda k: k)
        block = 3 * in_width

        def chunk(c, carry):
            for i in range(image_count):
                value = conv_rows(
                    wide_ref,
                    i,
                    c,
                    shape,
                    lambda p, x: dot(x, kernel_ref[p * block : (p + 1) * block, :]),
                    False,
                )
                pre_ref[ds((i * places + c) * rows, rows), :] = value
            return carry

        lax.fori_loop(0, places, chunk, 0)

        def moments(at):
            v = pre_ref[at, :]
            mv = mask_ref[at, :] * v
            return mv, mv * v, v

        sums = sweep(pixels, part, moments, 3)
        mean = sums[2] / pixels
        stats_ref[...] = jnp.concatenate(sums[:2] + [counts_ref[...]] + [mean] * 4, axis=0)

        def centre(at):
            centred_ref[at, :] = (pre_ref[at, :] - mean).astype(BF)

        each_block(pixels, centre)

    return kernel_call(
        "trunk_forward",
        body,
        (),
        [labelled, counts, images, shards],
        [VMEM] * 4,
        [((pixels, part), BF), ((8, part), F32)],
        [VMEM] * 2,
        [
            pltpu.VMEM((depth, part), BF),
            pltpu.VMEM((image_count * (row_count * places + 2) * cols, 3 * in_width), BF),
            pltpu.VMEM((pixels, part), F32),
        ],
        flops=2 * pixels * depth * part,
    )


def rows_spec(rows, width):
    return pl.BlockSpec((rows, width), lambda i: (i, 0))


def fixed_spec(shape):
    return pl.BlockSpec(shape, lambda i: (0,) * len(shape))


def centre_on_first(value_ref, centre_ref, centred_ref):
    @pl.when(pl.program_id(0) == 0)
    def _():
        rows = value_ref.shape[0]
        (total,) = sweep(rows, value_ref.shape[1], lambda at: (value_ref[at, :],), 1)
        centre_ref[...] = total / rows

    centre = centre_ref[...]

    def step(at):
        centred_ref[at, :] = (value_ref[at, :] - centre).astype(BF)

    each_block(value_ref.shape[0], step)


def feat_hid(scaled, stats, totals, vectors, mask, kernel, rows, image_count):
    pixels, part = scaled[0].shape[1:]
    n = 2 * len(scaled)
    mid = part * n
    out_mid = mid

    def body(*refs):
        scaled_refs = views(refs[:2])
        stats_ref, totals_ref, vectors_ref, mask_ref, kernel_ref = refs[2:7]
        feat_ref, centred_ref, centre_ref, sums_ref, own_ref, affine_ref, hid_ref = refs[7:]

        @pl.when(pl.program_id(0) == 0)
        def _():
            count = jnp.maximum(totals_ref[2:3, :], 1.0)
            mean, rstd = scales(totals_ref[0:1, :], totals_ref[1:2, :], count)
            for k in range(n):
                here = slice(k * part, (k + 1) * part)
                at = lanes_of(peer(k), part)
                slope = rstd[:, here] * vectors_ref[TRUNK_GAIN, at]
                affine_ref[0:1, here] = slope
                affine_ref[1:2, here] = (stats_ref[4:5, here] - mean[:, here]) * slope + vectors_ref[TRUNK_BIAS, at]

        def activate(at):
            for k in range(n):
                here = slice(k * part, (k + 1) * part)
                v = scaled_refs[k][at, :].astype(F32) * affine_ref[0:1, here] + affine_ref[1:2, here]
                feat_ref[at, lanes_of(peer(k), part)] = gelu(v).astype(BF)

        each_block(rows, activate)
        hid_ref[...] = dot(feat_ref[...], kernel_ref[...])

        @pl.when(pl.program_id(0) % n == peer(0))
        def _():
            own_ref[pl.program_id(0) // n] = feat_ref[...]

        def moments(at):
            v = hid_ref[at, :]
            mv = spread(mask_ref, at, out_mid) * v
            return mv, mv * v

        accumulate(sums_ref, sweep(rows, out_mid, moments, 2))
        centre_on_first(hid_ref, centre_ref, centred_ref)

    return kernel_call(
        "feat_hid",
        body,
        (pixels // rows,),
        [*scaled, stats, totals, vectors, mask, kernel],
        [pl.BlockSpec((2, rows, part), lambda i: (0, i, 0))] * 2
        + [fixed_spec(x.shape) for x in (stats, totals, vectors)]
        + [rows_spec(rows, 128), pl.BlockSpec((mid, out_mid), lambda i: (0, 0))],
        [
            ((pixels, mid), BF),
            ((pixels, out_mid), BF),
            ((1, out_mid), F32),
            ((2, out_mid), F32),
            ((image_count, rows, mid), BF),
        ],
        [
            rows_spec(rows, mid),
            rows_spec(rows, out_mid),
            fixed_spec((1, out_mid)),
            fixed_spec((2, out_mid)),
            fixed_spec((image_count, rows, mid)),
        ],
        [pltpu.VMEM((2, mid), F32), pltpu.VMEM((rows, out_mid), F32)],
        flops=2 * pixels * mid * out_mid,
    )


def task_count(totals_ref):
    chosen = jnp.where(lax.axis_index("task") == 0, totals_ref[2:3, 0:1], totals_ref[3:4, 0:1])
    return jnp.maximum(chosen, 1.0)


def normed_rows(sums, count, centre):
    mean, rstd = scales(sums[0:1, :], sums[1:2, :], count)
    return rstd, (centre - mean) * rstd


def hid_gate(hid, centre, sums, totals, vectors, mask, kernel, rows):
    pixels, mid = hid.shape

    def body(*refs):
        hid_ref, middle_ref, sums_ref, totals_ref, vectors_ref, mask_ref, kernel_ref = refs[:7]
        hidden_ref, centred_ref, centre_ref, out_ref, gate_ref = refs[7:]
        count = task_count(totals_ref)
        gain, bias = vectors_ref[HID_GAIN, :], vectors_ref[HID_BIAS, :]
        scale, shift = normed_rows(sums_ref[...], count, middle_ref[...])
        scale, shift = scale * gain, shift * gain + bias

        def activate(at):
            hidden_ref[at, :] = gelu(hid_ref[at, :].astype(F32) * scale + shift).astype(BF)

        each_block(rows, activate)
        gate_ref[...] = dot(hidden_ref[...], kernel_ref[...])

        def moments(at):
            v = gate_ref[at, :]
            mv = spread(mask_ref, at, mid) * v
            return mv, mv * v

        accumulate(out_ref, sweep(rows, mid, moments, 2))
        centre_on_first(gate_ref, centre_ref, centred_ref)

    wide = rows_spec(rows, mid)
    return kernel_call(
        "hid_gate",
        body,
        (pixels // rows,),
        [hid, centre, sums, totals, vectors, mask, kernel],
        [wide]
        + [fixed_spec(x.shape) for x in (centre, sums, totals, vectors)]
        + [rows_spec(rows, 128), pl.BlockSpec((mid, mid), lambda i: (0, 1))],
        [((pixels, mid), BF), ((pixels, mid), BF), ((1, mid), F32), ((2, mid), F32)],
        [wide, wide, fixed_spec((1, mid)), fixed_spec((2, mid))],
        [pltpu.VMEM((rows, mid), F32)],
        flops=2 * pixels * mid * mid,
    )


def feature_back(cot, mask, kernels, shape, out_width):
    image_count, row_count, places, cols = shape
    rows = row_count * cols
    mid = sum(x.size for x in kernels) // out_width // 9
    pixels = image_count * places * rows
    n, m = len(cot), len(kernels)
    count = 2 * m if m > 1 else 1

    def body(*refs):
        cot_refs = views(refs[:n])
        mask_ref = refs[n]
        quarter_refs = refs[1 + n : 1 + n + m]
        if m > 1:
            quarter_refs = views(quarter_refs)
        out_ref, kernel_ref, wide_ref, turned_ref = refs[1 + n + m :]
        blocks, quarter = quarter_refs[0].shape[:2]
        for k, ref in enumerate(quarter_refs):
            for j in range(blocks):
                kernel_ref[ds((j * count + (peer(k) if m > 1 else 0)) * quarter, quarter), :] = ref[j]
        turn_taps(turned_ref, kernel_ref, mid)
        fill_wide(
            wide_ref,
            cot_refs,
            shape,
            True,
            lambda x, at: x.astype(F32) * spread(mask_ref, at, out_width),
            width=out_width,
        )

        def chunk(c, carry):
            for i in range(image_count):
                value = conv_rows(
                    wide_ref, i, c, shape, lambda p, x: dot_nt(x, turned_ref[p]), True
                )
                out_ref[ds((i * places + c) * rows, rows), :] = value.astype(BF)
            return carry

        lax.fori_loop(0, places, chunk, 0)

    return kernel_call(
        "feature_back",
        body,
        (),
        [*cot, mask, *kernels],
        [VMEM] * (n + 1 + m),
        [((pixels, mid), BF), ((9 * mid, out_width), BF)],
        [VMEM] * 2,
        [
            pltpu.VMEM((image_count * (row_count * places + 2) * cols, 3 * out_width), BF),
            pltpu.VMEM((3, mid, 3 * out_width), BF),
        ],
        limit=24,
        flops=2 * pixels * 9 * mid * out_width,
    )


def gate_back(gate, centre, sums, totals, vectors, feature_grad, feat, rows):
    pixels, mid = gate.shape

    def body(gate_ref, centre_ref, sums_ref, totals_ref, vectors_ref, grad_ref, feat_ref, *outs):
        features_ref, gate_grad_ref, share_ref, out_ref = outs
        scale, shift = normed_rows(sums_ref[...], task_count(totals_ref), centre_ref[...])
        slope = 0.5 * vectors_ref[ATTN_GAIN, :]
        offset = 0.5 * vectors_ref[ATTN_BIAS, :]

        def step(at):
            normed = gate_ref[at, :].astype(F32) * scale + shift
            t = jnp.tanh(normed * slope + offset)
            attention = 0.5 + 0.5 * t
            features = attention * feat_ref[at, :].astype(F32)
            features_ref[at, :] = features.astype(BF)
            grad = grad_ref[at, :].astype(F32)
            share_ref[at, :] = (grad * attention).astype(BF)
            gate_grad = grad * features * (0.5 - 0.5 * t)
            gate_grad_ref[at, :] = gate_grad.astype(BF)
            return gate_grad, gate_grad * normed

        accumulate(out_ref, sweep(rows, mid, step, 2))

    wide = rows_spec(rows, mid)
    return kernel_call(
        "gate_back",
        body,
        (pixels // rows,),
        [gate, centre, sums, totals, vectors, feature_grad, feat],
        [wide] + [fixed_spec(x.shape) for x in (centre, sums, totals, vectors)] + [wide, wide],
        [((pixels, mid), BF)] * 3 + [((2, mid), F32)],
        [wide] * 3 + [fixed_spec((2, mid))],
    )


def back_rows(gain, sums, count, centre, back):
    rstd, shift = normed_rows(sums, count, centre)
    scale = gain * rstd
    tilt = scale * back[1:2, :] / count
    return scale, scale * back[0:1, :] / count + tilt * shift, tilt * rstd


def hid_back(grad, gate, mask, centre, sums, totals, vectors, back, hid, h_centre, h_sums, kernel, rows):
    pixels, mid = grad.shape

    def body(*refs):
        grad_ref, gate_ref, mask_ref, centre_ref, sums_ref, totals_ref, vectors_ref, back_ref = refs[:8]
        hid_ref, h_centre_ref, h_sums_ref, kernel_ref = refs[8:12]
        pre_ref, act_ref, out_ref, value_ref = refs[12:]
        count = task_count(totals_ref)
        h_gain, h_bias = vectors_ref[HID_GAIN, :], vectors_ref[HID_BIAS, :]
        scale, lean, tilt = back_rows(
            vectors_ref[ATTN_GAIN, :], sums_ref[...], count, centre_ref[...], back_ref[...]
        )

        def step(at):
            lost = spread(mask_ref, at, mid) * (lean + gate_ref[at, :].astype(F32) * tilt)
            pre_ref[at, :] = (grad_ref[at, :].astype(F32) * scale - lost).astype(BF)

        each_block(rows, step)
        value_ref[...] = dot_nt(pre_ref[...], kernel_ref[...])
        h_scale, h_shift = normed_rows(h_sums_ref[...], count, h_centre_ref[...])

        def slope(at):
            x = hid_ref[at, :].astype(F32) * h_scale + h_shift
            value = value_ref[at, :] * gelu_slope(x * h_gain + h_bias)
            act_ref[at, :] = value.astype(BF)
            return value, value * x

        accumulate(out_ref, sweep(rows, mid, slope, 2))

    wide = rows_spec(rows, mid)
    return kernel_call(
        "hid_back",
        body,
        (pixels // rows,),
        [grad, gate, mask, centre, sums, totals, vectors, back, hid, h_centre, h_sums, kernel],
        [wide, wide, rows_spec(rows, 128)]
        + [fixed_spec(x.shape) for x in (centre, sums, totals, vectors, back)]
        + [wide]
        + [fixed_spec(x.shape) for x in (h_centre, h_sums)]
        + [pl.BlockSpec((mid, mid), lambda i: (0, 1))],
        [((pixels, mid), BF), ((pixels, mid), BF), ((2, mid), F32)],
        [wide, wide, fixed_spec((2, mid))],
        [pltpu.VMEM((rows, mid), F32)],
        flops=2 * pixels * mid * mid,
    )


def feat_back(act_grad, hid, mask, centre, sums, totals, vectors, back, share, kernel, rows, tasks):
    pixels, mid = act_grad.shape
    half = mid // 2

    def body(*refs):
        act_ref, hid_ref, mask_ref, centre_ref, sums_ref, totals_ref = refs[:6]
        vectors_ref, back_ref, share_ref, kernel_ref, pre_ref, kept_ref, sent_ref, part_ref = refs[6:]
        active = jnp.where(lax.axis_index("task") < tasks, 1.0, 0.0)
        scale, lean, tilt = back_rows(
            vectors_ref[HID_GAIN, :],
            sums_ref[...],
            task_count(totals_ref),
            centre_ref[...],
            back_ref[...],
        )

        def step(at):
            lost = spread(mask_ref, at, mid) * (lean + hid_ref[at, :].astype(F32) * tilt)
            pre_ref[at, :] = (act_ref[at, :].astype(F32) * scale - lost).astype(BF)

        each_block(rows, step)
        part_ref[...] = dot_nt(pre_ref[...], kernel_ref[...])

        def add(at):
            for ref, here in zip((kept_ref, sent_ref), halves(0, half, 128), strict=True):
                value = part_ref[at, here] + share_ref[at, here].astype(F32)
                ref[at, :] = (value * active).astype(BF)

        each_block(rows, add)

    wide = rows_spec(rows, mid)
    return kernel_call(
        "feat_back",
        body,
        (pixels // rows,),
        [act_grad, hid, mask, centre, sums, totals, vectors, back, share, kernel],
        [wide, wide, rows_spec(rows, 128)]
        + [fixed_spec(x.shape) for x in (centre, sums, totals, vectors, back)]
        + [wide]
        + [pl.BlockSpec((mid, mid), lambda i: (0, 0))],
        [((pixels, mid), BF), ((pixels, half), BF), ((pixels, half), BF)],
        [wide, rows_spec(rows, half), rows_spec(rows, half)],
        [pltpu.VMEM((rows, mid), F32)],
        flops=2 * pixels * mid * mid,
    )


def add_halve(level, kept, got, rows):
    pixels, width = kept.shape
    half = width // 2

    def body(kept_ref, got_ref, a_ref, b_ref):
        for ref, here in zip((a_ref, b_ref), halves(level, half, 128), strict=True):
            ref[...] = (kept_ref[:, here].astype(F32) + got_ref[:, here].astype(F32)).astype(BF)

    wide, slim = rows_spec(rows, width), rows_spec(rows, half)
    return kernel_call(
        "add_halve",
        body,
        (pixels // rows,),
        [kept, got],
        [wide, wide],
        [((pixels, half), BF)] * 2,
        [slim, slim],
    )


def trunk_back(parts, cots, trunk, stats, totals, vectors, shape):
    image_count, row_count, places, cols = shape
    rows = row_count * cols
    pixels, width = trunk.shape
    first = cots[0].shape[-1] - width
    n, m = len(parts), len(cots)

    def body(*refs):
        part_refs = refs[:n]
        cot_refs = views(refs[n : n + m])
        trunk_ref, stats_ref, totals_ref, vectors_ref, grad_ref, out_ref = refs[n + m :]
        lanes = lanes_of(peer(0), width)
        gain, bias = vectors_ref[TRUNK_GAIN, lanes], vectors_ref[TRUNK_BIAS, lanes]
        totals = totals_ref[:, :width]
        count = jnp.maximum(totals[2:3, :], 1.0)
        scale, shift = normed_rows(totals, count, stats_ref[4:5, :])
        total = [0.0, 0.0]
        for i in range(image_count):
            for k, cot_ref in enumerate(cot_refs):
                start = (i * places + peer(k)) * rows

                def step(at, start=start, cot_ref=cot_ref, i=i):
                    here = ds(start + at.start, at.size)
                    x = trunk_ref[here, :].astype(F32) * scale + shift
                    grad = cot_ref[i, at, first:].astype(F32)
                    for ref in part_refs:
                        grad = grad + ref[here, :].astype(F32)
                    grad = grad * gelu_slope(x * gain + bias)
                    grad_ref[here, :] = grad.astype(BF)
                    return grad, grad * x

                found = sweep(rows, width, step, 2)
                total = [a + b for a, b in zip(total, found, strict=True)]
        out_ref[...] = jnp.concatenate(total, axis=0)

    return kernel_call(
        "trunk_back",
        body,
        (),
        [*parts, *cots, trunk, stats, totals, vectors],
        [VMEM] * (n + m + 4),
        [((pixels, width), BF), ((2, width), F32)],
        [VMEM] * 2,
    )


def trunk_weights(images, grad, trunk, mask, stats, totals, vectors, back, shape):
    image_count, row_count, places, cols = shape
    rows = row_count * cols
    in_width = images.shape[-1]
    pixels, part = grad.shape
    depth = 9 * in_width // lax.axis_size("dp")
    outs = block_shapes(depth, part, True)
    span = (row_count * places + 2) * cols
    whole = row_count * places * cols

    def body(*refs):
        images_ref, grad_ref, trunk_ref, mask_ref, stats_ref, totals_ref, vectors_ref, back_ref = refs[:8]
        out_ref = refs[8]
        weight_ref, wide_ref = refs[-2:]
        totals = totals_ref[:, :part]
        count = jnp.maximum(totals[2:3, :], 1.0)
        scale, lean, tilt = back_rows(
            vectors_ref[TRUNK_GAIN, lanes_of(peer(0), part)], totals, count, stats_ref[4:5, :], back_ref[...]
        )

        def step(at):
            lost = mask_ref[at, :] * (lean + trunk_ref[at, :].astype(F32) * tilt)
            out_ref[at, :] = (grad_ref[at, :].astype(F32) * scale - lost).astype(BF)

        each_block(pixels, step)
        fill_wide(
            wide_ref,
            [images_ref.at[:, k] for k in range(places)],
            shape,
            False,
            place=lambda k: k,
        )
        for p in range(3):
            total = None
            for i in range(image_count):
                term = dot_tn(
                    wide_ref[ds(i * span + p * cols, whole), :], out_ref[ds(i * whole, whole), :]
                )
                total = term if total is None else total + term
            weight_ref[p * 3 * in_width : (p + 1) * 3 * in_width, :] = total.astype(BF)
        blocks_of(weight_ref, refs[9:-2], depth)

    return kernel_call(
        "trunk_weights",
        body,
        (),
        [images, grad, trunk, mask, stats, totals, vectors, back],
        [VMEM] * 8,
        [((pixels, part), BF), *outs],
        [VMEM] * (1 + len(outs)),
        [
            pltpu.VMEM((9 * in_width, part), BF),
            pltpu.VMEM((image_count * span, 3 * in_width), BF),
        ],
        flops=2 * pixels * 9 * in_width * part,
    )


def image_back(grad, shards, shape):
    image_count, row_count, places, cols = shape
    rows = row_count * cols
    part = grad.shape[-1]
    count, each = shards.shape[:2]
    in_width = count * each // 9

    def body(grad_ref, shards_ref, *refs):
        out_refs = [refs[k // 2].at[k % 2] for k in range(places)]
        kernel_ref, wide_ref, turned_ref = refs[2:]
        for k in range(count):
            kernel_ref[k * each : (k + 1) * each, :] = shards_ref[k]
        turn_taps(turned_ref, kernel_ref, in_width)
        pieces = [grad_ref.at[:, k] for k in range(places)]
        fill_wide(wide_ref, pieces, shape, True, place=lambda k: k)
        for k, ref in enumerate(out_refs):
            for i in range(image_count):
                value = conv_rows(
                    wide_ref, i, peer(k), shape, lambda p, x: dot_nt(x, turned_ref[p]), True
                )
                ref[i] = value.astype(BF)

    return kernel_call(
        "image_back",
        body,
        (),
        [grad.reshape(image_count, places, rows, part), shards],
        [VMEM, VMEM],
        [((2, image_count, rows, in_width), BF)] * 2,
        [VMEM] * 2,
        [
            pltpu.VMEM((count * each, part), BF),
            pltpu.VMEM((image_count * (row_count * places + 2) * cols, 3 * part), BF),
            pltpu.VMEM((3, in_width, 3 * part), BF),
        ],
        flops=2 * grad.size * 9 * in_width,
    )


def task_forward(features, kernel, shape):
    image_count, row_count, places, cols = shape
    rows = row_count * cols
    mid = features.shape[-1]
    out_width = kernel.shape[1]
    block = 3 * mid

    def body(features_ref, kernel_ref, *refs):
        out_refs = [refs[k // 2].at[k % 2] for k in range(places)]
        (wide_ref,) = refs[2:]
        pieces = [features_ref.at[:, k] for k in range(places)]
        fill_wide(wide_ref, pieces, shape, False, place=lambda k: k)
        for k, ref in enumerate(out_refs):
            for i in range(image_count):
                value = conv_rows(
                    wide_ref,
                    i,
                    peer(k),
                    shape,
                    lambda p, x: dot(x, kernel_ref[p * block : (p + 1) * block, :]),
                    False,
                )
                ref[i] = value.astype(BF)

    return kernel_call(
        "task_forward",
        body,
        (),
        [features.reshape(image_count, places, rows, mid), kernel],
        [VMEM, VMEM],
        [((2, image_count, rows, out_width), BF)] * 2,
        [VMEM] * 2,
        [
            pltpu.VMEM((image_count * (row_count * places + 2) * cols, 3 * mid), BF),
        ],
        limit=24,
        flops=2 * features.size * 9 * out_width,
    )


def add_split(level, kept, got, blocks):
    rows, width = kept.shape
    half = rows // blocks // 2

    def body(kept_ref, got_ref, a_ref, b_ref):
        bit = (lax.axis_index("task") >> level) % 2
        for ref, which in ((a_ref, bit), (b_ref, 1 - bit)):
            for j in range(blocks):
                at = ds((2 * j + which) * half, half)
                value = kept_ref[at, :].astype(F32) + got_ref[at, :].astype(F32)
                ref[j] = value.astype(BF)

    return kernel_call(
        "add_split",
        body,
        (),
        [kept, got],
        [VMEM, VMEM],
        [((blocks, half, width), BF)] * 2,
        [VMEM] * 2,
    )


def layer_weights(pairs):
    mid = pairs[0][0].shape[1]
    rows = mid // lax.axis_size("dp")
    outs = block_shapes(rows, mid * len(pairs), True)
    n = 2 * len(pairs)

    def body(*refs):
        for k in range(len(pairs)):
            value = dot_tn(refs[2 * k][...], refs[2 * k + 1][...])
            refs[-1][:, k * mid : (k + 1) * mid] = value.astype(BF)
        blocks_of(refs[-1], refs[n:-1], rows)

    ins = [x for pair in pairs for x in pair]
    return kernel_call(
        "layer_weights",
        body,
        (),
        ins,
        [VMEM] * n,
        outs,
        [VMEM] * len(outs),
        [pltpu.VMEM((mid, mid * len(pairs)), BF)],
        flops=2 * pairs[0][0].size * mid * len(pairs),
    )


def shared_weights(cot, mask, features, shape, tasks, out_width):
    image_count, row_count, places, cols = shape
    rows = row_count * cols
    mid = features.shape[-1]
    n = len(cot)
    half = out_width // 2
    span = (row_count * places + 2) * cols
    whole = row_count * places * cols

    def body(*refs):
        cot_refs = views(refs[:n])
        mask_ref, features_ref, kept_ref, sent_ref, wide_ref, part_ref = refs[n:]
        active = jnp.where(lax.axis_index("task") < tasks, 1.0, 0.0)
        fill_wide(
            wide_ref,
            cot_refs,
            shape,
            True,
            lambda x, at: x.astype(F32) * spread(mask_ref, at, out_width) * active,
            width=out_width,
        )
        for tap in range(9):
            p, q = divmod(tap, 3)
            total = None
            for i in range(image_count):
                term = dot_tn(
                    features_ref[ds(i * whole, whole), :],
                    wide_ref[
                        ds(i * span + (2 - p) * cols, whole), q * out_width : (q + 1) * out_width
                    ],
                )
                total = term if total is None else total + term
            part_ref[...] = total
            for ref, here in zip((kept_ref, sent_ref), halves(0, half, 128), strict=True):
                ref[tap * mid : (tap + 1) * mid, :] = part_ref[:, here].astype(BF)

    return kernel_call(
        "shared_weights",
        body,
        (),
        [*cot, mask, features],
        [VMEM] * (n + 2),
        [((9 * mid, half), BF)] * 2,
        [VMEM, VMEM],
        [
            pltpu.VMEM((image_count * span, 3 * out_width), BF),
            pltpu.VMEM((mid, out_width), F32),
        ],
        flops=2 * features.size * 9 * out_width,
    )


def shards(
    images,
    w_trunk,
    trunk_gain,
    trunk_bias,
    w_hid,
    hid_gain,
    hid_bias,
    w_attn,
    attn_gain,
    attn_bias,
    w_shared,
    labels,
    depth_valid,
    trunk_cot,
    task_cot,
):
    image_count, row_count, cols, in_width = images.shape
    mid = w_trunk.shape[1]
    out_width = w_shared.shape[1]
    tasks, depth, width = w_hid.shape
    places = lax.axis_size("task")
    assert tasks <= places == 4
    part = mid // places
    me = lax.axis_index("task")
    rows = row_count * cols
    pixels = image_count * places * rows
    shape = (image_count, row_count, places, cols)
    blocks = lax.axis_size("dp")

    quarter = w_shared.shape[0] // places
    staged = quarter % 16 == 0 and in_blocks(w_trunk.shape[0]) and blocks >= 4
    vectors = [trunk_gain[None], trunk_bias[None], hid_gain, hid_bias, attn_gain, attn_bias]
    first, second, vectors = pack_weights(
        w_trunk, w_hid, w_attn, w_shared, vectors, part, quarter * staged, blocks
    )
    trunk_shards = lax.all_to_all(first, "dp", 0, 0, tiled=True)
    gathered = lax.all_gather(second, "dp", axis=0, tiled=False)
    marks = jnp.stack([(labels >= 0).astype(F32), depth_valid.astype(F32)])
    marks = lax.all_gather(marks, "task", axis=2, tiled=True).reshape(2, pixels)
    marks, images = together(marks, images)
    all_images = lax.all_gather(
        images.reshape(image_count, rows, in_width), "task", axis=1, tiled=False
    )
    counts = jnp.broadcast_to(jnp.sum(marks, 1)[:, None], (2, part))
    labelled = jnp.broadcast_to(marks[0][:, None], (pixels, 128))
    mask = jnp.where(me == 0, labelled, jnp.broadcast_to(marks[1][:, None], (pixels, 128)))
    trunk_shards, all_images, labelled, mask, counts = together(
        trunk_shards, all_images, labelled, mask, counts
    )

    trunk, own_stats = trunk_forward(labelled, counts, all_images, trunk_shards, shape)
    hop, trunk = together(first_hop(own_stats), trunk)
    stats = side_by_side(relay(own_stats, hop))
    totals, (trunk, hop, trunk_cot, task_cot) = sum_dp(
        stats, lambda: (trunk, first_hop(trunk), trunk_cot, task_cot)
    )
    stay, cross = pack_cots(
        task_cot.reshape(tasks, image_count, rows, out_width),
        trunk_cot.reshape(image_count, rows, mid),
        places,
    )
    cot_hop = first_hop(cross)
    scaled = relay(trunk, hop)
    totals, gathered = together(totals, gathered)
    layers, *quarters = unpack_weights(gathered, depth, width, quarter * staged)
    if staged:
        hop = first_hop(quarters[0])
    feat, hid, hid_centre, sums, trunk_out = feat_hid(
        scaled, stats, totals, vectors, mask, layers, rows, image_count
    )
    hid_totals = sum_dp(sums)
    hidden, gate, gate_centre, sums = hid_gate(
        hid, hid_centre, hid_totals, totals, vectors, mask, layers, rows
    )
    if staged:
        sums, hop, cot_hop = together(sums, hop, cot_hop)
        quarters = relay(quarters[0], hop)
    else:
        quarters = [lax.all_gather(w_shared, "dp", axis=0, tiled=True)[None]]
    cots = trade(stay, cross, cot_hop)
    gate_totals, (feature_grad, full_shared) = sum_dp(
        sums, lambda: feature_back(cots, mask, quarters, shape, out_width)
    )
    features, gate_grad, share, sums = gate_back(
        gate, gate_centre, gate_totals, totals, vectors, feature_grad, feat, rows
    )

    sums, features = together(sums, features)
    gate_sums, (shared_kept, sent) = sum_dp(
        sums, lambda: shared_weights(cots, mask, features, shape, tasks, out_width)
    )
    def halve_shared(level, kept, got):
        if level == levels("task"):
            return kept, got
        kept, got = kept.reshape(-1, out_width // 2), got.reshape(-1, out_width // 2)
        if kept.shape[0] // blocks // 2 % 16 == 0:
            return add_split(level, kept, got, blocks)
        both = (kept.astype(F32) + got.astype(F32)).astype(BF)
        both = both.reshape(blocks, 2, -1, out_width // 2)
        bit = (me >> level) % 2
        return (
            lax.dynamic_index_in_dim(both, bit, 1, keepdims=False),
            lax.dynamic_index_in_dim(both, 1 - bit, 1, keepdims=False),
        )

    shared_got = swap(sent, "task", 1)
    gate_sums, shared_got = together(gate_sums, shared_got)
    shared_kept, sent = halve_shared(1, shared_kept, shared_got)
    gate_sums, sent = together(gate_sums, sent)
    shared_got = first_hop(sent)
    pre_grad, act_grad, sums = hid_back(
        gate_grad, gate, mask, gate_centre, gate_totals, totals, vectors, gate_sums, hid, hid_centre, hid_totals, layers, rows
    )
    hid_sums = sum_dp(sums)
    hid_sums, shared_got = together(hid_sums, shared_got)
    shared_kept = shared_kept.reshape(-1, out_width // 2)
    shared_got = shared_got.reshape(-1, out_width // 2)
    merged = staged and in_blocks(shared_kept.shape[0] // blocks)
    hid_pre_grad, kept, sent = feat_back(
        act_grad, hid, mask, hid_centre, hid_totals, totals, vectors, hid_sums, share, layers, rows, tasks
    )
    got = swap(sent, "task", 1)
    pairs = [(hidden, pre_grad), (feat, hid_pre_grad)]
    if merged:
        even, odd = merge_parts(shared_kept, shared_got, pairs)
        got, even, odd = together(got, even, odd)
    kept, sent = add_halve(1, kept, got, rows)
    sent, features = together(sent, features)
    got = first_hop(sent)
    if merged:
        sent, odd = together(sent, odd)
        part_got = swap(odd, "dp", 1)
    task_stay, task_cross = task_forward(features, full_shared, shape)
    got, task_stay, task_cross = together(got, task_stay, task_cross)
    act_grad, sums = trunk_back([kept, got], cots, trunk, own_stats, totals, vectors, shape)
    sums, task_cross = together(sums, task_cross)
    task_hop = first_hop(task_cross)
    if merged:
        trunk_sums, (even, part_got) = sum_dp(sums, lambda: (even, part_got))
        parts = add_cut(even, part_got, blocks // 2)
        parts = [swap(p, "dp", 2 * k) if k else p for k, p in enumerate(parts)]
    else:
        trunk_sums = sum_dp(sums)
    trunk_pre_grad, *weight_parts = trunk_weights(
        all_images, act_grad, trunk, labelled, own_stats, totals, vectors, trunk_sums, shape
    )
    if len(weight_parts) == 2:
        weight_got = swap(weight_parts[1], "dp", 1)
    image_stay, image_cross = image_back(trunk_pre_grad, trunk_shards, shape)
    if merged:
        parts, image_cross = together(parts, image_cross)
    image_hop = first_hop(image_cross)
    if len(weight_parts) == 2:
        weight_parts = add_cut(weight_parts[0], weight_got, blocks // 2)
        weight_parts = [swap(p, "dp", 2 * k) if k else p for k, p in enumerate(weight_parts)]
        weight_parts, image_hop, task_hop = together(weight_parts, image_hop, task_hop)
    else:
        weight_parts = [scatter_dp(weight_parts)]
    weight_rows = weight_parts[0].shape[0]
    near, far = relay(trunk_total(weight_parts, gate_sums, hid_sums, trunk_sums))
    trunk_grad, attn_bias_grad, attn_gain_grad, hid_bias_grad, hid_gain_grad, trunk_sums = split_trunk(
        (near, far), weight_rows, tasks
    )
    own, one = first_sums(image_stay, image_hop)
    image_grad = piece_sum([own, swap(one, "task", 1)], BF).reshape(images.shape)
    if merged:
        shared_grad, attn_grad, hid_grad = split_parts(
            relay(piece_sum(parts, BF)),
            w_shared.shape[0] // (places // 2),
            (depth, width),
            tasks,
        )
    else:
        shared_grad = scatter_dp(sum_in_blocks(shared_kept, shared_got))
        for level in reversed(range(levels("task"))):
            pair = [shared_grad, swap(shared_grad, "task", 1 << level)]
            last = level == 0
            shared_grad = lay_out(
                lambda k, level=level: (lax.axis_index("task") >> level) % 2 ^ k,
                pair,
                F32 if last else BF,
                1 if last else 0,
            )
        attn_grad, hid_grad = (
            by_task(relay(scatter_dp(layer_weights([pair]))), tasks, F32) for pair in pairs
        )
    task_out = by_task(trade(task_stay, task_cross, task_hop), tasks, BF)
    task_out = task_out.reshape(tasks, image_count, row_count, cols, out_width)
    trunk_out = trunk_out.reshape(image_count, row_count, cols, mid)
    return (
        trunk_out,
        task_out,
        image_grad,
        trunk_grad,
        trunk_sums[1],
        trunk_sums[0],
        hid_grad,
        hid_gain_grad,
        hid_bias_grad,
        attn_grad,
        attn_gain_grad,
        attn_bias_grad,
        shared_grad,
    )


def solution(mesh):
    rows = P("dp", "task", None, None)
    task_rows = P(None, "dp", "task", None, None)
    flat, stacked = P("dp", None), P(None, "dp", None)
    pixel = P("dp", "task", None)
    return jax.shard_map(
        shards,
        mesh=mesh,
        in_specs=(
            rows,
            flat,
            P(),
            P(),
            stacked,
            P(),
            P(),
            stacked,
            P(),
            P(),
            flat,
            pixel,
            pixel,
            rows,
            task_rows,
        ),
        out_specs=(
            rows,
            task_rows,
            rows,
            flat,
            P(),
            P(),
            stacked,
            P(),
            P(),
            stacked,
            P(),
            P(),
            flat,
        ),
        check_vma=False,
    )
```

```python
import math

import jax
import jax.numpy as jnp
from jax import lax
from jax.experimental import pallas as pl
from jax.experimental.pallas import tpu as pltpu
from jax.sharding import PartitionSpec as P

EPS = 1e-05
BF = jnp.bfloat16
F32 = jnp.float32
ROOT = math.sqrt(2.0 / math.pi)
CUBE = 0.044715
VMEM = pl.BlockSpec(memory_space=pltpu.VMEM)
TRUNK_GAIN, TRUNK_BIAS, HID_GAIN, HID_BIAS, ATTN_GAIN, ATTN_BIAS = (slice(k, k + 1) for k in range(6))


def swap(x, axis, step):
    count = lax.axis_size(axis)
    return lax.ppermute(x, axis, [(i, i ^ step) for i in range(count)])


def levels(axis):
    count = lax.axis_size(axis)
    assert count & (count - 1) == 0
    return count.bit_length() - 1


def slice_of(place):
    out = 0
    for bit in range(levels("task")):
        out = out * 2 + (place >> bit) % 2
    return out


def dp_steps():
    bits, low, out = levels("dp"), 1, []
    while low < bits:
        out.append([1 << low] + ([2 << low, 3 << low] if low + 1 < bits else []))
        low += 2
    return out + ([[1]] if bits else [])


def sum_dp(x, work=None):
    steps = dp_steps()
    for step in steps[:-1]:
        x = add_up(x, *[swap(x, "dp", s) for s in step])
    done = work() if work else None
    if work:
        x, done = together(x, done)
    for step in steps[-1:]:
        x = add_up(x, *[swap(x, "dp", s) for s in step])
    return (x, done) if work else x


def sum_dp_then(x, needs, work):
    steps = dp_steps()
    for step in steps[:-1]:
        x = add_up(x, *[swap(x, "dp", s) for s in step])
    x, needs = together(x, needs)
    got = swap(x, "dp", 1)
    got, done = together(got, work(needs))
    return add_up(x, got), done


def together(*xs):
    return lax.optimization_barrier(xs)


def others(x, axis):
    return [x] + [swap(x, axis, k) for k in range(1, lax.axis_size(axis))]


def in_blocks(rows):
    return rows % 16 == 0 and lax.axis_size("dp") <= 8


def gather_dp(x):
    if in_blocks(x.shape[0]):
        return others(x, "dp")
    return [lax.all_gather(x, "dp", axis=0, tiled=True)]


def scatter_dp(parts):
    count = lax.axis_size("dp")
    if len(parts) == 1:
        whole = parts[0].reshape((count, -1) + parts[0].shape[1:])
        return gathered_sum(lax.all_to_all(whole, "dp", 0, 0, tiled=True), BF)
    if len(parts) == 2 and count > 2:
        parts = add_cut(parts[0], swap(parts[1], "dp", 1), count // 2)
        return piece_sum([swap(p, "dp", 2 * k) if k else p for k, p in enumerate(parts)], BF)
    return piece_sum([swap(p, "dp", k) if k else p for k, p in enumerate(parts)], BF)


def first_hop(x):
    return swap(x, "task", 2)


def relay(x, hop=None):
    near = stack_two(x, first_hop(x) if hop is None else hop)
    return near, swap(near, "task", 1)


def trade(stay, cross, hop=None):
    got = first_hop(cross) if hop is None else hop
    return stay, got, swap(second_of(stay, got), "task", 1)


def kernel_call(name, body, grid, ins, in_specs, outs, out_specs, scratch=(), limit=32, flops=0):
    return pl.pallas_call(
        body,
        name=name,
        grid=grid,
        in_specs=in_specs,
        out_specs=out_specs,
        out_shape=[jax.ShapeDtypeStruct(s, d) for s, d in outs],
        scratch_shapes=list(scratch),
        compiler_params=pltpu.CompilerParams(vmem_limit_bytes=limit * 2**20),
        cost_estimate=pl.CostEstimate(
            flops=flops, bytes_accessed=sum(x.size * x.dtype.itemsize for x in ins), transcendentals=0
        ),
    )(*ins)


def views(refs):
    if len(refs) == 2:
        near, far = refs
        return [near.at[0], far.at[0], near.at[1], far.at[1]]
    stay, got, back = refs
    return [stay.at[0], back.at[0], got.at[0], back.at[1]]


def peer(k):
    return lax.axis_index("task") ^ k


def lanes_of(place, width):
    return ds(slice_of(place) * width, width, 128)


def halves(level, size, unit=16):
    bit = (lax.axis_index("task") >> level) % 2
    return ds(bit * size, size, unit), ds((1 - bit) * size, size, unit)


def ds(start, size, unit=16):
    if isinstance(start, int):
        return pl.ds(start, size)
    return pl.ds(pl.multiple_of(start, unit), size)


def dot(a, b):
    return jnp.dot(a, b, preferred_element_type=F32)


def dot_nt(a, b):
    return lax.dot_general(a, b, (((1,), (1,)), ((), ())), preferred_element_type=F32)


def dot_tn(a, b):
    return lax.dot_general(a, b, (((0,), (0,)), ((), ())), preferred_element_type=F32)


def gelu_parts(v):
    square = v * v
    t = jnp.tanh(ROOT * v * (1.0 + CUBE * square))
    return square, t


def gelu(v):
    _, t = gelu_parts(v)
    return 0.5 * v * (1.0 + t)


def gelu_slope(v):
    square, t = gelu_parts(v)
    return 0.5 * (1.0 + t) + (0.5 * ROOT) * v * (1.0 - t * t) * (1.0 + (3.0 * CUBE) * square)


def sigmoid(v):
    return 0.5 * (1.0 + jnp.tanh(0.5 * v))


def scales(first, second, count):
    mean = first / count
    return mean, lax.rsqrt(second / count - mean * mean + EPS)


def fold(v):
    return jnp.sum(v.reshape(-1, 8, v.shape[-1]), axis=0)


def sweep(rows, width, step, sums):
    block = 16

    def body(i, carry):
        values = step(ds(i * block, block))
        return tuple(c + fold(v) for c, v in zip(carry, values, strict=True))

    start = tuple(jnp.zeros((8, width), F32) for _ in range(sums))
    out = lax.fori_loop(0, rows // block, body, start, unroll=9)
    return [jnp.sum(c, axis=0, keepdims=True) for c in out]


def spread(ref, at, width):
    m = ref[at, :]
    return m if width == 128 else jnp.concatenate([m] * (width // 128), axis=1)


def each_block(rows, step):
    def body(i, carry):
        step(ds(i * 16, 16))
        return carry

    lax.fori_loop(0, rows // 16, body, 0, unroll=9)


def accumulate(ref, parts):
    total = jnp.concatenate(parts, axis=0)

    @pl.when(pl.program_id(0) == 0)
    def _():
        ref[...] = total

    @pl.when(pl.program_id(0) != 0)
    def _():
        ref[...] += total


def fill_wide(wide_ref, piece_refs, shape, reverse, change=None, place=peer, width=None):
    image_count, row_count, places, cols = shape
    rows = row_count * cols
    width = width or piece_refs[0].shape[-1]
    span = (row_count * places + 2) * cols
    zero = jnp.zeros((cols, wide_ref.shape[1]), BF)
    column = lax.broadcasted_iota(jnp.int32, (row_count, cols, width), 1).reshape(rows, width)
    for i in range(image_count):
        wide_ref[ds(i * span, cols), :] = zero
        wide_ref[ds((i + 1) * span - cols, cols), :] = zero
        for k, ref in enumerate(piece_refs):
            start = place(k) * rows
            x = ref[i, :, :width]
            if change is not None:
                x = change(x, ds(i * rows * places + start, rows))
            wide = x.astype(F32)
            left = jnp.where(column == 0, 0.0, pltpu.roll(wide, 1, 0)).astype(BF)
            right = jnp.where(column == cols - 1, 0.0, pltpu.roll(wide, rows - 1, 0)).astype(BF)
            if reverse:
                left, right = right, left
            at = ds(i * span + cols + start, rows)
            wide_ref[at, :width] = left
            wide_ref[at, width : 2 * width] = x.astype(BF)
            wide_ref[at, 2 * width :] = right


def turn_taps(turned_ref, kernel_ref, width):
    n = kernel_ref.shape[1]
    for tap in range(9):
        p, q = divmod(tap, 3)
        turned_ref[p, :, q * n : (q + 1) * n] = kernel_ref[tap * width : (tap + 1) * width, :]


def conv_rows(wide_ref, i, c, shape, product, reverse):
    row_count, places, cols = shape[1:]
    rows = row_count * cols
    start = i * (row_count * places + 2) * cols + c * rows
    total = None
    for p in range(3):
        at = (2 - p if reverse else p) * cols
        term = product(p, wide_ref[ds(start + at, rows), :])
        total = term if total is None else total + term
    return total


def add_up(*xs):
    def body(*refs):
        total = refs[0][...]
        for ref in refs[1:-1]:
            total = total + ref[...]
        refs[-1][...] = total

    return kernel_call(
        "add_up", body, (), list(xs), [VMEM] * len(xs), [(xs[0].shape, F32)], [VMEM], limit=2
    )[0]


def side_by_side(pieces):
    rows, width = pieces[0].shape[1:]

    def body(near_ref, far_ref, out_ref):
        for k, ref in enumerate(views((near_ref, far_ref))):
            out_ref[:, k * width : (k + 1) * width] = ref[...]

    return kernel_call(
        "side_by_side", body, (), list(pieces), [VMEM] * 2, [((rows, 4 * width), F32)], [VMEM], limit=2
    )[0]


def stack_two(a, b):
    def body(a_ref, b_ref, out_ref):
        out_ref[0] = a_ref[...]
        out_ref[1] = b_ref[...]

    return kernel_call(
        "stack_two", body, (), [a, b], [VMEM] * 2, [((2,) + a.shape, a.dtype)], [VMEM]
    )[0]


def second_of(a, b):
    def body(a_ref, b_ref, out_ref):
        out_ref[0] = a_ref[1]
        out_ref[1] = b_ref[1]

    return kernel_call("second_of", body, (), [a, b], [VMEM] * 2, [(a.shape, a.dtype)], [VMEM])[0]


def first_sums(stay, got):
    def body(stay_ref, got_ref, own_ref, one_ref):
        own_ref[...] = (stay_ref[0].astype(F32) + got_ref[0].astype(F32)).astype(BF)
        one_ref[...] = (stay_ref[1].astype(F32) + got_ref[1].astype(F32)).astype(BF)

    return kernel_call(
        "first_sums",
        body,
        (),
        [stay, got],
        [VMEM] * 2,
        [(stay.shape[1:], BF)] * 2,
        [VMEM] * 2,
    )


def pack_weights(w_trunk, w_hid, w_attn, w_shared, vectors, part, quarter, copies):
    rows, (depth, width) = w_trunk.shape[0], w_hid.shape[1:]
    tasks = w_hid.shape[0]
    block = w_shared.shape[1]
    cuts = width // block
    n = len(vectors)

    def body(trunk_ref, hid_ref, attn_ref, shared_ref, *refs):
        vector_refs = refs[:n]
        first_ref, second_ref, out_ref = refs[n:]
        me = lax.axis_index("task")
        task = jnp.minimum(me, tasks - 1)
        for k in range(copies):
            first_ref[k] = trunk_ref[:, lanes_of(me, part)]
        for c in range(cuts):
            here = slice(c * block, (c + 1) * block)
            second_ref[c * depth : (c + 1) * depth, :] = hid_ref[task, :, here]
            second_ref[(cuts + c) * depth : (cuts + c + 1) * depth, :] = attn_ref[task, :, here]
        if quarter:
            second_ref[2 * cuts * depth :, :] = shared_ref[ds(me * quarter, quarter), :]
        out_ref[...] = jnp.zeros_like(out_ref)
        for k, ref in enumerate(vector_refs):
            row = ref[...] if ref.shape[0] == 1 else ref[pl.ds(task, 1), :]
            out_ref[k : k + 1, :] = row

    ins = [w_trunk, w_hid, w_attn, w_shared, *vectors]
    return kernel_call(
        "pack_weights",
        body,
        (),
        ins,
        [VMEM] * len(ins),
        [
            ((copies, rows, part), BF),
            ((2 * cuts * depth + quarter, block), BF),
            ((8, width), F32),
        ],
        [VMEM] * 3,
        limit=56,
    )


def unpack_weights(gathered, depth, width, quarter):
    count, _, block = gathered.shape
    cuts = width // block

    def body(gathered_ref, layers_ref, *outs):
        for k in range(count):
            for c in range(2 * cuts):
                layers_ref[k * depth : (k + 1) * depth, c * block : (c + 1) * block] = gathered_ref[
                    k, c * depth : (c + 1) * depth, :
                ]
            if quarter:
                outs[0][k] = gathered_ref[k, 2 * cuts * depth :, :]

    outs = [((count * depth, 2 * width), BF)]
    if quarter:
        outs.append(((count, quarter, block), BF))
    return kernel_call(
        "unpack_weights", body, (), [gathered], [VMEM], outs, [VMEM] * len(outs), limit=44
    )


def gathered_sum(parts, dtype):
    shape = parts.shape[1:]

    def body(parts_ref, out_ref):
        total = parts_ref[0].astype(F32)
        for k in range(1, parts.shape[0]):
            total = total + parts_ref[k].astype(F32)
        out_ref[...] = total.astype(dtype)

    return kernel_call("gathered_sum", body, (), [parts], [VMEM], [(shape, dtype)], [VMEM])[0]


def piece_sum(pieces, dtype):
    def body(*refs):
        total = refs[0][...].astype(F32)
        for ref in refs[1:-1]:
            total = total + ref[...].astype(F32)
        refs[-1][...] = total.astype(dtype)

    return kernel_call(
        "piece_sum", body, (), list(pieces), [VMEM] * len(pieces), [(pieces[0].shape, dtype)], [VMEM]
    )[0]


def blocks_of(whole_ref, out_refs, rows):
    me = lax.axis_index("dp")
    if len(out_refs) == 1:
        out_refs[0][...] = whole_ref[...]
    elif len(out_refs) == 2:
        for k in range(whole_ref.shape[0] // rows):
            at = k // 2 * rows
            out_refs[k % 2][at : at + rows, :] = whole_ref[ds((me ^ k) * rows, rows), :]
    else:
        for k, ref in enumerate(out_refs):
            ref[...] = whole_ref[ds((me ^ k) * rows, rows), :]


def block_shapes(rows, width, pairs):
    count = lax.axis_size("dp")
    if not in_blocks(rows):
        return [((count * rows, width), BF)]
    if pairs:
        return [((count // 2 * rows, width), BF)] * 2
    return [((rows, width), BF)] * count


def add_cut(kept, got, count):
    rows, width = kept.shape[0] // count, kept.shape[1]

    def body(kept_ref, got_ref, *out_refs):
        for k, ref in enumerate(out_refs):
            at = slice(k * rows, (k + 1) * rows)
            ref[...] = (kept_ref[at, :].astype(F32) + got_ref[at, :].astype(F32)).astype(BF)

    return kernel_call(
        "add_cut", body, (), [kept, got], [VMEM] * 2, [((rows, width), BF)] * count, [VMEM] * count
    )


def sum_in_blocks(kept, got):
    rows, width = kept.shape[0] // lax.axis_size("dp"), kept.shape[1]
    outs = block_shapes(rows, width, True)

    def body(kept_ref, got_ref, *refs):
        refs[-1][...] = (kept_ref[...].astype(F32) + got_ref[...].astype(F32)).astype(BF)
        blocks_of(refs[-1], refs[:-1], rows)

    return kernel_call(
        "sum_in_blocks",
        body,
        (),
        [kept, got],
        [VMEM] * 2,
        outs,
        [VMEM] * len(outs),
        [pltpu.VMEM(kept.shape, BF)],
    )


def lanes_below(x, width):
    return [x[:, c * width : (c + 1) * width] for c in range(x.shape[1] // width)]


def merge_parts(shared_kept, shared_got, pairs):
    count = lax.axis_size("dp")
    each, width = shared_kept.shape[0] // count, shared_kept.shape[1]
    mid = pairs[0][0].shape[1]
    rows, cuts = mid // count, mid // width
    total = each + len(pairs) * cuts * rows
    n = 2 * len(pairs)

    def body(kept_ref, got_ref, *refs):
        sum_ref, product_ref = refs[-2:]
        out_refs = refs[n : n + 2]
        me = lax.axis_index("dp")
        sum_ref[...] = (kept_ref[...].astype(F32) + got_ref[...].astype(F32)).astype(BF)
        for k in range(count):
            at = k // 2 * total
            out_refs[k % 2][at : at + each, :] = sum_ref[ds((me ^ k) * each, each), :]
        for p in range(len(pairs)):
            product_ref[...] = dot_tn(refs[2 * p][...], refs[2 * p + 1][...]).astype(BF)
            for k in range(count):
                block = product_ref[ds((me ^ k) * rows, rows), :]
                for c in range(cuts):
                    at = k // 2 * total + each + (p * cuts + c) * rows
                    out_refs[k % 2][at : at + rows, :] = block[:, c * width : (c + 1) * width]

    ins = [shared_kept, shared_got, *(x for pair in pairs for x in pair)]
    return kernel_call(
        "merge_parts",
        body,
        (),
        ins,
        [VMEM] * len(ins),
        [((count // 2 * total, width), BF)] * 2,
        [VMEM] * 2,
        [pltpu.VMEM(shared_kept.shape, BF), pltpu.VMEM((mid, mid), BF)],
        flops=2 * pairs[0][0].size * mid * len(pairs),
    )


def product_parts(left, right, width):
    count = lax.axis_size("dp")
    mid = left.shape[1]
    rows, cuts = mid // count, mid // width

    def body(left_ref, right_ref, even_ref, odd_ref, product_ref):
        me = lax.axis_index("dp")
        product_ref[...] = dot_tn(left_ref[...], right_ref[...]).astype(BF)
        for k in range(count):
            block = product_ref[ds((me ^ k) * rows, rows), :]
            for c in range(cuts):
                at = (k // 2 * cuts + c) * rows
                (even_ref, odd_ref)[k % 2][at : at + rows, :] = block[:, c * width : (c + 1) * width]

    return kernel_call(
        "product_parts",
        body,
        (),
        [left, right],
        [VMEM] * 2,
        [((count // 2 * cuts * rows, width), BF)] * 2,
        [VMEM] * 2,
        [pltpu.VMEM((mid, mid), BF)],
        flops=2 * left.size * mid,
    )


def sum_both(first, second):
    rows, n = first[0].shape[0], len(first)
    shape = (rows + second[0].shape[0], first[0].shape[1])

    def body(*refs):
        for at, part in ((slice(0, rows), refs[:n]), (slice(rows, shape[0]), refs[n:-1])):
            total = part[0][...].astype(F32)
            for ref in part[1:]:
                total = total + ref[...].astype(F32)
            refs[-1][at, :] = total.astype(BF)

    ins = [*first, *second]
    return kernel_call("sum_both", body, (), ins, [VMEM] * len(ins), [(shape, BF)], [VMEM])[0]


def split_parts(pieces, shared_rows, layer_shape, tasks):
    rows, columns = layer_shape
    width = pieces[0].shape[2]

    def body(near_ref, far_ref, shared_ref, *layer_refs):
        for k, ref in enumerate(views((near_ref, far_ref))):
            place = peer(k)
            lanes = ds(place % 2 * width, width, 128)
            at = ds(place // 2 * shared_rows, shared_rows)
            shared_ref[at, lanes] = ref[:shared_rows, :].astype(F32)

            @pl.when(place < tasks)
            def _(ref=ref, place=place):
                start = shared_rows
                for layer_ref in layer_refs:
                    for c in range(columns // width):
                        value = ref[start : start + rows, :].astype(F32)
                        layer_ref[place, :, c * width : (c + 1) * width] = value
                        start += rows

    return kernel_call(
        "split_parts",
        body,
        (),
        list(pieces),
        [VMEM] * 2,
        [((shared_rows * 2, 2 * width), F32)] + [((tasks, rows, columns), F32)] * 2,
        [VMEM] * 3,
    )


def by_task(pieces, tasks, dtype):
    shape = pieces[0].shape[1:]
    n = len(pieces)

    def body(*refs):
        for k, ref in enumerate(views(refs[:n])):
            place = peer(k)

            @pl.when(place < tasks)
            def _(ref=ref, place=place):
                refs[n][place] = ref[...].astype(dtype)

    return kernel_call(
        "by_task", body, (), list(pieces), [VMEM] * n, [((tasks,) + shape, dtype)], [VMEM]
    )[0]


def trunk_total(parts, gate_sums, hid_sums, trunk_sums):
    rows, part = parts[0].shape
    width = gate_sums.shape[1]
    n = len(parts)

    def body(*refs):
        gate_ref, hid_ref, trunk_ref, out_ref = refs[n:]
        total = refs[0][...].astype(F32)
        for ref in refs[1:n]:
            total = total + ref[...].astype(F32)
        out_ref[:rows, :] = total
        out_ref[rows:, :] = jnp.zeros((out_ref.shape[0] - rows, part), F32)
        for c in range(width // part):
            here = slice(c * part, (c + 1) * part)
            at = rows + 8 * c
            out_ref[at : at + 2, :] = gate_ref[:, here]
            out_ref[at + 2 : at + 4, :] = hid_ref[:, here]
        out_ref[rows + 4 : rows + 6, :] = trunk_ref[...]

    ins = [*parts, gate_sums, hid_sums, trunk_sums]
    shape = (rows + 8 * (width // part), part)
    return kernel_call(
        "trunk_total", body, (), ins, [VMEM] * len(ins), [(shape, F32)], [VMEM]
    )[0]


def split_trunk(pieces, rows, tasks):
    part = pieces[0].shape[2]
    width = 4 * part

    def body(near_ref, far_ref, weight_ref, *refs):
        outs, trunk_ref = refs[:4], refs[4]
        for k, piece in enumerate(views((near_ref, far_ref))):
            place = peer(k)
            lanes = lanes_of(place, part)
            weight_ref[:, lanes] = piece[:rows, :]
            trunk_ref[:, lanes] = piece[rows + 4 : rows + 6, :]

            @pl.when(place < tasks)
            def _(piece=piece, place=place):
                for r, ref in enumerate(outs):
                    at = [rows + 8 * c + r for c in range(4)]
                    row = jnp.concatenate([piece[i : i + 1, :] for i in at], axis=1)
                    ref[pl.ds(place, 1), :] = row

    return kernel_call(
        "split_trunk",
        body,
        (),
        list(pieces),
        [VMEM] * 2,
        [((rows, width), F32)] + [((tasks, width), F32)] * 4 + [((2, width), F32)],
        [VMEM] * 6,
    )


def lay_out(order, pieces, dtype, along, count=None):
    n = len(pieces)
    shape = list(pieces[0].shape)
    if along == 0 and shape[0] % 16:
        out = jnp.zeros([shape[0] * n] + shape[1:], dtype)
        for k, piece in enumerate(pieces):
            out = lax.dynamic_update_slice_in_dim(out, piece.astype(dtype), order(k) * shape[0], axis=0)
        return out
    if along is None:
        whole = [count or n] + shape
    else:
        whole = list(shape)
        whole[along] *= n

    def body(*refs):
        for k in range(n):
            value = refs[k][...].astype(dtype)
            if along is None:

                @pl.when(order(k) < whole[0])
                def _(k=k, value=value):
                    refs[-1][order(k)] = value

            elif along == 0:
                refs[-1][ds(order(k) * shape[0], shape[0]), :] = value
            else:
                refs[-1][:, ds(order(k) * shape[1], shape[1], 128)] = value

    return kernel_call(
        "lay_out", body, (), list(pieces), [VMEM] * n, [(tuple(whole), dtype)], [VMEM]
    )[0]


def pack_cots(task_cot, trunk_cot, places):
    tasks, image_count, rows, out_width = task_cot.shape
    part = trunk_cot.shape[-1] // places

    def body(task_ref, trunk_ref, stay_ref, cross_ref):
        for k in range(places):
            ref = (stay_ref, cross_ref)[k // 2].at[k % 2]
            ref[:, :, :out_width] = task_ref[jnp.minimum(peer(k), tasks - 1)]
            ref[:, :, out_width:] = trunk_ref[:, :, lanes_of(peer(k), part)]

    return kernel_call(
        "pack_cots",
        body,
        (),
        [task_cot, trunk_cot],
        [VMEM, VMEM],
        [((2, image_count, rows, out_width + part), BF)] * 2,
        [VMEM] * 2,
    )


def trunk_forward(labelled, counts, images, shards, shape):
    image_count, row_count, places, cols = shape
    rows = row_count * cols
    count, each, part = shards.shape
    depth = count * each
    pixels = image_count * places * rows
    in_width = images.shape[-1]

    def body(mask_ref, counts_ref, images_ref, shards_ref, centred_ref, stats_ref, kernel_ref, wide_ref, pre_ref):
        for k in range(count):
            kernel_ref[k * each : (k + 1) * each, :] = shards_ref[k]
        pieces = [images_ref.at[:, k] for k in range(places)]
        fill_wide(wide_ref, pieces, shape, False, place=lambda k: k)
        block = 3 * in_width

        def chunk(c, carry):
            for i in range(image_count):
                value = conv_rows(
                    wide_ref,
                    i,
                    c,
                    shape,
                    lambda p, x: dot(x, kernel_ref[p * block : (p + 1) * block, :]),
                    False,
                )
                pre_ref[ds((i * places + c) * rows, rows), :] = value
            return carry

        lax.fori_loop(0, places, chunk, 0)

        def moments(at):
            v = pre_ref[at, :]
            mv = mask_ref[at, :] * v
            return mv, mv * v, v

        sums = sweep(pixels, part, moments, 3)
        mean = sums[2] / pixels
        stats_ref[...] = jnp.concatenate(sums[:2] + [counts_ref[...]] + [mean] * 4, axis=0)

        def centre(at):
            centred_ref[at, :] = (pre_ref[at, :] - mean).astype(BF)

        each_block(pixels, centre)

    return kernel_call(
        "trunk_forward",
        body,
        (),
        [labelled, counts, images, shards],
        [VMEM] * 4,
        [((pixels, part), BF), ((8, part), F32)],
        [VMEM] * 2,
        [
            pltpu.VMEM((depth, part), BF),
            pltpu.VMEM((image_count * (row_count * places + 2) * cols, 3 * in_width), BF),
            pltpu.VMEM((pixels, part), F32),
        ],
        flops=2 * pixels * depth * part,
    )


def rows_spec(rows, width):
    return pl.BlockSpec((rows, width), lambda i: (i, 0))


def fixed_spec(shape):
    return pl.BlockSpec(shape, lambda i: (0,) * len(shape))


def centre_on_first(value_ref, centre_ref, centred_ref):
    @pl.when(pl.program_id(0) == 0)
    def _():
        rows = value_ref.shape[0]
        (total,) = sweep(rows, value_ref.shape[1], lambda at: (value_ref[at, :],), 1)
        centre_ref[...] = total / rows

    centre = centre_ref[...]

    def step(at):
        centred_ref[at, :] = (value_ref[at, :] - centre).astype(BF)

    each_block(value_ref.shape[0], step)


def feat_hid(scaled, stats, totals, vectors, mask, kernel, rows, image_count):
    pixels, part = scaled[0].shape[1:]
    n = 2 * len(scaled)
    mid = part * n
    out_mid = mid

    def body(*refs):
        scaled_refs = views(refs[:2])
        stats_ref, totals_ref, vectors_ref, mask_ref, kernel_ref = refs[2:7]
        feat_ref, centred_ref, centre_ref, sums_ref, own_ref, affine_ref, hid_ref = refs[7:]

        @pl.when(pl.program_id(0) == 0)
        def _():
            count = jnp.maximum(totals_ref[2:3, :], 1.0)
            mean, rstd = scales(totals_ref[0:1, :], totals_ref[1:2, :], count)
            for k in range(n):
                here = slice(k * part, (k + 1) * part)
                at = lanes_of(peer(k), part)
                slope = rstd[:, here] * vectors_ref[TRUNK_GAIN, at]
                affine_ref[0:1, here] = slope
                affine_ref[1:2, here] = (stats_ref[4:5, here] - mean[:, here]) * slope + vectors_ref[TRUNK_BIAS, at]

        def activate(at):
            for k in range(n):
                here = slice(k * part, (k + 1) * part)
                v = scaled_refs[k][at, :].astype(F32) * affine_ref[0:1, here] + affine_ref[1:2, here]
                feat_ref[at, lanes_of(peer(k), part)] = gelu(v).astype(BF)

        each_block(rows, activate)
        hid_ref[...] = dot(feat_ref[...], kernel_ref[...])

        own_rows = own_ref.shape[1]
        each = rows // own_rows

        @pl.when(pl.program_id(0) % (n // each) == peer(0) // each)
        def _():
            at = ds(peer(0) % each * own_rows, own_rows)
            own_ref[pl.program_id(0) // (n // each)] = feat_ref[at, :]

        def moments(at):
            v = hid_ref[at, :]
            mv = spread(mask_ref, at, out_mid) * v
            return mv, mv * v

        accumulate(sums_ref, sweep(rows, out_mid, moments, 2))
        centre_on_first(hid_ref, centre_ref, centred_ref)

    return kernel_call(
        "feat_hid",
        body,
        (pixels // rows,),
        [*scaled, stats, totals, vectors, mask, kernel],
        [pl.BlockSpec((2, rows, part), lambda i: (0, i, 0))] * 2
        + [fixed_spec(x.shape) for x in (stats, totals, vectors)]
        + [rows_spec(rows, 128), pl.BlockSpec((mid, out_mid), lambda i: (0, 0))],
        [
            ((pixels, mid), BF),
            ((pixels, out_mid), BF),
            ((1, out_mid), F32),
            ((2, out_mid), F32),
            ((image_count, pixels // image_count // n, mid), BF),
        ],
        [
            rows_spec(rows, mid),
            rows_spec(rows, out_mid),
            fixed_spec((1, out_mid)),
            fixed_spec((2, out_mid)),
            fixed_spec((image_count, pixels // image_count // n, mid)),
        ],
        [pltpu.VMEM((2, mid), F32), pltpu.VMEM((rows, out_mid), F32)],
        flops=2 * pixels * mid * out_mid,
    )


def task_count(totals_ref):
    chosen = jnp.where(lax.axis_index("task") == 0, totals_ref[2:3, 0:1], totals_ref[3:4, 0:1])
    return jnp.maximum(chosen, 1.0)


def normed_rows(sums, count, centre):
    mean, rstd = scales(sums[0:1, :], sums[1:2, :], count)
    return rstd, (centre - mean) * rstd


def hid_gate(hid, centre, sums, totals, vectors, mask, kernel, rows):
    pixels, mid = hid.shape

    def body(*refs):
        hid_ref, middle_ref, sums_ref, totals_ref, vectors_ref, mask_ref, kernel_ref = refs[:7]
        hidden_ref, centred_ref, centre_ref, out_ref, gate_ref = refs[7:]
        count = task_count(totals_ref)
        gain, bias = vectors_ref[HID_GAIN, :], vectors_ref[HID_BIAS, :]
        scale, shift = normed_rows(sums_ref[...], count, middle_ref[...])
        scale, shift = scale * gain, shift * gain + bias

        def activate(at):
            hidden_ref[at, :] = gelu(hid_ref[at, :].astype(F32) * scale + shift).astype(BF)

        each_block(rows, activate)
        gate_ref[...] = dot(hidden_ref[...], kernel_ref[...])

        def moments(at):
            v = gate_ref[at, :]
            mv = spread(mask_ref, at, mid) * v
            return mv, mv * v

        accumulate(out_ref, sweep(rows, mid, moments, 2))
        centre_on_first(gate_ref, centre_ref, centred_ref)

    wide = rows_spec(rows, mid)
    return kernel_call(
        "hid_gate",
        body,
        (pixels // rows,),
        [hid, centre, sums, totals, vectors, mask, kernel],
        [wide]
        + [fixed_spec(x.shape) for x in (centre, sums, totals, vectors)]
        + [rows_spec(rows, 128), pl.BlockSpec((mid, mid), lambda i: (0, 1))],
        [((pixels, mid), BF), ((pixels, mid), BF), ((1, mid), F32), ((2, mid), F32)],
        [wide, wide, fixed_spec((1, mid)), fixed_spec((2, mid))],
        [pltpu.VMEM((rows, mid), F32)],
        flops=2 * pixels * mid * mid,
    )


def feature_back(cot, mask, kernels, shape, out_width):
    image_count, row_count, places, cols = shape
    rows = row_count * cols
    mid = sum(x.size for x in kernels) // out_width // 9
    pixels = image_count * places * rows
    n, m = len(cot), len(kernels)
    count = 2 * m if m > 1 else 1

    def body(*refs):
        cot_refs = views(refs[:n])
        mask_ref = refs[n]
        quarter_refs = refs[1 + n : 1 + n + m]
        if m > 1:
            quarter_refs = views(quarter_refs)
        out_ref, kernel_ref, wide_ref, turned_ref = refs[1 + n + m :]
        blocks, quarter = quarter_refs[0].shape[:2]
        for k, ref in enumerate(quarter_refs):
            for j in range(blocks):
                kernel_ref[ds((j * count + (peer(k) if m > 1 else 0)) * quarter, quarter), :] = ref[j]
        turn_taps(turned_ref, kernel_ref, mid)
        fill_wide(
            wide_ref,
            cot_refs,
            shape,
            True,
            lambda x, at: x.astype(F32) * spread(mask_ref, at, out_width),
            width=out_width,
        )

        def chunk(c, carry):
            for i in range(image_count):
                value = conv_rows(
                    wide_ref, i, c, shape, lambda p, x: dot_nt(x, turned_ref[p]), True
                )
                out_ref[ds((i * places + c) * rows, rows), :] = value.astype(BF)
            return carry

        lax.fori_loop(0, places, chunk, 0)

    return kernel_call(
        "feature_back",
        body,
        (),
        [*cot, mask, *kernels],
        [VMEM] * (n + 1 + m),
        [((pixels, mid), BF), ((9 * mid, out_width), BF)],
        [VMEM] * 2,
        [
            pltpu.VMEM((image_count * (row_count * places + 2) * cols, 3 * out_width), BF),
            pltpu.VMEM((3, mid, 3 * out_width), BF),
        ],
        limit=24,
        flops=2 * pixels * 9 * mid * out_width,
    )


def gate_back(gate, centre, sums, totals, vectors, feature_grad, feat, rows):
    pixels, mid = gate.shape

    def body(gate_ref, centre_ref, sums_ref, totals_ref, vectors_ref, grad_ref, feat_ref, *outs):
        features_ref, gate_grad_ref, share_ref, out_ref = outs
        scale, shift = normed_rows(sums_ref[...], task_count(totals_ref), centre_ref[...])
        slope = 0.5 * vectors_ref[ATTN_GAIN, :]
        offset = 0.5 * vectors_ref[ATTN_BIAS, :]

        def step(at):
            normed = gate_ref[at, :].astype(F32) * scale + shift
            t = jnp.tanh(normed * slope + offset)
            attention = 0.5 + 0.5 * t
            features = attention * feat_ref[at, :].astype(F32)
            features_ref[at, :] = features.astype(BF)
            grad = grad_ref[at, :].astype(F32)
            share_ref[at, :] = (grad * attention).astype(BF)
            gate_grad = grad * features * (0.5 - 0.5 * t)
            gate_grad_ref[at, :] = gate_grad.astype(BF)
            return gate_grad, gate_grad * normed

        accumulate(out_ref, sweep(rows, mid, step, 2))

    wide = rows_spec(rows, mid)
    return kernel_call(
        "gate_back",
        body,
        (pixels // rows,),
        [gate, centre, sums, totals, vectors, feature_grad, feat],
        [wide] + [fixed_spec(x.shape) for x in (centre, sums, totals, vectors)] + [wide, wide],
        [((pixels, mid), BF)] * 3 + [((2, mid), F32)],
        [wide] * 3 + [fixed_spec((2, mid))],
    )


def back_rows(gain, sums, count, centre, back):
    rstd, shift = normed_rows(sums, count, centre)
    scale = gain * rstd
    tilt = scale * back[1:2, :] / count
    return scale, scale * back[0:1, :] / count + tilt * shift, tilt * rstd


def hid_back(grad, gate, mask, centre, sums, totals, vectors, back, hid, h_centre, h_sums, kernel, rows):
    pixels, mid = grad.shape

    def body(*refs):
        grad_ref, gate_ref, mask_ref, centre_ref, sums_ref, totals_ref, vectors_ref, back_ref = refs[:8]
        hid_ref, h_centre_ref, h_sums_ref, kernel_ref = refs[8:12]
        pre_ref, act_ref, out_ref, value_ref = refs[12:]
        count = task_count(totals_ref)
        h_gain, h_bias = vectors_ref[HID_GAIN, :], vectors_ref[HID_BIAS, :]
        scale, lean, tilt = back_rows(
            vectors_ref[ATTN_GAIN, :], sums_ref[...], count, centre_ref[...], back_ref[...]
        )

        def step(at):
            lost = spread(mask_ref, at, mid) * (lean + gate_ref[at, :].astype(F32) * tilt)
            pre_ref[at, :] = (grad_ref[at, :].astype(F32) * scale - lost).astype(BF)

        each_block(rows, step)
        value_ref[...] = dot_nt(pre_ref[...], kernel_ref[...])
        h_scale, h_shift = normed_rows(h_sums_ref[...], count, h_centre_ref[...])

        def slope(at):
            x = hid_ref[at, :].astype(F32) * h_scale + h_shift
            value = value_ref[at, :] * gelu_slope(x * h_gain + h_bias)
            act_ref[at, :] = value.astype(BF)
            return value, value * x

        accumulate(out_ref, sweep(rows, mid, slope, 2))

    wide = rows_spec(rows, mid)
    return kernel_call(
        "hid_back",
        body,
        (pixels // rows,),
        [grad, gate, mask, centre, sums, totals, vectors, back, hid, h_centre, h_sums, kernel],
        [wide, wide, rows_spec(rows, 128)]
        + [fixed_spec(x.shape) for x in (centre, sums, totals, vectors, back)]
        + [wide]
        + [fixed_spec(x.shape) for x in (h_centre, h_sums)]
        + [pl.BlockSpec((mid, mid), lambda i: (0, 1))],
        [((pixels, mid), BF), ((pixels, mid), BF), ((2, mid), F32)],
        [wide, wide, fixed_spec((2, mid))],
        [pltpu.VMEM((rows, mid), F32)],
        flops=2 * pixels * mid * mid,
    )


def feat_back(act_grad, hid, mask, centre, sums, totals, vectors, back, share, kernel, rows, tasks):
    pixels, mid = act_grad.shape
    half = mid // 2

    def body(*refs):
        act_ref, hid_ref, mask_ref, centre_ref, sums_ref, totals_ref = refs[:6]
        vectors_ref, back_ref, share_ref, kernel_ref, pre_ref, kept_ref, sent_ref, part_ref = refs[6:]
        active = jnp.where(lax.axis_index("task") < tasks, 1.0, 0.0)
        scale, lean, tilt = back_rows(
            vectors_ref[HID_GAIN, :],
            sums_ref[...],
            task_count(totals_ref),
            centre_ref[...],
            back_ref[...],
        )

        def step(at):
            lost = spread(mask_ref, at, mid) * (lean + hid_ref[at, :].astype(F32) * tilt)
            pre_ref[at, :] = (act_ref[at, :].astype(F32) * scale - lost).astype(BF)

        each_block(rows, step)
        part_ref[...] = dot_nt(pre_ref[...], kernel_ref[...])

        def add(at):
            for ref, here in zip((kept_ref, sent_ref), halves(0, half, 128), strict=True):
                value = part_ref[at, here] + share_ref[at, here].astype(F32)
                ref[at, :] = (value * active).astype(BF)

        each_block(rows, add)

    wide = rows_spec(rows, mid)
    return kernel_call(
        "feat_back",
        body,
        (pixels // rows,),
        [act_grad, hid, mask, centre, sums, totals, vectors, back, share, kernel],
        [wide, wide, rows_spec(rows, 128)]
        + [fixed_spec(x.shape) for x in (centre, sums, totals, vectors, back)]
        + [wide]
        + [pl.BlockSpec((mid, mid), lambda i: (0, 0))],
        [((pixels, mid), BF), ((pixels, half), BF), ((pixels, half), BF)],
        [wide, rows_spec(rows, half), rows_spec(rows, half)],
        [pltpu.VMEM((rows, mid), F32)],
        flops=2 * pixels * mid * mid,
    )


def add_halve(level, kept, got, rows):
    pixels, width = kept.shape
    half = width // 2

    def body(kept_ref, got_ref, a_ref, b_ref):
        for ref, here in zip((a_ref, b_ref), halves(level, half, 128), strict=True):
            ref[...] = (kept_ref[:, here].astype(F32) + got_ref[:, here].astype(F32)).astype(BF)

    wide, slim = rows_spec(rows, width), rows_spec(rows, half)
    return kernel_call(
        "add_halve",
        body,
        (pixels // rows,),
        [kept, got],
        [wide, wide],
        [((pixels, half), BF)] * 2,
        [slim, slim],
    )


def trunk_back(parts, cots, trunk, stats, totals, vectors, shape):
    image_count, row_count, places, cols = shape
    rows = row_count * cols
    pixels, width = trunk.shape
    first = cots[0].shape[-1] - width
    n, m = len(parts), len(cots)

    def body(*refs):
        part_refs = refs[:n]
        cot_refs = views(refs[n : n + m])
        trunk_ref, stats_ref, totals_ref, vectors_ref, grad_ref, out_ref = refs[n + m :]
        lanes = lanes_of(peer(0), width)
        gain, bias = vectors_ref[TRUNK_GAIN, lanes], vectors_ref[TRUNK_BIAS, lanes]
        totals = totals_ref[:, :width]
        count = jnp.maximum(totals[2:3, :], 1.0)
        scale, shift = normed_rows(totals, count, stats_ref[4:5, :])
        total = [0.0, 0.0]
        for i in range(image_count):
            for k, cot_ref in enumerate(cot_refs):
                start = (i * places + peer(k)) * rows

                def step(at, start=start, cot_ref=cot_ref, i=i):
                    here = ds(start + at.start, at.size)
                    x = trunk_ref[here, :].astype(F32) * scale + shift
                    grad = cot_ref[i, at, first:].astype(F32)
                    for ref in part_refs:
                        grad = grad + ref[here, :].astype(F32)
                    grad = grad * gelu_slope(x * gain + bias)
                    grad_ref[here, :] = grad.astype(BF)
                    return grad, grad * x

                found = sweep(rows, width, step, 2)
                total = [a + b for a, b in zip(total, found, strict=True)]
        out_ref[...] = jnp.concatenate(total, axis=0)

    return kernel_call(
        "trunk_back",
        body,
        (),
        [*parts, *cots, trunk, stats, totals, vectors],
        [VMEM] * (n + m + 4),
        [((pixels, width), BF), ((2, width), F32)],
        [VMEM] * 2,
    )


def trunk_weights(images, grad, trunk, mask, stats, totals, vectors, back, shape):
    image_count, row_count, places, cols = shape
    rows = row_count * cols
    in_width = images.shape[-1]
    pixels, part = grad.shape
    depth = 9 * in_width // lax.axis_size("dp")
    outs = block_shapes(depth, part, True)
    span = (row_count * places + 2) * cols
    whole = row_count * places * cols

    def body(*refs):
        images_ref, grad_ref, trunk_ref, mask_ref, stats_ref, totals_ref, vectors_ref, back_ref = refs[:8]
        out_ref = refs[8]
        weight_ref, wide_ref = refs[-2:]
        totals = totals_ref[:, :part]
        count = jnp.maximum(totals[2:3, :], 1.0)
        scale, lean, tilt = back_rows(
            vectors_ref[TRUNK_GAIN, lanes_of(peer(0), part)], totals, count, stats_ref[4:5, :], back_ref[...]
        )

        def step(at):
            lost = mask_ref[at, :] * (lean + trunk_ref[at, :].astype(F32) * tilt)
            out_ref[at, :] = (grad_ref[at, :].astype(F32) * scale - lost).astype(BF)

        each_block(pixels, step)
        fill_wide(
            wide_ref,
            [images_ref.at[:, k] for k in range(places)],
            shape,
            False,
            place=lambda k: k,
        )
        for p in range(3):
            total = None
            for i in range(image_count):
                term = dot_tn(
                    wide_ref[ds(i * span + p * cols, whole), :], out_ref[ds(i * whole, whole), :]
                )
                total = term if total is None else total + term
            weight_ref[p * 3 * in_width : (p + 1) * 3 * in_width, :] = total.astype(BF)
        blocks_of(weight_ref, refs[9:-2], depth)

    return kernel_call(
        "trunk_weights",
        body,
        (),
        [images, grad, trunk, mask, stats, totals, vectors, back],
        [VMEM] * 8,
        [((pixels, part), BF), *outs],
        [VMEM] * (1 + len(outs)),
        [
            pltpu.VMEM((9 * in_width, part), BF),
            pltpu.VMEM((image_count * span, 3 * in_width), BF),
        ],
        flops=2 * pixels * 9 * in_width * part,
    )


def image_back(grad, shards, shape):
    image_count, row_count, places, cols = shape
    rows = row_count * cols
    part = grad.shape[-1]
    count, each = shards.shape[:2]
    in_width = count * each // 9

    def body(grad_ref, shards_ref, *refs):
        out_refs = [refs[k // 2].at[k % 2] for k in range(places)]
        kernel_ref, wide_ref, turned_ref = refs[2:]
        for k in range(count):
            kernel_ref[k * each : (k + 1) * each, :] = shards_ref[k]
        turn_taps(turned_ref, kernel_ref, in_width)
        pieces = [grad_ref.at[:, k] for k in range(places)]
        fill_wide(wide_ref, pieces, shape, True, place=lambda k: k)
        for k, ref in enumerate(out_refs):
            for i in range(image_count):
                value = conv_rows(
                    wide_ref, i, peer(k), shape, lambda p, x: dot_nt(x, turned_ref[p]), True
                )
                ref[i] = value.astype(BF)

    return kernel_call(
        "image_back",
        body,
        (),
        [grad.reshape(image_count, places, rows, part), shards],
        [VMEM, VMEM],
        [((2, image_count, rows, in_width), BF)] * 2,
        [VMEM] * 2,
        [
            pltpu.VMEM((count * each, part), BF),
            pltpu.VMEM((image_count * (row_count * places + 2) * cols, 3 * part), BF),
            pltpu.VMEM((3, in_width, 3 * part), BF),
        ],
        flops=2 * grad.size * 9 * in_width,
    )


def task_forward(features, kernel, shape):
    image_count, row_count, places, cols = shape
    rows = row_count * cols
    mid = features.shape[-1]
    out_width = kernel.shape[1]
    block = 3 * mid

    def body(features_ref, kernel_ref, *refs):
        out_refs = [refs[k // 2].at[k % 2] for k in range(places)]
        (wide_ref,) = refs[2:]
        pieces = [features_ref.at[:, k] for k in range(places)]
        fill_wide(wide_ref, pieces, shape, False, place=lambda k: k)
        for k, ref in enumerate(out_refs):
            for i in range(image_count):
                value = conv_rows(
                    wide_ref,
                    i,
                    peer(k),
                    shape,
                    lambda p, x: dot(x, kernel_ref[p * block : (p + 1) * block, :]),
                    False,
                )
                ref[i] = value.astype(BF)

    return kernel_call(
        "task_forward",
        body,
        (),
        [features.reshape(image_count, places, rows, mid), kernel],
        [VMEM, VMEM],
        [((2, image_count, rows, out_width), BF)] * 2,
        [VMEM] * 2,
        [
            pltpu.VMEM((image_count * (row_count * places + 2) * cols, 3 * mid), BF),
        ],
        limit=24,
        flops=2 * features.size * 9 * out_width,
    )


def add_split(level, kept, got, blocks):
    rows, width = kept.shape
    half = rows // blocks // 2

    def body(kept_ref, got_ref, a_ref, b_ref):
        bit = (lax.axis_index("task") >> level) % 2
        for ref, which in ((a_ref, bit), (b_ref, 1 - bit)):
            for j in range(blocks):
                at = ds((2 * j + which) * half, half)
                value = kept_ref[at, :].astype(F32) + got_ref[at, :].astype(F32)
                ref[j] = value.astype(BF)

    return kernel_call(
        "add_split",
        body,
        (),
        [kept, got],
        [VMEM, VMEM],
        [((blocks, half, width), BF)] * 2,
        [VMEM] * 2,
    )


def layer_weights(pairs):
    mid = pairs[0][0].shape[1]
    rows = mid // lax.axis_size("dp")
    outs = block_shapes(rows, mid * len(pairs), True)
    n = 2 * len(pairs)

    def body(*refs):
        for k in range(len(pairs)):
            value = dot_tn(refs[2 * k][...], refs[2 * k + 1][...])
            refs[-1][:, k * mid : (k + 1) * mid] = value.astype(BF)
        blocks_of(refs[-1], refs[n:-1], rows)

    ins = [x for pair in pairs for x in pair]
    return kernel_call(
        "layer_weights",
        body,
        (),
        ins,
        [VMEM] * n,
        outs,
        [VMEM] * len(outs),
        [pltpu.VMEM((mid, mid * len(pairs)), BF)],
        flops=2 * pairs[0][0].size * mid * len(pairs),
    )


def shared_weights(cot, mask, features, shape, tasks, out_width):
    image_count, row_count, places, cols = shape
    rows = row_count * cols
    mid = features.shape[-1]
    n = len(cot)
    half = out_width // 2
    span = (row_count * places + 2) * cols
    whole = row_count * places * cols

    def body(*refs):
        cot_refs = views(refs[:n])
        mask_ref, features_ref, kept_ref, sent_ref, wide_ref, part_ref = refs[n:]
        active = jnp.where(lax.axis_index("task") < tasks, 1.0, 0.0)
        fill_wide(
            wide_ref,
            cot_refs,
            shape,
            True,
            lambda x, at: x.astype(F32) * spread(mask_ref, at, out_width) * active,
            width=out_width,
        )
        for tap in range(9):
            p, q = divmod(tap, 3)
            total = None
            for i in range(image_count):
                term = dot_tn(
                    features_ref[ds(i * whole, whole), :],
                    wide_ref[
                        ds(i * span + (2 - p) * cols, whole), q * out_width : (q + 1) * out_width
                    ],
                )
                total = term if total is None else total + term
            part_ref[...] = total
            for ref, here in zip((kept_ref, sent_ref), halves(0, half, 128), strict=True):
                ref[tap * mid : (tap + 1) * mid, :] = part_ref[:, here].astype(BF)

    return kernel_call(
        "shared_weights",
        body,
        (),
        [*cot, mask, features],
        [VMEM] * (n + 2),
        [((9 * mid, half), BF)] * 2,
        [VMEM, VMEM],
        [
            pltpu.VMEM((image_count * span, 3 * out_width), BF),
            pltpu.VMEM((mid, out_width), F32),
        ],
        flops=2 * features.size * 9 * out_width,
    )


def shards(
    images,
    w_trunk,
    trunk_gain,
    trunk_bias,
    w_hid,
    hid_gain,
    hid_bias,
    w_attn,
    attn_gain,
    attn_bias,
    w_shared,
    labels,
    depth_valid,
    trunk_cot,
    task_cot,
):
    image_count, row_count, cols, in_width = images.shape
    mid = w_trunk.shape[1]
    out_width = w_shared.shape[1]
    tasks, depth, width = w_hid.shape
    places = lax.axis_size("task")
    assert tasks <= places == 4
    part = mid // places
    me = lax.axis_index("task")
    rows = row_count * cols
    pixels = image_count * places * rows
    block = rows * 4
    shape = (image_count, row_count, places, cols)
    blocks = lax.axis_size("dp")

    quarter = w_shared.shape[0] // places
    staged = quarter % 16 == 0 and in_blocks(w_trunk.shape[0]) and blocks >= 4
    vectors = [trunk_gain[None], trunk_bias[None], hid_gain, hid_bias, attn_gain, attn_bias]
    first, second, vectors = pack_weights(
        w_trunk, w_hid, w_attn, w_shared, vectors, part, quarter * staged, blocks
    )
    trunk_shards = lax.all_to_all(first, "dp", 0, 0, tiled=True)
    gathered = lax.all_gather(second, "dp", axis=0, tiled=False)
    marks = jnp.stack([(labels >= 0).astype(F32), depth_valid.astype(F32)])
    marks = lax.all_gather(marks, "task", axis=2, tiled=True).reshape(2, pixels)
    marks, images = together(marks, images)
    all_images = lax.all_gather(
        images.reshape(image_count, rows, in_width), "task", axis=1, tiled=False
    )
    counts = jnp.broadcast_to(jnp.sum(marks, 1)[:, None], (2, part))
    labelled = jnp.broadcast_to(marks[0][:, None], (pixels, 128))
    mask = jnp.where(me == 0, labelled, jnp.broadcast_to(marks[1][:, None], (pixels, 128)))
    trunk_shards, all_images, labelled, mask, counts = together(
        trunk_shards, all_images, labelled, mask, counts
    )

    trunk, own_stats = trunk_forward(labelled, counts, all_images, trunk_shards, shape)
    hop, trunk = together(first_hop(own_stats), trunk)
    stats = side_by_side(relay(own_stats, hop))
    totals, (trunk, hop, trunk_cot, task_cot) = sum_dp(
        stats, lambda: (trunk, first_hop(trunk), trunk_cot, task_cot)
    )
    stay, cross = pack_cots(
        task_cot.reshape(tasks, image_count, rows, out_width),
        trunk_cot.reshape(image_count, rows, mid),
        places,
    )
    cot_hop = first_hop(cross)
    scaled = relay(trunk, hop)
    totals, gathered = together(totals, gathered)
    layers, *quarters = unpack_weights(gathered, depth, width, quarter * staged)
    if staged:
        hop = first_hop(quarters[0])
    feat, hid, hid_centre, sums, trunk_out = feat_hid(
        scaled, stats, totals, vectors, mask, layers, block, image_count
    )
    hid_totals = sum_dp(sums)
    hidden, gate, gate_centre, sums = hid_gate(
        hid, hid_centre, hid_totals, totals, vectors, mask, layers, block
    )
    if staged:
        sums, hop, cot_hop = together(sums, hop, cot_hop)
        quarters = relay(quarters[0], hop)
    else:
        quarters = [lax.all_gather(w_shared, "dp", axis=0, tiled=True)[None]]
    cots = trade(stay, cross, cot_hop)
    gate_totals, (feature_grad, full_shared) = sum_dp_then(
        sums,
        (cots, quarters),
        lambda needs: feature_back(needs[0], mask, needs[1], shape, out_width),
    )
    features, gate_grad, share, sums = gate_back(
        gate, gate_centre, gate_totals, totals, vectors, feature_grad, feat, block
    )

    sums, features = together(sums, features)
    gate_sums, (shared_kept, sent) = sum_dp(
        sums, lambda: shared_weights(cots, mask, features, shape, tasks, out_width)
    )
    def halve_shared(level, kept, got):
        if level == levels("task"):
            return kept, got
        kept, got = kept.reshape(-1, out_width // 2), got.reshape(-1, out_width // 2)
        if kept.shape[0] // blocks // 2 % 16 == 0:
            return add_split(level, kept, got, blocks)
        both = (kept.astype(F32) + got.astype(F32)).astype(BF)
        both = both.reshape(blocks, 2, -1, out_width // 2)
        bit = (me >> level) % 2
        return (
            lax.dynamic_index_in_dim(both, bit, 1, keepdims=False),
            lax.dynamic_index_in_dim(both, 1 - bit, 1, keepdims=False),
        )

    shared_got = swap(sent, "task", 1)
    gate_sums, shared_got = together(gate_sums, shared_got)
    shared_kept, sent = halve_shared(1, shared_kept, shared_got)
    gate_sums, sent = together(gate_sums, sent)
    shared_got = first_hop(sent)
    pre_grad, act_grad, sums = hid_back(
        gate_grad, gate, mask, gate_centre, gate_totals, totals, vectors, gate_sums, hid, hid_centre, hid_totals, layers, block
    )
    shared_kept = shared_kept.reshape(-1, out_width // 2)
    shared_got = shared_got.reshape(-1, out_width // 2)
    merged = staged and in_blocks(shared_kept.shape[0] // blocks)
    if merged:
        attn_even, attn_odd = product_parts(hidden, pre_grad, part)
        hid_sums, attn_odd = sum_dp(sums, lambda: attn_odd)
        hid_sums, attn_odd, shared_got = together(hid_sums, attn_odd, shared_got)
        attn_got = swap(attn_odd, "dp", 1)
    else:
        hid_sums = sum_dp(sums)
    hid_pre_grad, kept, sent = feat_back(
        act_grad, hid, mask, hid_centre, hid_totals, totals, vectors, hid_sums, share, layers, block, tasks
    )
    got = swap(sent, "task", 1)
    if merged:
        even, odd = merge_parts(shared_kept, shared_got, [(feat, hid_pre_grad)])
        got, even, odd = together(got, even, odd)
    kept, sent = add_halve(1, kept, got, block)
    sent, features = together(sent, features)
    got = first_hop(sent)
    if merged:
        sent, odd = together(sent, odd)
        part_got = swap(odd, "dp", 1)
        attn_parts = add_cut(attn_even, attn_got, blocks // 2)
        attn_parts = [swap(p, "dp", 2 * k) if k else p for k, p in enumerate(attn_parts)]
    task_stay, task_cross = task_forward(features, full_shared, shape)
    got, task_stay, task_cross = together(got, task_stay, task_cross)
    if merged:
        got, attn_parts = together(got, attn_parts)
    act_grad, sums = trunk_back([kept, got], cots, trunk, own_stats, totals, vectors, shape)
    sums, task_cross = together(sums, task_cross)
    task_hop = first_hop(task_cross)
    if merged:
        trunk_sums, (even, part_got) = sum_dp(sums, lambda: (even, part_got))
        parts = add_cut(even, part_got, blocks // 2)
        parts = [swap(p, "dp", 2 * k) if k else p for k, p in enumerate(parts)]
    else:
        trunk_sums = sum_dp(sums)
    trunk_pre_grad, *weight_parts = trunk_weights(
        all_images, act_grad, trunk, labelled, own_stats, totals, vectors, trunk_sums, shape
    )
    if len(weight_parts) == 2:
        weight_got = swap(weight_parts[1], "dp", 1)
    image_stay, image_cross = image_back(trunk_pre_grad, trunk_shards, shape)
    if merged:
        parts, image_cross = together(parts, image_cross)
    image_hop = first_hop(image_cross)
    if len(weight_parts) == 2:
        weight_parts = add_cut(weight_parts[0], weight_got, blocks // 2)
        weight_parts = [swap(p, "dp", 2 * k) if k else p for k, p in enumerate(weight_parts)]
        weight_parts, image_hop, task_hop = together(weight_parts, image_hop, task_hop)
    else:
        weight_parts = [scatter_dp(weight_parts)]
    weight_rows = weight_parts[0].shape[0]
    near, far = relay(trunk_total(weight_parts, gate_sums, hid_sums, trunk_sums))
    trunk_grad, attn_bias_grad, attn_gain_grad, hid_bias_grad, hid_gain_grad, trunk_sums = split_trunk(
        (near, far), weight_rows, tasks
    )
    own, one = first_sums(image_stay, image_hop)
    image_grad = piece_sum([own, swap(one, "task", 1)], BF).reshape(images.shape)
    if merged:
        shared_grad, hid_grad, attn_grad = split_parts(
            relay(sum_both(parts, attn_parts)),
            w_shared.shape[0] // (places // 2),
            (depth, width),
            tasks,
        )
    else:
        shared_grad = scatter_dp(sum_in_blocks(shared_kept, shared_got))
        for level in reversed(range(levels("task"))):
            pair = [shared_grad, swap(shared_grad, "task", 1 << level)]
            last = level == 0
            shared_grad = lay_out(
                lambda k, level=level: (lax.axis_index("task") >> level) % 2 ^ k,
                pair,
                F32 if last else BF,
                1 if last else 0,
            )
        attn_grad, hid_grad = (
            by_task(relay(scatter_dp(layer_weights([pair]))), tasks, F32) for pair in ((hidden, pre_grad), (feat, hid_pre_grad))
        )
    task_out = by_task(trade(task_stay, task_cross, task_hop), tasks, BF)
    task_out = task_out.reshape(tasks, image_count, row_count, cols, out_width)
    trunk_out = trunk_out.reshape(image_count, row_count, cols, mid)
    return (
        trunk_out,
        task_out,
        image_grad,
        trunk_grad,
        trunk_sums[1],
        trunk_sums[0],
        hid_grad,
        hid_gain_grad,
        hid_bias_grad,
        attn_grad,
        attn_gain_grad,
        attn_bias_grad,
        shared_grad,
    )


def solution(mesh):
    rows = P("dp", "task", None, None)
    task_rows = P(None, "dp", "task", None, None)
    flat, stacked = P("dp", None), P(None, "dp", None)
    pixel = P("dp", "task", None)
    return jax.shard_map(
        shards,
        mesh=mesh,
        in_specs=(
            rows,
            flat,
            P(),
            P(),
            stacked,
            P(),
            P(),
            stacked,
            P(),
            P(),
            flat,
            pixel,
            pixel,
            rows,
            task_rows,
        ),
        out_specs=(
            rows,
            task_rows,
            rows,
            flat,
            P(),
            P(),
            stacked,
            P(),
            P(),
            stacked,
            P(),
            P(),
            flat,
        ),
        check_vma=False,
    )
```
